32 devices in a mesh: shard: 8 (over y, x, core), seq: 4 (over z).
Axes of the slice: x: 2, y: 2, z: 4, core: 2. Of those that a mesh axis runs over, the one named last changes fastest.
Arguments:
- tokens: bfloat16 [4, 8192, 512], P(None, ('shard', 'seq')), may hold values from -7.1 to 7.1
- ln1_gain: bfloat16 [512], P('shard'), may hold values from 0.25 to 1.75
- ln1_bias: bfloat16 [512], P('shard'), may hold values from -2.5 to 2.5
- qkv_weight: bfloat16 [512, 1536], P('shard'), may hold values from -0.25 to 0.25
- out_weight: bfloat16 [512, 512], P('shard'), may hold values from -0.5 to 0.5
- out_bias: bfloat16 [512], P('shard'), may hold values from -2.5 to 2.5
- ln2_gain: bfloat16 [512], P('shard'), may hold values from 0.25 to 1.75
- ln2_bias: bfloat16 [512], P('shard'), may hold values from -2.5 to 2.5
- up_weight: bfloat16 [512, 2048], P('shard'), may hold values from -0.25 to 0.25
- up_bias: bfloat16 [2048], P('shard'), may hold values from -2.5 to 2.5
- down_weight: bfloat16 [2048, 512], P('shard'), may hold values from -0.125 to 0.125
- down_bias: bfloat16 [512], P('shard'), may hold values from -2.5 to 2.5
- cotangent: bfloat16 [4, 8192, 512], P(None, ('shard', 'seq')), may hold values from -15.4 to 15.4
Outputs:
- block_out: bfloat16 [4, 8192, 512], P(None, ('shard', 'seq'))
- grad_tokens: float32 [4, 8192, 512], P(None, ('shard', 'seq'))
- grad_ln1_gain: float32 [512], P('shard')
- grad_ln1_bias: float32 [512], P('shard')
- grad_qkv_weight: float32 [512, 1536], P('shard')
- grad_out_weight: float32 [512, 512], P('shard')
- grad_out_bias: float32 [512], P('shard')
- grad_ln2_gain: float32 [512], P('shard')
- grad_ln2_bias: float32 [512], P('shard')
- grad_up_weight: float32 [512, 2048], P('shard')
- grad_up_bias: float32 [2048], P('shard')
- grad_down_weight: float32 [2048, 512], P('shard')
- grad_down_bias: float32 [512], P('shard')
The draws below stay inside these ranges and needn't reach their ends.
All inputs are finite; a program needn't handle non-finite values.
Results may differ from the reference program's by a relative error of at most 0.02.
Values may be sent and summed in bfloat16 or wider, within the bound.
A program may use at most 128 MiB of HBM per device.

```python
import math
import jax
import jax.numpy as jnp
from jax import lax

D = 512
H = 8
HD = 64
FF = 2048
SPAN = 128
SPANS = 64
LENGTH = 8192
BATCH = 4


def draw_tokens(key, part):
    noise_key, common_key = jax.random.split(key)
    token_noise = jnp.clip(jax.random.normal(noise_key, (BATCH, LENGTH, D), jnp.float32), -4.0, 4.0)
    span_common = jnp.clip(jax.random.normal(common_key, (BATCH, SPANS, 1, D), jnp.float32), -4.0, 4.0)
    span_common = jnp.broadcast_to(span_common, (BATCH, SPANS, SPAN, D)).reshape(BATCH, LENGTH, D)
    values = 0.8 * token_noise + 0.8 * span_common
    return values.astype(jnp.bfloat16)


def draw_cotangent(key, part):
    position = jnp.arange(LENGTH, dtype=jnp.float32) / LENGTH
    rising = (1.0 + 2.0 * position)[None, :, None]
    values = jnp.clip(jax.random.normal(key, (BATCH, LENGTH, D), jnp.float32), -4.0, 4.0) * rising
    return values.astype(jnp.bfloat16)


def block_scale(rng, extent, shards, smallest, largest):
    def one(axis_at, shards_of):
        draws = jax.random.uniform(jax.random.fold_in(jax.random.fold_in(rng, 6), axis_at), (shards_of,), jnp.float32, smallest / len(shards), largest / len(shards))
        return jnp.repeat(jnp.exp(draws), extent[axis_at] // shards_of).reshape((-1,) + (1,) * (len(extent) - axis_at - 1))

    gain = one(*shards[0])
    for cut in shards[1:]:
        gain = gain * one(*cut)
    return gain


def scatter_about(rng, dims, scale, reach, cuts=(), kind=jnp.bfloat16):
    array = jax.random.normal(rng, dims, jnp.float32) * scale
    if len(cuts) > 0:
        array = block_scale(rng, dims, cuts, -0.22, 0.18) * array
    return jnp.clip(array, min=-reach, max=reach).astype(kind)


def setup_inputs(seed: int = 0) -> dict:
    splits = jax.random.split(jax.random.key(seed), 14)
    return {
        "tokens": draw_tokens(jax.random.fold_in(splits[13], 71), 0),
        "ln1_gain": jnp.clip(1.0 + 0.15 * jax.random.normal(splits[1], (D,), jnp.float32), 0.25, 1.75).astype(jnp.bfloat16),
        "ln1_bias": scatter_about(splits[2], (D,), 0.3, 2.5, ((0, 8),)),
        "qkv_weight": scatter_about(splits[3], (D, 3 * D), D ** -0.5, 0.25, ((0, 8),)),
        "out_weight": scatter_about(splits[4], (D, D), (D // 4) ** -0.5, 0.5, ((0, 8),)),
        "out_bias": scatter_about(splits[5], (D,), 0.3, 2.5, ((0, 8),)),
        "ln2_gain": jnp.clip(1.0 + 0.15 * jax.random.normal(splits[6], (D,), jnp.float32), 0.25, 1.75).astype(jnp.bfloat16),
        "ln2_bias": scatter_about(splits[7], (D,), 0.3, 2.5, ((0, 8),)),
        "up_weight": scatter_about(splits[8], (D, FF), D ** -0.5, 0.25, ((0, 8),)),
        "up_bias": scatter_about(splits[9], (FF,), 0.3, 2.5, ((0, 8),)),
        "down_weight": scatter_about(splits[10], (FF, D), FF ** -0.5, 0.125, ((0, 8),)),
        "down_bias": scatter_about(splits[11], (D,), 0.3, 2.5, ((0, 8),)),
        "cotangent": draw_cotangent(jax.random.fold_in(splits[13], 71), 0),
    }


@jax.custom_vjp
def low(v):
    return lax.optimization_barrier(v.astype(jnp.bfloat16)).astype(jnp.float32)

@jax.custom_vjp
def low_back(v):
    return v

def low_keep(v):
    return (low(v), None)

def low_pass(kept, grad):
    return (grad,)

def back_keep(v):
    return (v, None)

def back_low(kept, grad):
    return (low(grad),)
low.defvjp(low_keep, low_pass)
low_back.defvjp(back_keep, back_low)
epsilon = 1e-05
highest = lax.Precision.HIGHEST

def layer_norm(values, norm_gain, norm_shift):
    center = values - lax.optimization_barrier(jnp.mean(values, axis=-1, keepdims=True))
    spread = lax.optimization_barrier(jnp.mean(center * center, axis=-1, keepdims=True))
    return center * lax.rsqrt(spread + epsilon) * norm_gain + norm_shift

def product(left_matrix, right_matrix):
    return jnp.dot(left_matrix, right_matrix, precision=highest, preferred_element_type=jnp.float32)

def span_attention(packed):
    grouped = packed.reshape(SPANS, SPAN, 3, H, HD)
    query_rows = grouped[:, :, 0]
    key_rows = grouped[:, :, 1]
    value_rows = grouped[:, :, 2]
    key_means = low(lax.optimization_barrier(jnp.mean(key_rows, axis=1)))
    value_means = low(lax.optimization_barrier(jnp.mean(value_rows, axis=1)))
    factor = HD ** (-0.5)
    local_scores = low_back(factor * jnp.einsum('gihd,gjhd->ghij', query_rows, key_rows, precision=highest))
    summary_scores = low_back(factor * jnp.einsum('gihd,fhd->ghif', query_rows, key_means, precision=highest)) + math.log(SPAN)
    span_place = jnp.arange(SPAN)
    causal = span_place[:, None] >= span_place[None, :]
    span_order = jnp.arange(SPANS)
    earlier = span_order[:, None] > span_order[None, :]
    local_scores = jnp.where(causal[None, None], local_scores, -jnp.inf)
    summary_scores = jnp.where(earlier[:, None, None, :], summary_scores, -jnp.inf)
    joint = jnp.concatenate([local_scores, summary_scores], axis=-1)
    row_max = lax.optimization_barrier(jnp.max(joint, axis=-1, keepdims=True))
    expo = jnp.exp(joint - row_max)
    weights = expo / lax.optimization_barrier(jnp.sum(expo, axis=-1, keepdims=True))
    local_weights = low(weights[..., :SPAN])
    summary_weights = low(weights[..., SPAN:])
    mixed_heads = jnp.einsum('ghij,gjhd->gihd', local_weights, value_rows, precision=highest)
    mixed_heads = mixed_heads + jnp.einsum('ghif,fhd->gihd', summary_weights, value_means, precision=highest)
    return low_back(low(mixed_heads.reshape(SPANS * SPAN, H * HD)))

def forward(sequence, params):
    ln1_gain, ln1_bias, qkv_weight, out_weight, out_bias, ln2_gain, ln2_bias, up_weight, up_bias, down_weight, down_bias = params
    normed = low(layer_norm(sequence, ln1_gain, ln1_bias))
    packed = low_back(low(product(normed, qkv_weight)))
    attended = span_attention(packed)
    middle = sequence + low_back(product(attended, out_weight) + out_bias)
    second = low(layer_norm(middle, ln2_gain, ln2_bias))
    before = low_back(product(second, up_weight) + up_bias)
    hidden = low(jax.nn.gelu(before, approximate=False))
    return middle + product(hidden, down_weight) + down_bias

def reference(tokens, ln1_gain, ln1_bias, qkv_weight, out_weight, out_bias, ln2_gain, ln2_bias, up_weight, up_bias, down_weight, down_bias, cotangent):
    params = tuple((member.astype(jnp.float32) for member in (ln1_gain, ln1_bias, qkv_weight, out_weight, out_bias, ln2_gain, ln2_bias, up_weight, up_bias, down_weight, down_bias)))

    def one_sequence(running, sequence_pair):
        sequence, incoming = sequence_pair
        result, pullback = jax.vjp(forward, sequence.astype(jnp.float32), params)
        grad_sequence, grad_params = pullback(incoming.astype(jnp.float32))
        running = tuple((partial_sum + gradient for partial_sum, gradient in zip(running, grad_params)))
        return (running, (result.astype(jnp.bfloat16), grad_sequence))
    initial = tuple((jnp.zeros(member.shape, jnp.float32) for member in params))
    totals, (outputs, input_grads) = lax.scan(one_sequence, initial, (tokens, cotangent))
    return (outputs, input_grads, totals[0], totals[1], totals[2], totals[3], totals[4], totals[5], totals[6], totals[7], totals[8], totals[9], totals[10])
```

```python
import functools
import math

import jax
import jax.numpy as jnp
from jax import lax
from jax.experimental import pallas as pl
from jax.experimental.pallas import tpu as pltpu
from jax.sharding import PartitionSpec as P

H = 8
HD = 64
SPAN = 128


epsilon = 1e-05
MESH = pl.DeviceIdType.MESH
BF = jnp.bfloat16
F32 = jnp.float32


def dot(left, right, left_dim, right_dim):
    return lax.dot_general(
        left, right, (((left_dim,), (right_dim,)), ((), ())), preferred_element_type=F32
    )


def rows_of(index, count):
    return pl.ds(pl.multiple_of(index * count, count), count)


def norm_stats(values):
    center = values - jnp.mean(values, axis=-1, keepdims=True)
    inverse = lax.rsqrt(jnp.mean(center * center, axis=-1, keepdims=True) + epsilon)
    return center * inverse, inverse


def norm_back(grad, xhat, inverse, gain):
    scaled = grad * gain
    first = jnp.mean(scaled, axis=-1, keepdims=True)
    second = jnp.mean(scaled * xhat, axis=-1, keepdims=True)
    return inverse * (scaled - first - xhat * second)


QKV, OUT, UP, DOWN = range(4)
GD, GU, GO, GQ, GK, GV = range(6)
GATHER_STEPS = 9
REDUCE_STEPS = 8


def block_kernel(
    batch,
    shard_count,
    seq_count,
    tok_hbm,
    cot_hbm,
    vecs_ref,
    wq_hbm,
    wo_hbm,
    wu_hbm,
    wd_hbm,
    block_out_hbm,
    grad_tok_hbm,
    gq_hbm,
    go_hbm,
    gu_hbm,
    gd_hbm,
    vec_out_ref,
    tok,
    cot,
    wq,
    wo,
    wu,
    wd,
    vec_all,
    xhat1,
    inv1,
    xb_stage,
    xb_all,
    vfull,
    up_bias,
    normed,
    packed,
    nbar,
    kv_mean,
    probs,
    att,
    middle,
    inv2,
    second,
    xhat2,
    hidden,
    gbefore,
    bout,
    gatt,
    gbranch,
    gkv,
    gn_send,
    gn_recv,
    gnbar,
    vsum,
    upsum,
    vec_send,
    vec_recv,
    g_down,
    g_up,
    g_rest,
    r1_down,
    r1_up,
    r1_rest,
    r2_down,
    r2_up,
    r2_rest,
    r3_down,
    r3_up,
    r3_rest,
    r4_down,
    r4_up,
    r4_rest,
    own_down,
    own_up,
    own_rest,
    w_send,
    w_recv,
    w_local,
    io_sem,
    vec_s,
    vec_r,
    xb_s,
    xb_r,
    gn_s,
    gn_r,
    vo_s,
    vo_r,
    red_s,
    red_r,
    out_sem,
):
    rows, width = tok.shape
    ff = up_bias.shape[1]
    total = shard_count * seq_count
    groups = rows // SPAN
    spans_here = groups // batch
    spans_all = spans_here * total
    pairs = H // 2
    lanes = 2 * HD
    ms = lax.axis_index("shard")
    mq = lax.axis_index("seq")
    mt = ms * seq_count + mq
    core = lax.rem(ms, 2)
    yx = ms // 2

    def flip(value, bit):
        return value + bit - 2 * bit * lax.rem(value // bit, 2)

    core_dev = (flip(ms, 1), mq)
    x_dev = (flip(ms, 2), mq)
    y_dev = (flip(ms, 4), mq)

    def place(index):
        return (index // seq_count, lax.rem(index, seq_count))

    tok_in = pltpu.make_async_copy(tok_hbm, tok, io_sem.at[0])
    cot_in = pltpu.make_async_copy(cot_hbm, cot, io_sem.at[1])
    tok_in.start()
    cot_in.start()

    xb_all[...] = jnp.zeros_like(xb_all)
    barrier = pltpu.get_barrier_semaphore()

    def greet(step, carry):
        pl.semaphore_signal(
            barrier, inc=1, device_id=place(lax.rem(mt + step, total)), device_id_type=MESH
        )
        return carry

    lax.fori_loop(1, total, greet, 0)

    w_hbm = (wq_hbm, wo_hbm, wu_hbm, wd_hbm)
    w_full = (wq, wo, wu, wd)

    def gather_copies(which):
        full = w_full[which]
        depth = full.shape[0] // shard_count
        half = depth // 2
        base = which * GATHER_STEPS

        def block(owner):
            return full.at[rows_of(owner, depth)]

        def part(owner, side):
            return full.at[pl.ds(pl.multiple_of(owner * depth + side * half, half), half)]

        x_own, y_own, d_own = flip(ms, 2), flip(ms, 4), flip(flip(ms, 2), 4)
        plan = (
            (w_hbm[which], block(ms), x_dev),
            (w_hbm[which], block(ms), y_dev),
            (w_hbm[which], block(ms), core_dev),
            (block(x_own), block(x_own), core_dev),
            (block(y_own), block(y_own), core_dev),
            (part(x_own, 0), part(x_own, 0), y_dev),
            (part(y_own, 1), part(y_own, 1), x_dev),
            (part(d_own, 0), part(d_own, 0), core_dev),
            (part(d_own, 1), part(d_own, 1), core_dev),
        )
        return [
            pltpu.make_async_remote_copy(
                src_ref=src,
                dst_ref=dst,
                send_sem=w_send.at[base + step],
                recv_sem=w_recv.at[base + step],
                device_id=dev,
                device_id_type=MESH,
            )
            for step, (src, dst, dev) in enumerate(plan)
        ]

    w_copies = [gather_copies(which) for which in range(4)]

    def own_copy(which):
        depth = w_full[which].shape[0] // shard_count
        return pltpu.make_async_copy(
            w_hbm[which], w_full[which].at[rows_of(ms, depth)], w_local.at[which]
        )

    def gather_own(which):
        for step in (0, 1, 2):
            w_copies[which][step].start()
        own_copy(which).start()

    def gather_forward(which):
        c = w_copies[which]
        c[0].wait_recv()
        c[5].start()
        c[3].start()
        c[1].wait_recv()
        c[6].start()
        c[4].start()

    def gather_last(which):
        c = w_copies[which]
        c[5].wait_recv()
        c[7].start()
        c[6].wait_recv()
        c[8].start()

    def gather_done(which):
        c = w_copies[which]
        for step in (2, 3, 4, 7, 8):
            c[step].wait_recv()
        own_copy(which).wait()

    tok_in.wait()

    def first_norm(g, carry):
        at = rows_of(g, SPAN)
        xhat, inverse = norm_stats(tok[at, :].astype(F32))
        xhat1[at, :] = xhat
        inv1[at, :] = inverse
        xb_stage[pl.ds(g, 1), :] = jnp.mean(xhat, axis=0, keepdims=True)
        return carry

    lax.fori_loop(0, groups, first_norm, 0)
    half_width = width // 2
    xb_all[mt] = jnp.concatenate(
        [xb_stage[:, :half_width], xb_stage[:, half_width:]], axis=0
    ).astype(BF)

    pl.semaphore_wait(barrier, total - 1)

    vec_copies = []
    for step in range(1, shard_count):
        target = lax.rem(ms + step, shard_count)
        vec_copies.append(
            pltpu.make_async_remote_copy(
                src_ref=vecs_ref,
                dst_ref=vec_all.at[ms],
                send_sem=vec_s.at[step],
                recv_sem=vec_r.at[step],
                device_id=(target, mq),
                device_id_type=MESH,
            )
        )
    gather_own(QKV)
    for c in vec_copies:
        c.start()
    vec_all[ms] = vecs_ref[...]

    def xb_copy(source, target, send_at):
        return pltpu.make_async_remote_copy(
            src_ref=xb_all.at[source],
            dst_ref=xb_all.at[source],
            send_sem=xb_s.at[send_at],
            recv_sem=xb_r.at[source],
            device_id=place(target),
            device_id_type=MESH,
        )

    def xb_start(target, carry):
        xb_copy(mt, target, target).start()
        return carry

    lax.fori_loop(mt + 1, total, xb_start, 0)

    gather_own(OUT)
    gather_forward(QKV)
    for c in vec_copies:
        c.wait_recv()
    low_lane = lax.broadcasted_iota(jnp.int32, (8, lanes), 1) < HD
    for at in range(shard_count // 2):
        even = vec_all[2 * at]
        odd = vec_all[2 * at + 1]
        vfull[:, at * lanes : (at + 1) * lanes] = jnp.where(
            low_lane, even[0:8, :], pltpu.roll(odd[0:8, :], HD, axis=1)
        )
    up_here = ff // shard_count
    for owner in range(shard_count):
        piece = vec_all[owner]
        for r in range(up_here // lanes):
            start = owner * up_here + r * lanes
            up_bias[0:1, start : start + lanes] = piece[8 + r : 9 + r, :]
    gather_last(QKV)
    gather_own(UP)
    gather_done(QKV)
    gain1, bias1 = vfull[0:1, :], vfull[1:2, :]
    out_shift = vfull[2:3, :]
    gain2, bias2 = vfull[3:4, :], vfull[4:5, :]
    down_shift = vfull[5:6, :]

    big = 512

    def project(i, carry):
        at = rows_of(i, big)
        tile = (xhat1[at, :] * gain1 + bias1).astype(BF)
        normed[at, :] = tile
        for n in range(3):
            packed[at, n * width : (n + 1) * width] = dot(
                tile, wq[:, n * width : (n + 1) * width], 1, 0
            ).astype(BF)
        return carry

    lax.fori_loop(0, rows // big, project, 0)
    gather_forward(OUT)

    def xb_wait(source, carry):
        xb_copy(source, flip(mt, 1), 0).wait_recv()
        return carry

    lax.fori_loop(0, mt, xb_wait, 0)
    mean_rows = total * groups
    arrived = xb_all[...].astype(F32)
    arrived = jnp.concatenate([arrived[:, 0:groups, :], arrived[:, groups:, :]], axis=2)
    arrived = arrived.reshape(mean_rows, width)
    new_row = lax.broadcasted_iota(jnp.int32, (mean_rows, mean_rows), 0)
    old_row = lax.broadcasted_iota(jnp.int32, (mean_rows, mean_rows), 1)
    wanted = (
        lax.rem(new_row, spans_all) // spans_here * groups
        + new_row // spans_all * spans_here
        + lax.rem(new_row, spans_here)
    )
    order = (old_row == wanted).astype(BF)
    nbar[...] = dot(order, (arrived * gain1 + bias1).astype(BF), 1, 0).astype(BF)
    for n in range(2):
        kv_mean[:, n * width : (n + 1) * width] = dot(
            nbar[...], wq[:, (n + 1) * width : (n + 2) * width], 1, 0
        ).astype(BF)
    gather_last(OUT)
    gather_own(DOWN)
    gather_forward(UP)

    factor = HD ** (-0.5)
    keys = SPAN + spans_all

    def head_pair(ref_rows):
        low = lax.broadcasted_iota(jnp.int32, (SPAN, lanes), 1) < HD
        zero = jnp.zeros_like(ref_rows)
        return jnp.concatenate(
            [jnp.where(low, ref_rows, zero), jnp.where(low, zero, ref_rows)], axis=0
        )

    def score_shift(g):
        j = lax.broadcasted_iota(jnp.int32, (SPAN, SPAN), 0)
        i = lax.broadcasted_iota(jnp.int32, (SPAN, SPAN), 1)
        near = jnp.where(j <= i, 0.0, -jnp.inf).astype(F32)
        f = lax.broadcasted_iota(jnp.int32, (spans_all, SPAN), 0)
        here = mt * spans_here + lax.rem(g, spans_here)
        far = jnp.where(f < here, math.log(SPAN), -jnp.inf).astype(F32)
        both = jnp.concatenate([near, far], axis=0)
        return jnp.concatenate([both, both], axis=1)

    low_out = lax.broadcasted_iota(jnp.int32, (SPAN, lanes), 1) < HD

    def attend(g, carry):
        at = rows_of(g, SPAN)
        mean_at = rows_of(g // spans_here, spans_all)
        shift = score_shift(g)
        for p in range(pairs):
            lo = p * lanes
            q = packed[at, lo : lo + lanes]
            k = jnp.concatenate(
                [
                    packed[at, width + lo : width + lo + lanes],
                    kv_mean[mean_at, lo : lo + lanes],
                ],
                axis=0,
            )
            v = jnp.concatenate(
                [
                    packed[at, 2 * width + lo : 2 * width + lo + lanes],
                    kv_mean[mean_at, width + lo : width + lo + lanes],
                ],
                axis=0,
            )
            scores = dot(k, head_pair(q * factor), 1, 1) + shift
            expo = jnp.exp(scores - jnp.max(scores, axis=0, keepdims=True))
            weights = (expo * (1.0 / jnp.sum(expo, axis=0, keepdims=True))).astype(BF)
            probs[g * pairs + p] = weights
            mixed = dot(weights, v, 0, 0)
            att[at, lo : lo + lanes] = jnp.where(
                low_out, mixed[0:SPAN], mixed[SPAN : 2 * SPAN]
            ).astype(BF)
        return carry

    lax.fori_loop(0, groups, attend, 0)
    gather_done(OUT)
    gather_last(UP)
    gather_forward(DOWN)

    def second_norm(i, carry):
        at = rows_of(i, 256)
        mid = tok[at, :].astype(F32) + dot(att[at, :], wo[...], 1, 0) + out_shift
        middle[at, :] = mid
        xhat, inverse = norm_stats(mid)
        xhat2[at, :] = xhat
        inv2[at, :] = inverse
        second[at, :] = (xhat * gain2 + bias2).astype(BF)
        return carry

    lax.fori_loop(0, rows // 256, second_norm, 0)
    gather_done(UP)
    gather_last(DOWN)

    def feed_up(i, carry):
        at = rows_of(i // (ff // 512), big)
        cols = rows_of(lax.rem(i, ff // 512), 512)
        before = dot(second[at, :], wu[:, cols], 1, 0) + up_bias[0:1, cols]
        cdf = 0.5 + 0.5 * lax.erf(before * math.sqrt(0.5))
        density = jnp.exp(before * before * -0.5) * (1.0 / math.sqrt(2.0 * math.pi))
        hidden[at, cols] = (before * cdf).astype(BF)
        gbefore[at, cols] = (cdf + before * density).astype(BF)
        return carry

    lax.fori_loop(0, rows // big * (ff // 512), feed_up, 0)
    gather_done(DOWN)
    cot_in.wait()

    def chunk(which):
        if which == GD:
            return (g_down, r1_down, r2_down, r3_down, r4_down, own_down)
        if which == GU:
            return (g_up, r1_up, r2_up, r3_up, r4_up, own_up)
        n = which - GO
        return tuple(
            ref.at[n] for ref in (g_rest, r1_rest, r2_rest, r3_rest, r4_rest, own_rest)
        )

    here, x_blk, y_blk, d_blk = yx, flip(yx, 1), flip(yx, 2), flip(flip(yx, 1), 2)
    z_dev = (ms, flip(mq, 1))
    z_mid = (ms, seq_count - 1 - mq)

    def reduce_copies(which):
        g, r1, r2, r3, r4, own = chunk(which)
        half = g.shape[2] // 2
        base = which * REDUCE_STEPS
        plan = (
            (g.at[1 - core], r1, core_dev),
            (g.at[core, d_blk, pl.ds(0, half)], r2.at[0], x_dev),
            (g.at[core, d_blk, pl.ds(half, half)], r2.at[1], y_dev),
            (g.at[core, x_blk], r3.at[0], x_dev),
            (g.at[core, y_blk], r3.at[1], y_dev),
            (own, r4.at[0], z_dev),
            (own, r4.at[1], z_mid),
            (own, r4.at[0], z_dev),
        )
        copies = [
            pltpu.make_async_remote_copy(
                src_ref=src,
                dst_ref=dst,
                send_sem=red_s.at[base + step],
                recv_sem=red_r.at[base + step],
                device_id=dev,
                device_id_type=MESH,
            )
            for step, (src, dst, dev) in enumerate(plan)
        ]
        return copies

    r_copies = [reduce_copies(which) for which in range(6)]
    edge = jnp.logical_or(mq == 0, mq == seq_count - 1)
    inner = jnp.logical_not(edge)

    def add_rows(target, *sources):
        count = target.shape[0]
        step = min(count, 32)

        def one(i, carry):
            at = rows_of(i, step)
            value = target[at, :].astype(F32)
            for source in sources:
                value = value + source[at, :].astype(F32)
            target[at, :] = value.astype(BF)
            return carry

        lax.fori_loop(0, count // step, one, 0)

    def reduce_a(which):
        r_copies[which][0].start()

    def reduce_b(which):
        g, r1, r2, r3, r4, own = chunk(which)
        c = r_copies[which]
        c[0].wait_recv()
        add_rows(g.at[core, d_blk], r1.at[d_blk])
        c[1].start()
        c[2].start()
        for blk in (x_blk, y_blk, here):
            add_rows(g.at[core, blk], r1.at[blk])

    def reduce_c(which):
        g, r1, r2, r3, r4, own = chunk(which)
        half = g.shape[2] // 2
        c = r_copies[which]
        c[1].wait_recv()
        add_rows(g.at[core, y_blk, pl.ds(0, half)], r2.at[0])
        c[4].start()
        c[2].wait_recv()
        add_rows(g.at[core, x_blk, pl.ds(half, half)], r2.at[1])
        c[3].start()

    def reduce_d(which):
        g, r1, r2, r3, r4, own = chunk(which)
        c = r_copies[which]
        c[3].wait_recv()
        c[4].wait_recv()
        count = own.shape[0]

        def one(i, carry):
            at = rows_of(i, 32)
            value = (
                g[core, here, at, :].astype(F32)
                + r3[0, at, :].astype(F32)
                + r3[1, at, :].astype(F32)
            )
            own[at, :] = value.astype(BF)
            return carry

        lax.fori_loop(0, count // 32, one, 0)

        @pl.when(edge)
        def _():
            c[5].start()

    def reduce_e(which):
        g, r1, r2, r3, r4, own = chunk(which)
        c = r_copies[which]

        @pl.when(inner)
        def _():
            c[5].wait_recv()
            add_rows(own, r4.at[0])
            c[6].start()

    g_out = (gd_hbm, gu_hbm, go_hbm)

    def emit(which, source):
        if which <= GO:
            target = g_out[which]
        else:
            target = gq_hbm.at[:, pl.ds((which - GQ) * width, width)]
        return pltpu.make_async_copy(source, target, out_sem.at[which])

    def reduce_f(which):
        g, r1, r2, r3, r4, own = chunk(which)
        c = r_copies[which]

        @pl.when(inner)
        def _():
            c[6].wait_recv()
            c[6].wait_send()
            add_rows(own, r4.at[1])
            c[7].start()
            emit(which, own).start()

    def reduce_g(which):
        g, r1, r2, r3, r4, own = chunk(which)
        c = r_copies[which]

        @pl.when(edge)
        def _():
            c[5].wait_send()
            c[7].wait_recv()
            emit(which, r4.at[0]).start()

        @pl.when(inner)
        def _():
            c[7].wait_send()

        for step in range(5):
            c[step].wait_send()
        emit(which, own).wait()

    def down_grad(o, carry):
        g_down[lax.rem(o, 2), o // 2] = dot(
            hidden[:, rows_of(o, ff // shard_count)], cot[...], 0, 0
        ).astype(BF)
        return carry

    lax.fori_loop(0, shard_count, down_grad, 0)
    reduce_a(GD)

    def back_down(i, carry):
        at = rows_of(i // (ff // 512), big)
        cols = rows_of(lax.rem(i, ff // 512), 512)
        grad = dot(cot[at, :], wd[cols, :], 1, 1)
        grad = (grad * gbefore[at, cols].astype(F32)).astype(BF)
        gbefore[at, cols] = grad
        return carry

    lax.fori_loop(0, rows // big * (ff // 512), back_down, 0)
    reduce_b(GD)

    shard_rows = width // shard_count

    def up_grad(n, carry):
        cols = rows_of(n, 512)
        piece = dot(second[...], gbefore[:, cols], 0, 0).astype(BF)
        for owner in range(shard_count):
            g_up[owner % 2, owner // 2, :, cols] = piece[
                owner * shard_rows : (owner + 1) * shard_rows
            ]
        upsum[0:1, cols] = jnp.sum(gbefore[:, cols].astype(F32), axis=0, keepdims=True)
        return carry

    lax.fori_loop(0, ff // 512, up_grad, 0)
    reduce_c(GD)
    reduce_a(GU)

    vsum[...] = jnp.zeros_like(vsum)

    def out_block(i, carry):
        at = rows_of(i, 256)
        bout[at, :] = (
            middle[at, :] + dot(hidden[at, :], wd[...], 1, 0) + down_shift
        ).astype(BF)
        vsum[5:6, :] += jnp.sum(cot[at, :].astype(F32), axis=0, keepdims=True)
        return carry

    lax.fori_loop(0, rows // 256, out_block, 0)
    bout_out = pltpu.make_async_copy(bout, block_out_hbm, io_sem.at[2])
    bout_out.start()
    reduce_b(GU)
    reduce_d(GD)

    def back_second(i, carry):
        at = rows_of(i, 256)
        grad = dot(gbefore[at, :], wu[...], 1, 1)
        xhat = xhat2[at, :]
        vsum[3:4, :] += jnp.sum(grad * xhat, axis=0, keepdims=True)
        vsum[4:5, :] += jnp.sum(grad, axis=0, keepdims=True)
        grad_mid = cot[at, :].astype(F32) + norm_back(grad, xhat, inv2[at, :], gain2)
        middle[at, :] = grad_mid
        branch = grad_mid.astype(BF)
        gbranch[at, :] = branch
        vsum[2:3, :] += jnp.sum(branch.astype(F32), axis=0, keepdims=True)
        gatt[at, :] = dot(branch, wo[...], 1, 1).astype(BF)
        return carry

    lax.fori_loop(0, rows // 256, back_second, 0)
    reduce_c(GU)
    reduce_e(GD)

    def put_rest(which, piece):
        for owner in range(shard_count):
            g_rest[which - GO, owner % 2, owner // 2] = piece[
                owner * shard_rows : (owner + 1) * shard_rows
            ]

    put_rest(GO, dot(att[...], gbranch[...], 0, 0).astype(BF))
    reduce_a(GO)

    gkv[...] = jnp.zeros_like(gkv)
    low_keys = lax.broadcasted_iota(jnp.int32, (SPAN, lanes), 1) < HD

    def attend_back(g, carry):
        at = rows_of(g, SPAN)
        mean_at = rows_of(g // spans_here, spans_all)
        for p in range(pairs):
            lo = p * lanes
            q = head_pair(packed[at, lo : lo + lanes])
            k = jnp.concatenate(
                [
                    packed[at, width + lo : width + lo + lanes],
                    kv_mean[mean_at, lo : lo + lanes],
                ],
                axis=0,
            )
            v = jnp.concatenate(
                [
                    packed[at, 2 * width + lo : 2 * width + lo + lanes],
                    kv_mean[mean_at, width + lo : width + lo + lanes],
                ],
                axis=0,
            )
            go = head_pair(gatt[at, lo : lo + lanes])
            weights = probs[g * pairs + p]
            gw = dot(v, go, 1, 1)
            prob = weights.astype(F32)
            row_inner = jnp.sum(prob * gw, axis=0, keepdims=True)
            gs = (prob * (gw - row_inner)).astype(BF)
            gq = dot(gs, k, 0, 0)
            gk = dot(gs, q, 1, 0) * factor
            gv = dot(weights, go, 1, 0)
            packed[at, lo : lo + lanes] = (
                jnp.where(low_keys, gq[0:SPAN], gq[SPAN : 2 * SPAN]) * factor
            ).astype(BF)
            packed[at, width + lo : width + lo + lanes] = gk[0:SPAN].astype(BF)
            packed[at, 2 * width + lo : 2 * width + lo + lanes] = gv[0:SPAN].astype(BF)
            gkv[mean_at, lo : lo + lanes] += gk[SPAN:]
            gkv[mean_at, width + lo : width + lo + lanes] += gv[SPAN:]
        return carry

    half_groups = groups // 2
    lax.fori_loop(0, half_groups, attend_back, 0)
    reduce_b(GO)
    reduce_d(GU)
    reduce_f(GD)
    lax.fori_loop(half_groups, groups, attend_back, 0)
    reduce_c(GO)
    reduce_e(GU)

    gkv_low = gkv[...].astype(BF)
    gmean = dot(gkv_low, wq[:, width : 3 * width], 1, 1).astype(BF)
    gmean = dot(order, gmean, 0, 0).reshape(total, groups, width)
    gn_send[...] = jnp.concatenate(
        [gmean[:, :, :half_width], gmean[:, :, half_width:]], axis=1
    ).astype(BF)

    def gn_copy(source, target, send_at):
        return pltpu.make_async_remote_copy(
            src_ref=gn_send.at[target],
            dst_ref=gn_recv.at[source],
            send_sem=gn_s.at[send_at],
            recv_sem=gn_r.at[source],
            device_id=place(target),
            device_id_type=MESH,
        )

    def gn_start(target, carry):
        gn_copy(mt, target, target).start()
        return carry

    lax.fori_loop(0, mt, gn_start, 0)

    put_rest(GQ, dot(normed[...], packed[:, 0:width], 0, 0).astype(BF))
    reduce_a(GQ)
    put_rest(
        GK,
        (
            dot(normed[...], packed[:, width : 2 * width], 0, 0)
            + dot(nbar[...], gkv_low[:, 0:width], 0, 0)
        ).astype(BF),
    )
    reduce_a(GK)
    reduce_b(GQ)
    put_rest(
        GV,
        (
            dot(normed[...], packed[:, 2 * width :], 0, 0)
            + dot(nbar[...], gkv_low[:, width:], 0, 0)
        ).astype(BF),
    )
    reduce_a(GV)
    reduce_b(GK)
    reduce_c(GQ)
    reduce_b(GV)
    reduce_d(GO)
    reduce_f(GU)

    def gn_wait(source, carry):
        make = gn_copy(source, flip(mt, 1), 0)
        make.wait_recv()
        gnbar[...] += gn_recv[source].astype(F32)
        return carry

    gnbar[...] = gn_send[mt].astype(F32)
    lax.fori_loop(mt + 1, total, gn_wait, 0)
    reduce_c(GK)
    reduce_e(GO)
    reduce_c(GV)
    reduce_d(GQ)

    def back_first(g, carry):
        at = rows_of(g, SPAN)
        share = jnp.concatenate(
            [gnbar[pl.ds(g, 1), :], gnbar[pl.ds(groups + g, 1), :]], axis=1
        ) * (1.0 / SPAN)
        grad = dot(packed[at, :], wq[...], 1, 1) + share
        xhat = xhat1[at, :]
        vsum[0:1, :] += jnp.sum(grad * xhat, axis=0, keepdims=True)
        vsum[1:2, :] += jnp.sum(grad, axis=0, keepdims=True)
        middle[at, :] = middle[at, :] + norm_back(grad, xhat, inv1[at, :], gain1)
        return carry

    lax.fori_loop(0, groups, back_first, 0)
    tok_out = pltpu.make_async_copy(middle, grad_tok_hbm, io_sem.at[3])
    tok_out.start()

    for owner in range(shard_count):
        at = owner // 2
        piece = vsum[:, at * lanes : (at + 1) * lanes]
        if owner % 2 == 1:
            piece = pltpu.roll(piece, HD, axis=1)
        vec_send[owner, 0:8, :] = piece
        vec_send[owner, 8:16, :] = jnp.zeros((8, lanes), F32)
        for r in range(up_here // lanes):
            start = owner * up_here + r * lanes
            vec_send[owner, 8 + r : 9 + r, :] = upsum[0:1, start : start + lanes]

    def vo_copy(source, target, send_at):
        return pltpu.make_async_remote_copy(
            src_ref=vec_send.at[target // seq_count],
            dst_ref=vec_recv.at[source],
            send_sem=vo_s.at[send_at],
            recv_sem=vo_r.at[source],
            device_id=place(target),
            device_id_type=MESH,
        )

    def vo_start(step, carry):
        target = lax.rem(mt + step, total)
        vo_copy(mt, target, target).start()
        return carry

    lax.fori_loop(1, total, vo_start, 0)
    vec_recv[mt] = vec_send[ms]
    reduce_d(GK)
    reduce_e(GQ)
    reduce_d(GV)
    reduce_e(GK)
    reduce_f(GO)
    reduce_e(GV)
    reduce_f(GQ)
    reduce_f(GK)
    reduce_f(GV)

    def vo_wait(step, carry):
        source = lax.rem(mt + step, total)
        vo_copy(source, flip(mt, 1), 0).wait_recv()
        return carry

    lax.fori_loop(1, total, vo_wait, 0)
    vec_out_ref[...] = jnp.sum(vec_recv[...], axis=0)

    for which in (GD, GU, GO, GQ, GK, GV):
        reduce_g(which)

    def xb_sent(target, carry):
        xb_copy(mt, target, target).wait_send()
        return carry

    lax.fori_loop(mt + 1, total, xb_sent, 0)

    def gn_sent(target, carry):
        gn_copy(mt, target, target).wait_send()
        return carry

    lax.fori_loop(0, mt, gn_sent, 0)

    def vo_sent(step, carry):
        target = lax.rem(mt + step, total)
        vo_copy(mt, target, target).wait_send()
        return carry

    lax.fori_loop(1, total, vo_sent, 0)
    for c in vec_copies:
        c.wait_send()
    for which in range(4):
        for c in w_copies[which]:
            c.wait_send()
    bout_out.wait()
    tok_out.wait()


def local_block(
    tokens,
    ln1_gain,
    ln1_bias,
    qkv_weight,
    out_weight,
    out_bias,
    ln2_gain,
    ln2_bias,
    up_weight,
    up_bias,
    down_weight,
    down_bias,
    cotangent,
):
    seq_count = lax.axis_size("seq")
    shard_count = lax.axis_size("shard")
    total = seq_count * shard_count
    batch, local_len, width = tokens.shape
    rows = batch * local_len
    groups = rows // SPAN
    spans_all = local_len // SPAN * total
    keys = SPAN + spans_all
    ff = up_weight.shape[1]
    lanes = 2 * HD
    shard_rows = width // shard_count
    down_rows = ff // shard_count
    narrow = jnp.stack([ln1_gain, ln1_bias, out_bias, ln2_gain, ln2_bias, down_bias])
    narrow = jnp.pad(narrow, ((0, 2), (0, lanes - shard_rows)))
    wide = jnp.pad(up_bias.reshape(-1, lanes), ((0, 8 - down_rows // lanes), (0, 0)))
    vecs = jnp.concatenate([narrow, wide]).astype(F32)
    vmem = pl.BlockSpec(memory_space=pltpu.VMEM)
    hbm = pl.BlockSpec(memory_space=pl.ANY)
    dma = pltpu.SemaphoreType.DMA
    half_yx = shard_count // 2

    def grads(count, columns, lead=()):
        half = count // 2
        return (
            pltpu.VMEM(lead + (2, half_yx, count, columns), BF),
            pltpu.VMEM(lead + (half_yx, count, columns), BF),
            pltpu.VMEM(lead + (2, half, columns), BF),
            pltpu.VMEM(lead + (2, count, columns), BF),
            pltpu.VMEM(lead + (2, count, columns), BF),
            pltpu.VMEM(lead + (count, columns), BF),
        )

    down_bufs = grads(down_rows, width)
    up_bufs = grads(shard_rows, ff)
    rest_bufs = grads(shard_rows, width, (4,))
    grad_bufs = [buf for trio in zip(down_bufs, up_bufs, rest_bufs) for buf in trio]
    scratch = [
        pltpu.VMEM((rows, width), BF),
        pltpu.VMEM((rows, width), BF),
        pltpu.VMEM((width, 3 * width), BF),
        pltpu.VMEM((width, width), BF),
        pltpu.VMEM((width, ff), BF),
        pltpu.VMEM((ff, width), BF),
        pltpu.VMEM((shard_count, 16, lanes), F32),
        pltpu.VMEM((rows, width), F32),
        pltpu.VMEM((rows, 1), F32),
        pltpu.VMEM((groups, width), F32),
        pltpu.VMEM((total, 2 * groups, width // 2), BF),
        pltpu.VMEM((8, width), F32),
        pltpu.VMEM((8, ff), F32),
        pltpu.VMEM((rows, width), BF),
        pltpu.VMEM((rows, 3 * width), BF),
        pltpu.VMEM((batch * spans_all, width), BF),
        pltpu.VMEM((batch * spans_all, 2 * width), BF),
        pltpu.VMEM((groups * H // 2, keys, 2 * SPAN), BF),
        pltpu.VMEM((rows, width), BF),
        pltpu.VMEM((rows, width), F32),
        pltpu.VMEM((rows, 1), F32),
        pltpu.VMEM((rows, width), BF),
        pltpu.VMEM((rows, width), F32),
        pltpu.VMEM((rows, ff), BF),
        pltpu.VMEM((rows, ff), BF),
        pltpu.VMEM((rows, width), BF),
        pltpu.VMEM((rows, width), BF),
        pltpu.VMEM((rows, width), BF),
        pltpu.VMEM((batch * spans_all, 2 * width), F32),
        pltpu.VMEM((total, 2 * groups, width // 2), BF),
        pltpu.VMEM((total, 2 * groups, width // 2), BF),
        pltpu.VMEM((2 * groups, width // 2), F32),
        pltpu.VMEM((8, width), F32),
        pltpu.VMEM((8, ff), F32),
        pltpu.VMEM((shard_count, 16, lanes), F32),
        pltpu.VMEM((total, 16, lanes), F32),
        *grad_bufs,
        dma((4 * GATHER_STEPS,)),
        dma((4 * GATHER_STEPS,)),
        dma((4,)),
        dma((4,)),
        dma((shard_count,)),
        dma((shard_count,)),
        dma((total,)),
        dma((total,)),
        dma((total,)),
        dma((total,)),
        dma((total,)),
        dma((total,)),
        dma((6 * REDUCE_STEPS,)),
        dma((6 * REDUCE_STEPS,)),
        dma((6,)),
    ]
    outs = pl.pallas_call(
        functools.partial(block_kernel, batch, shard_count, seq_count),
        out_shape=(
            jax.ShapeDtypeStruct((rows, width), BF),
            jax.ShapeDtypeStruct((rows, width), F32),
            jax.ShapeDtypeStruct((shard_rows, 3 * width), BF),
            jax.ShapeDtypeStruct((shard_rows, width), BF),
            jax.ShapeDtypeStruct((shard_rows, ff), BF),
            jax.ShapeDtypeStruct((down_rows, width), BF),
            jax.ShapeDtypeStruct((16, lanes), F32),
        ),
        in_specs=[hbm, hbm, vmem, hbm, hbm, hbm, hbm],
        out_specs=(hbm, hbm, hbm, hbm, hbm, hbm, vmem),
        scratch_shapes=scratch,
        compiler_params=pltpu.CompilerParams(
            collective_id=0, has_side_effects=True, vmem_limit_bytes=63 * 2**20
        ),
        name="block",
    )(
        tokens.reshape(rows, width),
        cotangent.reshape(rows, width),
        vecs,
        qkv_weight,
        out_weight,
        up_weight,
        down_weight,
    )
    block_out, grad_tokens, g_qkv, g_out, g_up, g_down, g_vec = outs
    return (
        block_out.reshape(tokens.shape),
        grad_tokens.reshape(tokens.shape),
        g_vec[0, :shard_rows],
        g_vec[1, :shard_rows],
        g_qkv.astype(F32),
        g_out.astype(F32),
        g_vec[2, :shard_rows],
        g_vec[3, :shard_rows],
        g_vec[4, :shard_rows],
        g_up.astype(F32),
        g_vec[8 : 8 + down_rows // lanes].reshape(down_rows),
        g_down.astype(F32),
        g_vec[5, :shard_rows],
    )


def layer_norm(values, norm_gain, norm_shift):
    center = values - jnp.mean(values, axis=-1, keepdims=True)
    spread = jnp.mean(center * center, axis=-1, keepdims=True)
    return center * lax.rsqrt(spread + epsilon) * norm_gain + norm_shift


def gelu_exact(values):
    return jax.nn.gelu(values, approximate=False)


def contract_rows(left_matrix, right_matrix):
    return lax.dot_general(
        left_matrix, right_matrix, (((0,), (0,)), ((), ())), preferred_element_type=jnp.float32
    )


def times_transpose(left_matrix, right_matrix):
    return lax.dot_general(
        left_matrix, right_matrix, (((1,), (1,)), ((), ())), preferred_element_type=jnp.float32
    )


def joint_scores(query_rows, key_rows, key_all, causal, earlier):
    factor = HD ** (-0.5)
    local_part = factor * jnp.einsum(
        "bjihd,bjkhd->bjhik", query_rows, key_rows, preferred_element_type=jnp.float32
    )
    summary = factor * jnp.einsum(
        "bjihd,bfhd->bjhif", query_rows, key_all, preferred_element_type=jnp.float32
    ) + math.log(SPAN)
    local_part = jnp.where(causal[None, None, None], local_part, -jnp.inf)
    summary = jnp.where(earlier[None, :, None, None, :], summary, -jnp.inf)
    return (local_part, summary)


def attend(query_rows, key_rows, value_rows, key_all, value_all, causal, earlier):
    local_part, summary = joint_scores(query_rows, key_rows, key_all, causal, earlier)
    row_max = jnp.maximum(jnp.max(local_part, axis=-1), jnp.max(summary, axis=-1))
    local_exp = jnp.exp(local_part - row_max[..., None])
    summary_exp = jnp.exp(summary - row_max[..., None])
    row_total = jnp.sum(local_exp, axis=-1) + jnp.sum(summary_exp, axis=-1)
    log_total = row_max + jnp.log(row_total)
    local_weights = (local_exp / row_total[..., None]).astype(jnp.bfloat16)
    summary_weights = (summary_exp / row_total[..., None]).astype(jnp.bfloat16)
    mixed_heads = jnp.einsum(
        "bjhik,bjkhd->bjihd", local_weights, value_rows, preferred_element_type=jnp.float32
    )
    mixed_heads = mixed_heads + jnp.einsum(
        "bjhif,bfhd->bjihd", summary_weights, value_all, preferred_element_type=jnp.float32
    )
    return (mixed_heads, log_total, local_weights, summary_weights)


def attend_back(
    grad_mixed,
    query_rows,
    key_rows,
    value_rows,
    key_all,
    value_all,
    causal,
    earlier,
    log_total,
    local_weights,
    summary_weights,
):
    factor = HD ** (-0.5)
    local_part, summary = joint_scores(query_rows, key_rows, key_all, causal, earlier)
    local_prob = jnp.exp(local_part - log_total[..., None])
    summary_prob = jnp.exp(summary - log_total[..., None])
    grad_local_w = jnp.einsum(
        "bjihd,bjkhd->bjhik", grad_mixed, value_rows, preferred_element_type=jnp.float32
    )
    grad_summary_w = jnp.einsum(
        "bjihd,bfhd->bjhif", grad_mixed, value_all, preferred_element_type=jnp.float32
    )
    row_inner = jnp.sum(local_prob * grad_local_w, axis=-1) + jnp.sum(
        summary_prob * grad_summary_w, axis=-1
    )
    grad_local = (local_prob * (grad_local_w - row_inner[..., None])).astype(jnp.bfloat16)
    grad_summary = (summary_prob * (grad_summary_w - row_inner[..., None])).astype(jnp.bfloat16)
    grad_query = jnp.einsum(
        "bjhik,bjkhd->bjihd", grad_local, key_rows, preferred_element_type=jnp.float32
    )
    grad_query = factor * (
        grad_query
        + jnp.einsum("bjhif,bfhd->bjihd", grad_summary, key_all, preferred_element_type=jnp.float32)
    )
    grad_key = factor * jnp.einsum(
        "bjhik,bjihd->bjkhd", grad_local, query_rows, preferred_element_type=jnp.float32
    )
    grad_key_all = factor * jnp.einsum(
        "bjhif,bjihd->bfhd", grad_summary, query_rows, preferred_element_type=jnp.float32
    )
    grad_value = jnp.einsum(
        "bjhik,bjihd->bjkhd", local_weights, grad_mixed, preferred_element_type=jnp.float32
    )
    grad_value_all = jnp.einsum(
        "bjhif,bjihd->bfhd", summary_weights, grad_mixed, preferred_element_type=jnp.float32
    )
    return (grad_query, grad_key, grad_value, grad_key_all, grad_value_all)


def local_general(
    tokens,
    ln1_gain,
    ln1_bias,
    qkv_weight,
    out_weight,
    out_bias,
    ln2_gain,
    ln2_bias,
    up_weight,
    up_bias,
    down_weight,
    down_bias,
    cotangent,
):
    seq_count = lax.axis_size("seq")
    shard_count = lax.axis_size("shard")
    shard_place = lax.axis_index("shard")
    batch_size, local_len, model_width = tokens.shape
    heads_here = H // seq_count
    head_width = heads_here * HD
    group_len = local_len * seq_count
    spans_here = group_len // SPAN
    spans_all = spans_here * shard_count
    row_count = batch_size * local_len
    shards = (
        ln1_gain,
        ln1_bias,
        qkv_weight,
        out_weight,
        out_bias,
        ln2_gain,
        ln2_bias,
        up_weight,
        up_bias,
        down_weight,
        down_bias,
    )
    gathered = (
        lax.all_gather(shards[0], "shard", axis=0, tiled=True),
        lax.all_gather(shards[1], "shard", axis=0, tiled=True),
        lax.all_gather(shards[2], "shard", axis=0, tiled=True),
        lax.all_gather(shards[3], "shard", axis=0, tiled=True),
        lax.all_gather(shards[4], "shard", axis=0, tiled=True),
        lax.all_gather(shards[5], "shard", axis=0, tiled=True),
        lax.all_gather(shards[6], "shard", axis=0, tiled=True),
        lax.all_gather(shards[7], "shard", axis=0, tiled=True),
        lax.all_gather(shards[8], "shard", axis=0, tiled=True),
        lax.all_gather(shards[9], "shard", axis=0, tiled=True),
        lax.all_gather(shards[10], "shard", axis=0, tiled=True),
    )
    (
        gain_one,
        bias_one,
        qkv_full,
        out_full,
        out_shift,
        gain_two,
        bias_two,
        up_full,
        up_shift,
        down_full,
        down_shift,
    ) = gathered
    flat_tokens = tokens.reshape(row_count, model_width).astype(jnp.float32)
    normed = layer_norm(
        flat_tokens, gain_one.astype(jnp.float32), bias_one.astype(jnp.float32)
    ).astype(jnp.bfloat16)
    packed = jnp.dot(normed, qkv_full, preferred_element_type=jnp.float32).astype(jnp.bfloat16)
    span_place = jnp.arange(SPAN)
    packed_heads = packed.reshape(batch_size, local_len, 3, seq_count, head_width)
    headed = lax.all_to_all(packed_heads, "seq", split_axis=3, concat_axis=1, tiled=True)
    headed = headed.reshape(batch_size, spans_here, SPAN, 3, heads_here, HD)
    query_rows = headed[:, :, :, 0]
    key_rows = headed[:, :, :, 1]
    value_rows = headed[:, :, :, 2]
    key_means = jnp.mean(key_rows, axis=2, dtype=jnp.float32).astype(jnp.bfloat16)
    value_means = jnp.mean(value_rows, axis=2, dtype=jnp.float32).astype(jnp.bfloat16)
    key_all, value_all = (
        lax.all_gather(key_means, "shard", axis=1, tiled=True),
        lax.all_gather(value_means, "shard", axis=1, tiled=True),
    )
    causal = span_place[:, None] >= span_place[None, :]
    global_span = shard_place * spans_here + jnp.arange(spans_here)
    earlier = global_span[:, None] > jnp.arange(spans_all)[None, :]
    mixed_heads, log_total, local_weights, summary_weights = attend(
        query_rows, key_rows, value_rows, key_all, value_all, causal, earlier
    )
    attended = mixed_heads.astype(jnp.bfloat16).reshape(batch_size, group_len, head_width)
    attended = lax.all_to_all(attended, "seq", split_axis=1, concat_axis=2, tiled=True)
    attended_rows = attended.reshape(row_count, model_width)
    middle = (
        flat_tokens
        + jnp.dot(attended_rows, out_full, preferred_element_type=jnp.float32)
        + out_shift.astype(jnp.float32)
    )
    second = layer_norm(middle, gain_two.astype(jnp.float32), bias_two.astype(jnp.float32)).astype(
        jnp.bfloat16
    )
    before = jnp.dot(second, up_full, preferred_element_type=jnp.float32) + up_shift.astype(
        jnp.float32
    )
    hidden = gelu_exact(before).astype(jnp.bfloat16)
    block_out = (
        middle
        + jnp.dot(hidden, down_full, preferred_element_type=jnp.float32)
        + down_shift.astype(jnp.float32)
    )
    block_out = block_out.astype(jnp.bfloat16).reshape(batch_size, local_len, model_width)
    incoming = cotangent.reshape(row_count, model_width)
    grad_down = contract_rows(hidden, incoming)
    grad_down_shift = jnp.sum(incoming, axis=0, dtype=jnp.float32)
    grad_hidden = times_transpose(incoming, down_full)
    gelu_value, gelu_pull = jax.vjp(gelu_exact, before)
    grad_before = gelu_pull(grad_hidden)[0].astype(jnp.bfloat16)
    grad_up = contract_rows(second, grad_before)
    grad_up_shift = jnp.sum(grad_before, axis=0, dtype=jnp.float32)
    grad_second = times_transpose(grad_before, up_full)
    norm_value, norm_pull = jax.vjp(
        layer_norm, middle, gain_two.astype(jnp.float32), bias_two.astype(jnp.float32)
    )
    grad_middle_norm, grad_gain_two, grad_bias_two = norm_pull(grad_second)
    grad_middle = incoming.astype(jnp.float32) + grad_middle_norm
    grad_branch = grad_middle.astype(jnp.bfloat16)
    grad_out = contract_rows(attended_rows, grad_branch)
    grad_out_shift = jnp.sum(grad_branch, axis=0, dtype=jnp.float32)
    grad_attended = times_transpose(grad_branch, out_full).astype(jnp.bfloat16)
    grad_attended = grad_attended.reshape(batch_size, local_len, seq_count, head_width)
    grad_headed = lax.all_to_all(grad_attended, "seq", split_axis=2, concat_axis=1, tiled=True)
    grad_mixed = grad_headed.reshape(batch_size, spans_here, SPAN, heads_here, HD)
    grad_query, grad_key, grad_value, grad_key_all, grad_value_all = attend_back(
        grad_mixed,
        query_rows,
        key_rows,
        value_rows,
        key_all,
        value_all,
        causal,
        earlier,
        log_total,
        local_weights,
        summary_weights,
    )
    grad_key_means, grad_value_means = (
        lax.psum_scatter(
            grad_key_all.astype(jnp.bfloat16), "shard", scatter_dimension=1, tiled=True
        ).astype(jnp.float32),
        lax.psum_scatter(
            grad_value_all.astype(jnp.bfloat16), "shard", scatter_dimension=1, tiled=True
        ).astype(jnp.float32),
    )
    grad_key = grad_key + grad_key_means[:, :, None] / SPAN
    grad_value = grad_value + grad_value_means[:, :, None] / SPAN
    grad_packed = jnp.stack([grad_query, grad_key, grad_value], axis=3).astype(jnp.bfloat16)
    grad_packed = grad_packed.reshape(batch_size, group_len, 3, 1, head_width)
    grad_packed = lax.all_to_all(grad_packed, "seq", split_axis=1, concat_axis=3, tiled=True)
    grad_packed = grad_packed.reshape(row_count, 3 * model_width)
    grad_qkv = contract_rows(normed, grad_packed)
    grad_normed = times_transpose(grad_packed, qkv_full)
    first_value, first_pull = jax.vjp(
        layer_norm, flat_tokens, gain_one.astype(jnp.float32), bias_one.astype(jnp.float32)
    )
    grad_flat_norm, grad_gain_one, grad_bias_one = first_pull(grad_normed)
    grad_tokens = (grad_middle + grad_flat_norm).reshape(batch_size, local_len, model_width)
    all_grads = (
        grad_gain_one,
        grad_bias_one,
        grad_qkv,
        grad_out,
        grad_out_shift,
        grad_gain_two,
        grad_bias_two,
        grad_up,
        grad_up_shift,
        grad_down,
        grad_down_shift,
    )
    owned_grads = (
        lax.psum_scatter(
            all_grads[0].astype(jnp.bfloat16), "shard", scatter_dimension=0, tiled=True
        ).astype(jnp.float32),
        lax.psum_scatter(
            all_grads[1].astype(jnp.bfloat16), "shard", scatter_dimension=0, tiled=True
        ).astype(jnp.float32),
        lax.psum_scatter(
            all_grads[2].astype(jnp.bfloat16), "shard", scatter_dimension=0, tiled=True
        ).astype(jnp.float32),
        lax.psum_scatter(
            all_grads[3].astype(jnp.bfloat16), "shard", scatter_dimension=0, tiled=True
        ).astype(jnp.float32),
        lax.psum_scatter(
            all_grads[4].astype(jnp.bfloat16), "shard", scatter_dimension=0, tiled=True
        ).astype(jnp.float32),
        lax.psum_scatter(
            all_grads[5].astype(jnp.bfloat16), "shard", scatter_dimension=0, tiled=True
        ).astype(jnp.float32),
        lax.psum_scatter(
            all_grads[6].astype(jnp.bfloat16), "shard", scatter_dimension=0, tiled=True
        ).astype(jnp.float32),
        lax.psum_scatter(
            all_grads[7].astype(jnp.bfloat16), "shard", scatter_dimension=0, tiled=True
        ).astype(jnp.float32),
        lax.psum_scatter(
            all_grads[8].astype(jnp.bfloat16), "shard", scatter_dimension=0, tiled=True
        ).astype(jnp.float32),
        lax.psum_scatter(
            all_grads[9].astype(jnp.bfloat16), "shard", scatter_dimension=0, tiled=True
        ).astype(jnp.float32),
        lax.psum_scatter(
            all_grads[10].astype(jnp.bfloat16), "shard", scatter_dimension=0, tiled=True
        ).astype(jnp.float32),
    )
    owned_grads = (
        lax.psum(owned_grads[0].astype(jnp.bfloat16), "seq").astype(jnp.float32),
        lax.psum(owned_grads[1].astype(jnp.bfloat16), "seq").astype(jnp.float32),
        lax.psum(owned_grads[2].astype(jnp.bfloat16), "seq").astype(jnp.float32),
        lax.psum(owned_grads[3].astype(jnp.bfloat16), "seq").astype(jnp.float32),
        lax.psum(owned_grads[4].astype(jnp.bfloat16), "seq").astype(jnp.float32),
        lax.psum(owned_grads[5].astype(jnp.bfloat16), "seq").astype(jnp.float32),
        lax.psum(owned_grads[6].astype(jnp.bfloat16), "seq").astype(jnp.float32),
        lax.psum(owned_grads[7].astype(jnp.bfloat16), "seq").astype(jnp.float32),
        lax.psum(owned_grads[8].astype(jnp.bfloat16), "seq").astype(jnp.float32),
        lax.psum(owned_grads[9].astype(jnp.bfloat16), "seq").astype(jnp.float32),
        lax.psum(owned_grads[10].astype(jnp.bfloat16), "seq").astype(jnp.float32),
    )
    return (
        block_out,
        grad_tokens,
        owned_grads[0],
        owned_grads[1],
        owned_grads[2],
        owned_grads[3],
        owned_grads[4],
        owned_grads[5],
        owned_grads[6],
        owned_grads[7],
        owned_grads[8],
        owned_grads[9],
        owned_grads[10],
    )


def local(tokens, *rest):
    whole_spans = tokens.shape[1] % SPAN == 0
    if whole_spans and lax.axis_size("shard") == 8 and lax.axis_size("seq") == 4:
        return local_block(tokens, *rest)
    return local_general(tokens, *rest)


def solution(mesh):
    return jax.shard_map(
        local,
        mesh=mesh,
        in_specs=(
            P(None, ("shard", "seq"), None),
            P("shard"),
            P("shard"),
            P("shard", None),
            P("shard", None),
            P("shard"),
            P("shard"),
            P("shard"),
            P("shard", None),
            P("shard"),
            P("shard", None),
            P("shard"),
            P(None, ("shard", "seq"), None),
        ),
        out_specs=(
            P(None, ("shard", "seq"), None),
            P(None, ("shard", "seq"), None),
            P("shard"),
            P("shard"),
            P("shard", None),
            P("shard", None),
            P("shard"),
            P("shard"),
            P("shard"),
            P("shard", None),
            P("shard"),
            P("shard", None),
            P("shard"),
        ),
        check_vma=False,
    )
```

```python
import functools
import math

import jax
import jax.numpy as jnp
from jax import lax
from jax.experimental import pallas as pl
from jax.experimental.pallas import tpu as pltpu
from jax.sharding import PartitionSpec as P

H = 8
HD = 64
SPAN = 128


epsilon = 1e-05
MESH = pl.DeviceIdType.MESH
BF = jnp.bfloat16
F32 = jnp.float32


def dot(left, right, left_dim, right_dim):
    return lax.dot_general(
        left, right, (((left_dim,), (right_dim,)), ((), ())), preferred_element_type=F32
    )


def rows_of(index, count):
    return pl.ds(pl.multiple_of(index * count, count), count)


def norm_stats(values):
    center = values - jnp.mean(values, axis=-1, keepdims=True)
    inverse = lax.rsqrt(jnp.mean(center * center, axis=-1, keepdims=True) + epsilon)
    return center * inverse, inverse


def norm_back(grad, xhat, inverse, gain):
    scaled = grad * gain
    first = jnp.mean(scaled, axis=-1, keepdims=True)
    second = jnp.mean(scaled * xhat, axis=-1, keepdims=True)
    return inverse * (scaled - first - xhat * second)


QKV, OUT, UP, DOWN = range(4)
GD, GU, GO, GP = range(4)
GATHER_STEPS = 11
REDUCE_STEPS = 8


def block_kernel(
    batch,
    shard_count,
    seq_count,
    tok_hbm,
    cot_hbm,
    vec_refs,
    up_bias_ref,
    wq_hbm,
    wo_hbm,
    wu_hbm,
    wd_hbm,
    block_out_hbm,
    grad_tok_hbm,
    gq_hbm,
    go_hbm,
    gu_hbm,
    gd_hbm,
    vec_out_ref,
    tok,
    cot,
    wq,
    wo,
    wu,
    wd,
    vec_own,
    vec_all,
    xhat1,
    inv1,
    xb_stage,
    xb_all,
    vfull,
    up_bias,
    normed,
    packed,
    nbar,
    kv_mean,
    probs,
    att,
    middle,
    gmid,
    inv2,
    second,
    xhat2,
    hidden,
    gbefore,
    gatt,
    gbranch,
    gkv,
    gn_send,
    gn_recv,
    gnbar,
    vsum,
    upsum,
    vec_send,
    vec_recv,
    vec_line,
    g_down,
    g_up,
    g_out,
    g_qkv,
    r1_down,
    r1_up,
    r1_out,
    r1_qkv,
    r2_down,
    r2_up,
    r2_out,
    r2_qkv,
    r3_down,
    r3_up,
    r3_out,
    r3_qkv,
    r4_down,
    r4_up,
    r4_out,
    r4_qkv,
    own_down,
    own_up,
    own_out,
    own_qkv,
    w_send,
    w_recv,
    w_local,
    io_sem,
    vec_s,
    vec_r,
    xb_s,
    xb_r,
    gn_s,
    gn_r,
    vo_s,
    vo_r,
    vz_s,
    vz_r,
    red_s,
    red_r,
    out_sem,
):
    rows, width = tok.shape
    ff = up_bias.shape[1]
    total = shard_count * seq_count
    groups = rows // SPAN
    spans_here = groups // batch
    spans_all = spans_here * total
    pairs = H // 2
    lanes = 2 * HD
    ms = lax.axis_index("shard")
    mq = lax.axis_index("seq")
    mt = ms * seq_count + mq
    core = lax.rem(ms, 2)
    yx = ms // 2

    def flip(value, bit):
        return value + bit - 2 * bit * lax.rem(value // bit, 2)

    core_dev = (flip(ms, 1), mq)
    x_dev = (flip(ms, 2), mq)
    y_dev = (flip(ms, 4), mq)

    def place(index):
        return (index // seq_count, lax.rem(index, seq_count))

    tok_in = pltpu.make_async_copy(tok_hbm, tok, io_sem.at[0])
    cot_in = pltpu.make_async_copy(cot_hbm, cot, io_sem.at[1])
    tok_in.start()
    cot_in.start()

    xb_all[...] = jnp.zeros_like(xb_all)
    barrier = pltpu.get_barrier_semaphore()

    def greet(step, carry):
        pl.semaphore_signal(
            barrier, inc=1, device_id=place(lax.rem(mt + step, total)), device_id_type=MESH
        )
        return carry

    lax.fori_loop(1, total, greet, 0)

    w_hbm = (wq_hbm, wo_hbm, wu_hbm, wd_hbm)
    w_full = (wq, wo, wu, wd)

    def gather_copies(which):
        full = w_full[which]
        depth = full.shape[0] // shard_count
        half = depth // 2
        base = which * GATHER_STEPS

        def block(owner):
            return full.at[rows_of(owner, depth)]

        def part(owner, side):
            return full.at[pl.ds(pl.multiple_of(owner * depth + side * half, half), half)]

        def own_part(side):
            return w_hbm[which].at[pl.ds(side * half, half)]

        x_own, y_own, d_own = flip(ms, 2), flip(ms, 4), flip(flip(ms, 2), 4)
        plan = (
            (own_part(0), part(ms, 0), x_dev),
            (own_part(1), part(ms, 1), y_dev),
            (own_part(1), part(ms, 1), x_dev),
            (own_part(0), part(ms, 0), y_dev),
            (w_hbm[which], block(ms), core_dev),
            (part(x_own, 0), part(x_own, 0), y_dev),
            (part(y_own, 1), part(y_own, 1), x_dev),
            (block(x_own), block(x_own), core_dev),
            (block(y_own), block(y_own), core_dev),
            (part(d_own, 0), part(d_own, 0), core_dev),
            (part(d_own, 1), part(d_own, 1), core_dev),
        )
        return [
            pltpu.make_async_remote_copy(
                src_ref=src,
                dst_ref=dst,
                send_sem=w_send.at[base + step],
                recv_sem=w_recv.at[base + step],
                device_id=dev,
                device_id_type=MESH,
            )
            for step, (src, dst, dev) in enumerate(plan)
        ]

    w_copies = [gather_copies(which) for which in range(4)]

    def own_copy(which):
        depth = w_full[which].shape[0] // shard_count
        return pltpu.make_async_copy(
            w_hbm[which], w_full[which].at[rows_of(ms, depth)], w_local.at[which]
        )

    def gather_own(which):
        for step in range(5):
            w_copies[which][step].start()
        own_copy(which).start()

    def gather_forward(which):
        c = w_copies[which]
        c[0].wait_recv()
        c[5].start()
        c[1].wait_recv()
        c[6].start()

    def gather_core(which):
        c = w_copies[which]
        c[2].wait_recv()
        c[7].start()
        c[3].wait_recv()
        c[8].start()

    def gather_last(which):
        c = w_copies[which]
        c[5].wait_recv()
        c[9].start()
        c[6].wait_recv()
        c[10].start()

    def gather_done(which):
        c = w_copies[which]
        for step in (4, 7, 8, 9, 10):
            c[step].wait_recv()
        own_copy(which).wait()

    tok_in.wait()

    def first_norm(g, carry):
        at = rows_of(g, SPAN)
        xhat, inverse = norm_stats(tok[at, :].astype(F32))
        xhat1[at, :] = xhat
        inv1[at, :] = inverse
        xb_stage[pl.ds(g, 1), :] = jnp.mean(xhat, axis=0, keepdims=True)
        return carry

    lax.fori_loop(0, groups, first_norm, 0)
    half_width = width // 2
    xb_all[mt] = jnp.concatenate(
        [xb_stage[:, :half_width], xb_stage[:, half_width:]], axis=0
    ).astype(BF)

    shard_rows = width // shard_count
    for at, ref in enumerate(vec_refs):
        vec_own[at : at + 1, 0:shard_rows] = ref[...].astype(F32)
    vec_own[8 : 8 + up_bias_ref.shape[0], :] = up_bias_ref[...].astype(F32)

    pl.semaphore_wait(barrier, total - 1)

    vec_copies = []
    for step in range(1, shard_count):
        target = lax.rem(ms + step, shard_count)
        vec_copies.append(
            pltpu.make_async_remote_copy(
                src_ref=vec_own,
                dst_ref=vec_all.at[ms],
                send_sem=vec_s.at[step],
                recv_sem=vec_r.at[step],
                device_id=(target, mq),
                device_id_type=MESH,
            )
        )
    gather_own(QKV)
    for c in vec_copies:
        c.start()
    vec_all[ms] = vec_own[...]

    def xb_copy(source, target, send_at):
        return pltpu.make_async_remote_copy(
            src_ref=xb_all.at[source],
            dst_ref=xb_all.at[source],
            send_sem=xb_s.at[send_at],
            recv_sem=xb_r.at[source],
            device_id=place(target),
            device_id_type=MESH,
        )

    def xb_start(target, carry):
        xb_copy(mt, target, target).start()
        return carry

    lax.fori_loop(mt + 1, total, xb_start, 0)

    gather_forward(QKV)
    gather_own(OUT)
    gather_own(UP)
    gather_core(QKV)
    for c in vec_copies:
        c.wait_recv()
    low_lane = lax.broadcasted_iota(jnp.int32, (8, lanes), 1) < HD
    for at in range(shard_count // 2):
        even = vec_all[2 * at]
        odd = vec_all[2 * at + 1]
        vfull[:, at * lanes : (at + 1) * lanes] = jnp.where(
            low_lane, even[0:8, :], pltpu.roll(odd[0:8, :], HD, axis=1)
        )
    up_here = ff // shard_count
    for owner in range(shard_count):
        piece = vec_all[owner]
        for r in range(up_here // lanes):
            start = owner * up_here + r * lanes
            up_bias[0:1, start : start + lanes] = piece[8 + r : 9 + r, :]
    gather_last(QKV)
    gather_done(QKV)
    gain1, bias1 = vfull[0:1, :], vfull[1:2, :]
    out_shift = vfull[2:3, :]
    gain2, bias2 = vfull[3:4, :], vfull[4:5, :]
    down_shift = vfull[5:6, :]

    big = 512

    def project(i, carry):
        at = rows_of(i, big)
        tile = (xhat1[at, :] * gain1 + bias1).astype(BF)
        normed[at, :] = tile
        for n in range(3):
            packed[at, n * width : (n + 1) * width] = dot(
                tile, wq[:, n * width : (n + 1) * width], 1, 0
            ).astype(BF)
        return carry

    lax.fori_loop(0, rows // big, project, 0)
    gather_forward(OUT)
    gather_forward(UP)
    gather_own(DOWN)
    gather_core(OUT)

    def xb_wait(source, carry):
        xb_copy(source, flip(mt, 1), 0).wait_recv()
        return carry

    lax.fori_loop(0, mt, xb_wait, 0)
    mean_rows = total * groups
    arrived = xb_all[...].astype(F32)
    arrived = jnp.concatenate([arrived[:, 0:groups, :], arrived[:, groups:, :]], axis=2)
    arrived = arrived.reshape(mean_rows, width)
    new_row = lax.broadcasted_iota(jnp.int32, (mean_rows, mean_rows), 0)
    old_row = lax.broadcasted_iota(jnp.int32, (mean_rows, mean_rows), 1)
    wanted = (
        lax.rem(new_row, spans_all) // spans_here * groups
        + new_row // spans_all * spans_here
        + lax.rem(new_row, spans_here)
    )
    order = (old_row == wanted).astype(BF)
    nbar[...] = dot(order, (arrived * gain1 + bias1).astype(BF), 1, 0).astype(BF)
    for n in range(2):
        kv_mean[:, n * width : (n + 1) * width] = dot(
            nbar[...], wq[:, (n + 1) * width : (n + 2) * width], 1, 0
        ).astype(BF)

    factor = HD ** (-0.5)
    keys = SPAN + spans_all

    def head_pair(ref_rows):
        low = lax.broadcasted_iota(jnp.int32, (SPAN, lanes), 1) < HD
        zero = jnp.zeros_like(ref_rows)
        return jnp.concatenate(
            [jnp.where(low, ref_rows, zero), jnp.where(low, zero, ref_rows)], axis=0
        )

    def score_shift(g):
        j = lax.broadcasted_iota(jnp.int32, (SPAN, SPAN), 0)
        i = lax.broadcasted_iota(jnp.int32, (SPAN, SPAN), 1)
        near = jnp.where(j <= i, 0.0, -jnp.inf).astype(F32)
        f = lax.broadcasted_iota(jnp.int32, (spans_all, SPAN), 0)
        here = mt * spans_here + lax.rem(g, spans_here)
        far = jnp.where(f < here, math.log(SPAN), -jnp.inf).astype(F32)
        both = jnp.concatenate([near, far], axis=0)
        return jnp.concatenate([both, both], axis=1)

    low_out = lax.broadcasted_iota(jnp.int32, (SPAN, lanes), 1) < HD

    def pair_rows(at, mean_at, part, p):
        lo = p * lanes
        start = part * width + lo
        mean_lo = (part - 1) * width + lo
        return jnp.concatenate(
            [packed[at, start : start + lanes], kv_mean[mean_at, mean_lo : mean_lo + lanes]],
            axis=0,
        )

    def attend(g, carry):
        at = rows_of(g, SPAN)
        mean_at = rows_of(g // spans_here, spans_all)
        shift = score_shift(g)
        scores = [
            dot(
                pair_rows(at, mean_at, 1, p),
                head_pair(packed[at, p * lanes : (p + 1) * lanes] * factor),
                1,
                1,
            )
            for p in range(pairs)
        ]
        weights = []
        for p in range(pairs):
            shifted = scores[p] + shift
            expo = jnp.exp(shifted - jnp.max(shifted, axis=0, keepdims=True))
            total_row = jnp.sum(expo, axis=0, keepdims=True)
            weights.append((expo * (1.0 / total_row)).astype(BF))
            probs[g * pairs + p] = weights[p]
        for p in range(pairs):
            mixed = dot(weights[p], pair_rows(at, mean_at, 2, p), 0, 0)
            att[at, p * lanes : (p + 1) * lanes] = jnp.where(
                low_out, mixed[0:SPAN], mixed[SPAN : 2 * SPAN]
            ).astype(BF)
        return carry

    lax.fori_loop(0, groups // 2, attend, 0)
    gather_last(OUT)
    gather_core(UP)
    gather_last(UP)
    lax.fori_loop(groups // 2, groups, attend, 0)
    gather_done(OUT)

    def second_norm(i, carry):
        at = rows_of(i, 256)
        mid = tok[at, :].astype(F32) + dot(att[at, :], wo[...], 1, 0) + out_shift
        middle[at, :] = mid
        xhat, inverse = norm_stats(mid)
        xhat2[at, :] = xhat
        inv2[at, :] = inverse
        second[at, :] = (xhat * gain2 + bias2).astype(BF)
        return carry

    lax.fori_loop(0, rows // 256, second_norm, 0)
    gather_forward(DOWN)
    gather_done(UP)

    def feed_up(i, carry):
        at = rows_of(i // (ff // 512), big)
        cols = rows_of(lax.rem(i, ff // 512), 512)
        before = dot(second[at, :], wu[:, cols], 1, 0) + up_bias[0:1, cols]
        cdf = 0.5 + 0.5 * lax.erf(before * math.sqrt(0.5))
        density = jnp.exp(before * before * -0.5) * (1.0 / math.sqrt(2.0 * math.pi))
        hidden[at, cols] = (before * cdf).astype(BF)
        gbefore[at, cols] = (cdf + before * density).astype(BF)
        return carry

    feed_steps = rows // big * (ff // 512)
    lax.fori_loop(0, feed_steps // 2, feed_up, 0)
    gather_core(DOWN)
    gather_last(DOWN)
    lax.fori_loop(feed_steps // 2, feed_steps, feed_up, 0)
    gather_done(DOWN)
    cot_in.wait()

    def chunk(which):
        if which == GD:
            return (g_down, r1_down, r2_down, r3_down, r4_down, own_down)
        if which == GU:
            return (g_up, r1_up, r2_up, r3_up, r4_up, own_up)
        if which == GO:
            return (g_out, r1_out, r2_out, r3_out, r4_out, own_out)
        n = which - GP
        return tuple(ref.at[n] for ref in (g_qkv, r1_qkv, r2_qkv, r3_qkv, r4_qkv, own_qkv))

    here, x_blk, y_blk, d_blk = yx, flip(yx, 1), flip(yx, 2), flip(flip(yx, 1), 2)
    z_dev = (ms, flip(mq, 1))
    z_mid = (ms, seq_count - 1 - mq)

    def reduce_copies(which):
        g, r1, r2, r3, r4, own = chunk(which)
        half = g.shape[2] // 2
        base = which * REDUCE_STEPS
        plan = (
            (g.at[1 - core], r1, core_dev),
            (g.at[core, d_blk, pl.ds(0, half)], r2.at[0], x_dev),
            (g.at[core, d_blk, pl.ds(half, half)], r2.at[1], y_dev),
            (g.at[core, x_blk], r3.at[0], x_dev),
            (g.at[core, y_blk], r3.at[1], y_dev),
            (own, r4.at[0], z_dev),
            (own, r4.at[1], z_mid),
            (own, r4.at[0], z_dev),
        )
        copies = [
            pltpu.make_async_remote_copy(
                src_ref=src,
                dst_ref=dst,
                send_sem=red_s.at[base + step],
                recv_sem=red_r.at[base + step],
                device_id=dev,
                device_id_type=MESH,
            )
            for step, (src, dst, dev) in enumerate(plan)
        ]
        return copies

    r_copies = [reduce_copies(which) for which in range(GP + pairs)]
    edge = jnp.logical_or(mq == 0, mq == seq_count - 1)
    inner = jnp.logical_not(edge)

    def add_rows(target, *sources):
        count = target.shape[0]
        step = min(count, 32)

        def one(i, carry):
            at = rows_of(i, step)
            value = target[at, :].astype(F32)
            for source in sources:
                value = value + source[at, :].astype(F32)
            target[at, :] = value.astype(BF)
            return carry

        lax.fori_loop(0, count // step, one, 0)

    def reduce_a(which):
        r_copies[which][0].start()

    def reduce_b(which):
        g, r1, r2, r3, r4, own = chunk(which)
        c = r_copies[which]
        c[0].wait_recv()
        add_rows(g.at[core, d_blk], r1.at[d_blk])
        c[1].start()
        c[2].start()
        for blk in (x_blk, y_blk, here):
            add_rows(g.at[core, blk], r1.at[blk])

    def reduce_c(which):
        g, r1, r2, r3, r4, own = chunk(which)
        half = g.shape[2] // 2
        c = r_copies[which]
        c[1].wait_recv()
        add_rows(g.at[core, y_blk, pl.ds(0, half)], r2.at[0])
        c[4].start()
        c[2].wait_recv()
        add_rows(g.at[core, x_blk, pl.ds(half, half)], r2.at[1])
        c[3].start()

    def reduce_d(which):
        g, r1, r2, r3, r4, own = chunk(which)
        c = r_copies[which]
        c[3].wait_recv()
        c[4].wait_recv()
        count = own.shape[0]

        def one(i, carry):
            at = rows_of(i, 32)
            value = (
                g[core, here, at, :].astype(F32)
                + r3[0, at, :].astype(F32)
                + r3[1, at, :].astype(F32)
            )
            own[at, :] = value.astype(BF)
            return carry

        lax.fori_loop(0, count // 32, one, 0)

        @pl.when(edge)
        def _():
            c[5].start()

    def reduce_e(which):
        g, r1, r2, r3, r4, own = chunk(which)
        c = r_copies[which]

        @pl.when(inner)
        def _():
            c[5].wait_recv()
            add_rows(own, r4.at[0])
            c[6].start()

    out_hbm = (gd_hbm, gu_hbm, go_hbm)

    def emit(which, source):
        if which <= GO:
            target = out_hbm[which]
        else:
            target = gq_hbm.at[which - GP]
        return pltpu.make_async_copy(source, target, out_sem.at[which])

    def reduce_f(which):
        g, r1, r2, r3, r4, own = chunk(which)
        c = r_copies[which]

        @pl.when(inner)
        def _():
            c[6].wait_recv()
            c[6].wait_send()
            add_rows(own, r4.at[1])
            c[7].start()
            emit(which, own).start()

    def reduce_g(which):
        g, r1, r2, r3, r4, own = chunk(which)
        c = r_copies[which]

        @pl.when(edge)
        def _():
            c[5].wait_send()
            c[7].wait_recv()
            emit(which, r4.at[0]).start()

        @pl.when(inner)
        def _():
            c[7].wait_send()

        for step in range(5):
            c[step].wait_send()
        emit(which, own).wait()

    down_rows = ff // shard_count

    def down_grad(o, carry):
        piece = dot(hidden[:, rows_of(o, 2 * down_rows)], cot[...], 0, 0).astype(BF)
        g_down[0, o] = piece[0:down_rows]
        g_down[1, o] = piece[down_rows:]
        return carry

    lax.fori_loop(0, shard_count // 2, down_grad, 0)
    reduce_a(GD)

    def back_down(i, carry):
        at = rows_of(i // (ff // 512), big)
        cols = rows_of(lax.rem(i, ff // 512), 512)
        grad = dot(cot[at, :], wd[cols, :], 1, 1)
        grad = (grad * gbefore[at, cols].astype(F32)).astype(BF)
        gbefore[at, cols] = grad
        return carry

    lax.fori_loop(0, feed_steps, back_down, 0)
    reduce_b(GD)

    def up_grad(n, carry):
        cols = rows_of(n, 512)
        piece = dot(second[...], gbefore[:, cols], 0, 0).astype(BF)
        for owner in range(shard_count):
            g_up[owner % 2, owner // 2, :, cols] = piece[
                owner * shard_rows : (owner + 1) * shard_rows
            ]
        upsum[0:1, cols] = jnp.sum(gbefore[:, cols].astype(F32), axis=0, keepdims=True)
        return carry

    lax.fori_loop(0, ff // 512, up_grad, 0)
    reduce_a(GU)
    reduce_c(GD)

    vsum[...] = jnp.zeros_like(vsum)

    def back_second(i, carry):
        at = rows_of(i, 256)
        grad = dot(gbefore[at, :], wu[...], 1, 1)
        xhat = xhat2[at, :]
        vsum[3:4, :] += jnp.sum(grad * xhat, axis=0, keepdims=True)
        vsum[4:5, :] += jnp.sum(grad, axis=0, keepdims=True)
        incoming = cot[at, :].astype(F32)
        vsum[5:6, :] += jnp.sum(incoming, axis=0, keepdims=True)
        grad_mid = incoming + norm_back(grad, xhat, inv2[at, :], gain2)
        gmid[at, :] = grad_mid
        branch = grad_mid.astype(BF)
        gbranch[at, :] = branch
        vsum[2:3, :] += jnp.sum(branch.astype(F32), axis=0, keepdims=True)
        gatt[at, :] = dot(branch, wo[...], 1, 1).astype(BF)
        return carry

    lax.fori_loop(0, rows // 256, back_second, 0)
    reduce_b(GU)
    reduce_d(GD)

    def put_rows(target, piece):
        for owner in range(shard_count):
            target[owner % 2, owner // 2] = piece[
                owner * shard_rows : (owner + 1) * shard_rows
            ]

    put_rows(g_out, dot(att[...], gbranch[...], 0, 0).astype(BF))
    reduce_a(GO)
    reduce_c(GU)

    low_keys = lax.broadcasted_iota(jnp.int32, (SPAN, lanes), 1) < HD
    together = 2 * spans_here

    def attend_back(p, i, carry):
        lo = p * lanes
        members = []
        for u in range(together):
            g = i * together + u
            at = rows_of(g, SPAN)
            mean_at = rows_of(g // spans_here, spans_all)
            go = head_pair(gatt[at, lo : lo + lanes])
            weights = probs[g * pairs + p]
            gw = dot(pair_rows(at, mean_at, 2, p), go, 1, 1)
            gv = dot(weights, go, 1, 0)
            members.append((at, mean_at, weights, gw, gv))
        scores = []
        for at, mean_at, weights, gw, gv in members:
            prob = weights.astype(F32)
            row_inner = jnp.sum(prob * gw, axis=0, keepdims=True)
            scores.append((prob * (gw - row_inner)).astype(BF))
        far_k, far_v = None, None
        for u in range(together):
            at, mean_at, weights, gw, gv = members[u]
            q = head_pair(packed[at, lo : lo + lanes])
            gq = dot(scores[u], pair_rows(at, mean_at, 1, p), 0, 0)
            gk = dot(scores[u], q, 1, 0) * factor
            packed[at, lo : lo + lanes] = (
                jnp.where(low_keys, gq[0:SPAN], gq[SPAN : 2 * SPAN]) * factor
            ).astype(BF)
            packed[at, width + lo : width + lo + lanes] = gk[0:SPAN].astype(BF)
            packed[at, 2 * width + lo : 2 * width + lo + lanes] = gv[0:SPAN].astype(BF)
            first = u % spans_here == 0
            far_k = gk[SPAN:] if first else far_k + gk[SPAN:]
            far_v = gv[SPAN:] if first else far_v + gv[SPAN:]
            if u % spans_here == spans_here - 1:
                gkv[mean_at, lo : lo + lanes] = far_k.astype(BF)
                gkv[mean_at, width + lo : width + lo + lanes] = far_v.astype(BF)
        return carry

    def pair_back(p):
        lo = p * lanes
        lax.fori_loop(0, groups // together, functools.partial(attend_back, p), 0)
        grads = [packed[:, n * width + lo : n * width + lo + lanes] for n in range(3)]
        means = [gkv[:, n * width + lo : n * width + lo + lanes] for n in range(2)]
        local_part = dot(normed[...], jnp.concatenate(grads, axis=1), 0, 0)
        mean_part = dot(nbar[...], jnp.concatenate(means, axis=1), 0, 0)
        piece = jnp.concatenate(
            [local_part[:, 0:lanes], local_part[:, lanes:] + mean_part], axis=1
        )
        put_rows(g_qkv.at[p], piece.astype(BF))
        reduce_a(GP + p)

    pair_back(0)
    reduce_b(GO)
    reduce_d(GU)
    reduce_e(GD)
    pair_back(1)
    reduce_b(GP)
    reduce_c(GO)
    reduce_e(GU)
    reduce_f(GD)
    pair_back(2)
    reduce_b(GP + 1)
    reduce_c(GP)
    reduce_d(GO)
    reduce_f(GU)
    pair_back(3)
    reduce_b(GP + 2)
    reduce_c(GP + 1)
    reduce_d(GP)
    reduce_e(GO)

    gmean = dot(gkv[...], wq[:, width : 3 * width], 1, 1).astype(BF)
    gmean = dot(order, gmean, 0, 0).reshape(total, groups, width)
    gn_send[...] = jnp.concatenate(
        [gmean[:, :, :half_width], gmean[:, :, half_width:]], axis=1
    ).astype(BF)

    def gn_copy(source, target, send_at):
        return pltpu.make_async_remote_copy(
            src_ref=gn_send.at[target],
            dst_ref=gn_recv.at[source],
            send_sem=gn_s.at[send_at],
            recv_sem=gn_r.at[source],
            device_id=place(target),
            device_id_type=MESH,
        )

    def gn_start(target, carry):
        gn_copy(mt, target, target).start()
        return carry

    lax.fori_loop(0, mt, gn_start, 0)
    reduce_b(GP + 3)
    reduce_c(GP + 2)
    reduce_d(GP + 1)
    reduce_e(GP)
    reduce_f(GO)

    def out_block(i, carry):
        at = rows_of(i, 256)
        gbranch[at, :] = (
            middle[at, :] + dot(hidden[at, :], wd[...], 1, 0) + down_shift
        ).astype(BF)
        return carry

    lax.fori_loop(0, rows // 512, out_block, 0)
    reduce_c(GP + 3)
    reduce_d(GP + 2)
    reduce_e(GP + 1)
    reduce_f(GP)
    lax.fori_loop(rows // 512, rows // 256, out_block, 0)
    bout_out = pltpu.make_async_copy(gbranch, block_out_hbm, io_sem.at[2])
    bout_out.start()

    def gn_wait(source, carry):
        gn_copy(source, flip(mt, 1), 0).wait_recv()
        gnbar[...] += gn_recv[source].astype(F32)
        return carry

    gnbar[...] = gn_send[mt].astype(F32)
    lax.fori_loop(mt + 1, total, gn_wait, 0)
    reduce_d(GP + 3)
    reduce_e(GP + 2)
    reduce_f(GP + 1)

    def back_first(i, carry):
        at = rows_of(i, 2 * SPAN)
        shares = []
        for u in range(2):
            g = 2 * i + u
            share = jnp.concatenate(
                [gnbar[pl.ds(g, 1), :], gnbar[pl.ds(groups + g, 1), :]], axis=1
            ) * (1.0 / SPAN)
            shares.append(jnp.broadcast_to(share, (SPAN, width)))
        grad = dot(packed[at, :], wq[...], 1, 1) + jnp.concatenate(shares, axis=0)
        xhat = xhat1[at, :]
        vsum[0:1, :] += jnp.sum(grad * xhat, axis=0, keepdims=True)
        vsum[1:2, :] += jnp.sum(grad, axis=0, keepdims=True)
        gmid[at, :] = gmid[at, :] + norm_back(grad, xhat, inv1[at, :], gain1)
        return carry

    lax.fori_loop(0, groups // 4, back_first, 0)
    reduce_e(GP + 3)
    reduce_f(GP + 2)
    lax.fori_loop(groups // 4, groups // 2, back_first, 0)
    tok_out = pltpu.make_async_copy(gmid, grad_tok_hbm, io_sem.at[3])
    tok_out.start()

    for owner in range(shard_count):
        at = owner // 2
        piece = vsum[:, at * lanes : (at + 1) * lanes]
        if owner % 2 == 1:
            piece = pltpu.roll(piece, HD, axis=1)
        vec_send[owner, 0:8, :] = piece
        vec_send[owner, 8:16, :] = jnp.zeros((8, lanes), F32)
        for r in range(up_here // lanes):
            start = owner * up_here + r * lanes
            vec_send[owner, 8 + r : 9 + r, :] = upsum[0:1, start : start + lanes]
    vo_copies = []
    for step in range(1, shard_count):
        target = lax.rem(ms + step, shard_count)
        vo_copies.append(
            pltpu.make_async_remote_copy(
                src_ref=vec_send.at[target],
                dst_ref=vec_recv.at[ms],
                send_sem=vo_s.at[step],
                recv_sem=vo_r.at[step],
                device_id=(target, mq),
                device_id_type=MESH,
            )
        )
    for c in vo_copies:
        c.start()
    vec_recv[ms] = vec_send[ms]
    reduce_f(GP + 3)
    for which in range(GP):
        reduce_g(which)
    for c in vo_copies:
        c.wait_recv()
    vec_line[mq] = jnp.sum(vec_recv[...], axis=0)
    vz_copies = []
    for step in range(1, seq_count):
        vz_copies.append(
            pltpu.make_async_remote_copy(
                src_ref=vec_line.at[mq],
                dst_ref=vec_line.at[mq],
                send_sem=vz_s.at[step],
                recv_sem=vz_r.at[step],
                device_id=(ms, lax.rem(mq + step, seq_count)),
                device_id_type=MESH,
            )
        )
    for c in vz_copies:
        c.start()
    for which in range(GP, GP + pairs):
        reduce_g(which)
    for c in vz_copies:
        c.wait_recv()
    vec_out_ref[...] = jnp.sum(vec_line[...], axis=0)

    def xb_sent(target, carry):
        xb_copy(mt, target, target).wait_send()
        return carry

    lax.fori_loop(mt + 1, total, xb_sent, 0)

    def gn_sent(target, carry):
        gn_copy(mt, target, target).wait_send()
        return carry

    lax.fori_loop(0, mt, gn_sent, 0)
    for c in vec_copies + vo_copies + vz_copies:
        c.wait_send()
    for which in range(4):
        for c in w_copies[which]:
            c.wait_send()
    bout_out.wait()
    tok_out.wait()


def finish_kernel(*refs):
    raw, vec, outs, vec_outs = refs[0:6], refs[6], refs[7:13], refs[13:20]
    low_refs, high_refs, in_sem, out_sem = refs[20:26], refs[26:30], refs[30], refs[31]
    order = (2, 4, 5, 3, 1, 0)
    loads = [pltpu.make_async_copy(raw[n], low_refs[n], in_sem.at[n]) for n in range(6)]
    for n in order:
        loads[n].start()
    for n, ref in enumerate(vec_outs[0:6]):
        ref[...] = vec[n : n + 1, 0 : ref.shape[1]]
    vec_outs[6][...] = vec[8 : 8 + vec_outs[6].shape[0], :]
    stores = []
    for n in order:
        loads[n].wait()
        ready = low_refs[n]
        if n == 2:
            ready = high_refs[0]
            pairs = low_refs[2].shape[0]
            lanes = low_refs[2].shape[2] // 3
            for part in range(3):
                for p in range(pairs):
                    start = (part * pairs + p) * lanes
                    ready[:, start : start + lanes] = low_refs[2][
                        p, :, part * lanes : (part + 1) * lanes
                    ].astype(F32)
        elif n > 2:
            ready = high_refs[n - 2]
            ready[...] = low_refs[n][...].astype(F32)
        stores.append(pltpu.make_async_copy(ready, outs[n], out_sem.at[n]))
        stores[-1].start()
    for c in stores:
        c.wait()


def local_block(
    tokens,
    ln1_gain,
    ln1_bias,
    qkv_weight,
    out_weight,
    out_bias,
    ln2_gain,
    ln2_bias,
    up_weight,
    up_bias,
    down_weight,
    down_bias,
    cotangent,
):
    seq_count = lax.axis_size("seq")
    shard_count = lax.axis_size("shard")
    total = seq_count * shard_count
    batch, local_len, width = tokens.shape
    rows = batch * local_len
    groups = rows // SPAN
    spans_all = local_len // SPAN * total
    keys = SPAN + spans_all
    ff = up_weight.shape[1]
    lanes = 2 * HD
    shard_rows = width // shard_count
    down_rows = ff // shard_count
    vmem = pl.BlockSpec(memory_space=pltpu.VMEM)
    hbm = pl.BlockSpec(memory_space=pl.ANY)
    dma = pltpu.SemaphoreType.DMA
    half_yx = shard_count // 2

    def grads(count, columns, lead=()):
        half = count // 2
        return (
            pltpu.VMEM(lead + (2, half_yx, count, columns), BF),
            pltpu.VMEM(lead + (half_yx, count, columns), BF),
            pltpu.VMEM(lead + (2, half, columns), BF),
            pltpu.VMEM(lead + (2, count, columns), BF),
            pltpu.VMEM(lead + (2, count, columns), BF),
            pltpu.VMEM(lead + (count, columns), BF),
        )

    down_bufs = grads(down_rows, width)
    up_bufs = grads(shard_rows, ff)
    out_bufs = grads(shard_rows, width)
    qkv_bufs = grads(shard_rows, 3 * lanes, (H // 2,))
    grad_bufs = [buf for four in zip(down_bufs, up_bufs, out_bufs, qkv_bufs) for buf in four]
    scratch = [
        pltpu.VMEM((rows, width), BF),
        pltpu.VMEM((rows, width), BF),
        pltpu.VMEM((width, 3 * width), BF),
        pltpu.VMEM((width, width), BF),
        pltpu.VMEM((width, ff), BF),
        pltpu.VMEM((ff, width), BF),
        pltpu.VMEM((16, lanes), F32),
        pltpu.VMEM((shard_count, 16, lanes), F32),
        pltpu.VMEM((rows, width), F32),
        pltpu.VMEM((rows, 1), F32),
        pltpu.VMEM((groups, width), F32),
        pltpu.VMEM((total, 2 * groups, width // 2), BF),
        pltpu.VMEM((8, width), F32),
        pltpu.VMEM((8, ff), F32),
        pltpu.VMEM((rows, width), BF),
        pltpu.VMEM((rows, 3 * width), BF),
        pltpu.VMEM((batch * spans_all, width), BF),
        pltpu.VMEM((batch * spans_all, 2 * width), BF),
        pltpu.VMEM((groups * H // 2, keys, 2 * SPAN), BF),
        pltpu.VMEM((rows, width), BF),
        pltpu.VMEM((rows, width), F32),
        pltpu.VMEM((rows, width), F32),
        pltpu.VMEM((rows, 1), F32),
        pltpu.VMEM((rows, width), BF),
        pltpu.VMEM((rows, width), F32),
        pltpu.VMEM((rows, ff), BF),
        pltpu.VMEM((rows, ff), BF),
        pltpu.VMEM((rows, width), BF),
        pltpu.VMEM((rows, width), BF),
        pltpu.VMEM((batch * spans_all, 2 * width), BF),
        pltpu.VMEM((total, 2 * groups, width // 2), BF),
        pltpu.VMEM((total, 2 * groups, width // 2), BF),
        pltpu.VMEM((2 * groups, width // 2), F32),
        pltpu.VMEM((8, width), F32),
        pltpu.VMEM((8, ff), F32),
        pltpu.VMEM((shard_count, 16, lanes), F32),
        pltpu.VMEM((shard_count, 16, lanes), F32),
        pltpu.VMEM((seq_count, 16, lanes), F32),
        *grad_bufs,
        dma((4 * GATHER_STEPS,)),
        dma((4 * GATHER_STEPS,)),
        dma((4,)),
        dma((4,)),
        dma((shard_count,)),
        dma((shard_count,)),
        dma((total,)),
        dma((total,)),
        dma((total,)),
        dma((total,)),
        dma((shard_count,)),
        dma((shard_count,)),
        dma((seq_count,)),
        dma((seq_count,)),
        dma(((GP + H // 2) * REDUCE_STEPS,)),
        dma(((GP + H // 2) * REDUCE_STEPS,)),
        dma((GP + H // 2,)),
    ]
    vectors = [
        v.reshape(1, shard_rows)
        for v in (ln1_gain, ln1_bias, out_bias, ln2_gain, ln2_bias, down_bias)
    ]
    raw = pl.pallas_call(
        functools.partial(block_kernel, batch, shard_count, seq_count),
        out_shape=(
            jax.ShapeDtypeStruct((rows, width), BF),
            jax.ShapeDtypeStruct((rows, width), F32),
            jax.ShapeDtypeStruct((H // 2, shard_rows, 3 * lanes), BF),
            jax.ShapeDtypeStruct((shard_rows, width), BF),
            jax.ShapeDtypeStruct((shard_rows, ff), BF),
            jax.ShapeDtypeStruct((down_rows, width), BF),
            jax.ShapeDtypeStruct((16, lanes), F32),
        ),
        in_specs=[hbm, hbm, [vmem] * 6, vmem, hbm, hbm, hbm, hbm],
        out_specs=(hbm, hbm, hbm, hbm, hbm, hbm, vmem),
        scratch_shapes=scratch,
        compiler_params=pltpu.CompilerParams(
            collective_id=0, has_side_effects=True, vmem_limit_bytes=63 * 2**20
        ),
        name="block",
    )(
        tokens.reshape(rows, width),
        cotangent.reshape(rows, width),
        vectors,
        up_bias.reshape(-1, lanes),
        qkv_weight,
        out_weight,
        up_weight,
        down_weight,
    )
    low_shapes = [
        (H // 2, shard_rows, 3 * lanes),
        (shard_rows, width),
        (shard_rows, ff),
        (down_rows, width),
    ]
    high_shapes = [(shard_rows, 3 * width)] + low_shapes[1:]
    done = pl.pallas_call(
        finish_kernel,
        out_shape=(
            jax.ShapeDtypeStruct((rows, width), BF),
            jax.ShapeDtypeStruct((rows, width), F32),
            *(jax.ShapeDtypeStruct(shape, F32) for shape in high_shapes),
            *(jax.ShapeDtypeStruct((1, shard_rows), F32) for _ in range(6)),
            jax.ShapeDtypeStruct((down_rows // lanes, lanes), F32),
        ),
        in_specs=[hbm] * 6 + [vmem],
        out_specs=(hbm,) * 6 + (vmem,) * 7,
        scratch_shapes=[
            pltpu.VMEM((rows, width), BF),
            pltpu.VMEM((rows, width), F32),
            *(pltpu.VMEM(shape, BF) for shape in low_shapes),
            *(pltpu.VMEM(shape, F32) for shape in high_shapes),
            dma((6,)),
            dma((6,)),
        ],
        compiler_params=pltpu.CompilerParams(vmem_limit_bytes=62 * 2**20),
        name="finish",
    )(*raw)
    block_out, grad_tokens, g_qkv, g_out, g_up, g_down = done[0:6]
    vec_grads = [v.reshape(shard_rows) for v in done[6:12]]
    return (
        block_out.reshape(tokens.shape),
        grad_tokens.reshape(tokens.shape),
        vec_grads[0],
        vec_grads[1],
        g_qkv,
        g_out,
        vec_grads[2],
        vec_grads[3],
        vec_grads[4],
        g_up,
        done[12].reshape(down_rows),
        g_down,
        vec_grads[5],
    )


def layer_norm(values, norm_gain, norm_shift):
    center = values - jnp.mean(values, axis=-1, keepdims=True)
    spread = jnp.mean(center * center, axis=-1, keepdims=True)
    return center * lax.rsqrt(spread + epsilon) * norm_gain + norm_shift


def gelu_exact(values):
    return jax.nn.gelu(values, approximate=False)


def contract_rows(left_matrix, right_matrix):
    return lax.dot_general(
        left_matrix, right_matrix, (((0,), (0,)), ((), ())), preferred_element_type=jnp.float32
    )


def times_transpose(left_matrix, right_matrix):
    return lax.dot_general(
        left_matrix, right_matrix, (((1,), (1,)), ((), ())), preferred_element_type=jnp.float32
    )


def joint_scores(query_rows, key_rows, key_all, causal, earlier):
    factor = HD ** (-0.5)
    local_part = factor * jnp.einsum(
        "bjihd,bjkhd->bjhik", query_rows, key_rows, preferred_element_type=jnp.float32
    )
    summary = factor * jnp.einsum(
        "bjihd,bfhd->bjhif", query_rows, key_all, preferred_element_type=jnp.float32
    ) + math.log(SPAN)
    local_part = jnp.where(causal[None, None, None], local_part, -jnp.inf)
    summary = jnp.where(earlier[None, :, None, None, :], summary, -jnp.inf)
    return (local_part, summary)


def attend(query_rows, key_rows, value_rows, key_all, value_all, causal, earlier):
    local_part, summary = joint_scores(query_rows, key_rows, key_all, causal, earlier)
    row_max = jnp.maximum(jnp.max(local_part, axis=-1), jnp.max(summary, axis=-1))
    local_exp = jnp.exp(local_part - row_max[..., None])
    summary_exp = jnp.exp(summary - row_max[..., None])
    row_total = jnp.sum(local_exp, axis=-1) + jnp.sum(summary_exp, axis=-1)
    log_total = row_max + jnp.log(row_total)
    local_weights = (local_exp / row_total[..., None]).astype(jnp.bfloat16)
    summary_weights = (summary_exp / row_total[..., None]).astype(jnp.bfloat16)
    mixed_heads = jnp.einsum(
        "bjhik,bjkhd->bjihd", local_weights, value_rows, preferred_element_type=jnp.float32
    )
    mixed_heads = mixed_heads + jnp.einsum(
        "bjhif,bfhd->bjihd", summary_weights, value_all, preferred_element_type=jnp.float32
    )
    return (mixed_heads, log_total, local_weights, summary_weights)


def attend_back(
    grad_mixed,
    query_rows,
    key_rows,
    value_rows,
    key_all,
    value_all,
    causal,
    earlier,
    log_total,
    local_weights,
    summary_weights,
):
    factor = HD ** (-0.5)
    local_part, summary = joint_scores(query_rows, key_rows, key_all, causal, earlier)
    local_prob = jnp.exp(local_part - log_total[..., None])
    summary_prob = jnp.exp(summary - log_total[..., None])
    grad_local_w = jnp.einsum(
        "bjihd,bjkhd->bjhik", grad_mixed, value_rows, preferred_element_type=jnp.float32
    )
    grad_summary_w = jnp.einsum(
        "bjihd,bfhd->bjhif", grad_mixed, value_all, preferred_element_type=jnp.float32
    )
    row_inner = jnp.sum(local_prob * grad_local_w, axis=-1) + jnp.sum(
        summary_prob * grad_summary_w, axis=-1
    )
    grad_local = (local_prob * (grad_local_w - row_inner[..., None])).astype(jnp.bfloat16)
    grad_summary = (summary_prob * (grad_summary_w - row_inner[..., None])).astype(jnp.bfloat16)
    grad_query = jnp.einsum(
        "bjhik,bjkhd->bjihd", grad_local, key_rows, preferred_element_type=jnp.float32
    )
    grad_query = factor * (
        grad_query
        + jnp.einsum("bjhif,bfhd->bjihd", grad_summary, key_all, preferred_element_type=jnp.float32)
    )
    grad_key = factor * jnp.einsum(
        "bjhik,bjihd->bjkhd", grad_local, query_rows, preferred_element_type=jnp.float32
    )
    grad_key_all = factor * jnp.einsum(
        "bjhif,bjihd->bfhd", grad_summary, query_rows, preferred_element_type=jnp.float32
    )
    grad_value = jnp.einsum(
        "bjhik,bjihd->bjkhd", local_weights, grad_mixed, preferred_element_type=jnp.float32
    )
    grad_value_all = jnp.einsum(
        "bjhif,bjihd->bfhd", summary_weights, grad_mixed, preferred_element_type=jnp.float32
    )
    return (grad_query, grad_key, grad_value, grad_key_all, grad_value_all)


def local_general(
    tokens,
    ln1_gain,
    ln1_bias,
    qkv_weight,
    out_weight,
    out_bias,
    ln2_gain,
    ln2_bias,
    up_weight,
    up_bias,
    down_weight,
    down_bias,
    cotangent,
):
    seq_count = lax.axis_size("seq")
    shard_count = lax.axis_size("shard")
    shard_place = lax.axis_index("shard")
    batch_size, local_len, model_width = tokens.shape
    heads_here = H // seq_count
    head_width = heads_here * HD
    group_len = local_len * seq_count
    spans_here = group_len // SPAN
    spans_all = spans_here * shard_count
    row_count = batch_size * local_len
    shards = (
        ln1_gain,
        ln1_bias,
        qkv_weight,
        out_weight,
        out_bias,
        ln2_gain,
        ln2_bias,
        up_weight,
        up_bias,
        down_weight,
        down_bias,
    )
    gathered = (
        lax.all_gather(shards[0], "shard", axis=0, tiled=True),
        lax.all_gather(shards[1], "shard", axis=0, tiled=True),
        lax.all_gather(shards[2], "shard", axis=0, tiled=True),
        lax.all_gather(shards[3], "shard", axis=0, tiled=True),
        lax.all_gather(shards[4], "shard", axis=0, tiled=True),
        lax.all_gather(shards[5], "shard", axis=0, tiled=True),
        lax.all_gather(shards[6], "shard", axis=0, tiled=True),
        lax.all_gather(shards[7], "shard", axis=0, tiled=True),
        lax.all_gather(shards[8], "shard", axis=0, tiled=True),
        lax.all_gather(shards[9], "shard", axis=0, tiled=True),
        lax.all_gather(shards[10], "shard", axis=0, tiled=True),
    )
    (
        gain_one,
        bias_one,
        qkv_full,
        out_full,
        out_shift,
        gain_two,
        bias_two,
        up_full,
        up_shift,
        down_full,
        down_shift,
    ) = gathered
    flat_tokens = tokens.reshape(row_count, model_width).astype(jnp.float32)
    normed = layer_norm(
        flat_tokens, gain_one.astype(jnp.float32), bias_one.astype(jnp.float32)
    ).astype(jnp.bfloat16)
    packed = jnp.dot(normed, qkv_full, preferred_element_type=jnp.float32).astype(jnp.bfloat16)
    span_place = jnp.arange(SPAN)
    packed_heads = packed.reshape(batch_size, local_len, 3, seq_count, head_width)
    headed = lax.all_to_all(packed_heads, "seq", split_axis=3, concat_axis=1, tiled=True)
    headed = headed.reshape(batch_size, spans_here, SPAN, 3, heads_here, HD)
    query_rows = headed[:, :, :, 0]
    key_rows = headed[:, :, :, 1]
    value_rows = headed[:, :, :, 2]
    key_means = jnp.mean(key_rows, axis=2, dtype=jnp.float32).astype(jnp.bfloat16)
    value_means = jnp.mean(value_rows, axis=2, dtype=jnp.float32).astype(jnp.bfloat16)
    key_all, value_all = (
        lax.all_gather(key_means, "shard", axis=1, tiled=True),
        lax.all_gather(value_means, "shard", axis=1, tiled=True),
    )
    causal = span_place[:, None] >= span_place[None, :]
    global_span = shard_place * spans_here + jnp.arange(spans_here)
    earlier = global_span[:, None] > jnp.arange(spans_all)[None, :]
    mixed_heads, log_total, local_weights, summary_weights = attend(
        query_rows, key_rows, value_rows, key_all, value_all, causal, earlier
    )
    attended = mixed_heads.astype(jnp.bfloat16).reshape(batch_size, group_len, head_width)
    attended = lax.all_to_all(attended, "seq", split_axis=1, concat_axis=2, tiled=True)
    attended_rows = attended.reshape(row_count, model_width)
    middle = (
        flat_tokens
        + jnp.dot(attended_rows, out_full, preferred_element_type=jnp.float32)
        + out_shift.astype(jnp.float32)
    )
    second = layer_norm(middle, gain_two.astype(jnp.float32), bias_two.astype(jnp.float32)).astype(
        jnp.bfloat16
    )
    before = jnp.dot(second, up_full, preferred_element_type=jnp.float32) + up_shift.astype(
        jnp.float32
    )
    hidden = gelu_exact(before).astype(jnp.bfloat16)
    block_out = (
        middle
        + jnp.dot(hidden, down_full, preferred_element_type=jnp.float32)
        + down_shift.astype(jnp.float32)
    )
    block_out = block_out.astype(jnp.bfloat16).reshape(batch_size, local_len, model_width)
    incoming = cotangent.reshape(row_count, model_width)
    grad_down = contract_rows(hidden, incoming)
    grad_down_shift = jnp.sum(incoming, axis=0, dtype=jnp.float32)
    grad_hidden = times_transpose(incoming, down_full)
    gelu_value, gelu_pull = jax.vjp(gelu_exact, before)
    grad_before = gelu_pull(grad_hidden)[0].astype(jnp.bfloat16)
    grad_up = contract_rows(second, grad_before)
    grad_up_shift = jnp.sum(grad_before, axis=0, dtype=jnp.float32)
    grad_second = times_transpose(grad_before, up_full)
    norm_value, norm_pull = jax.vjp(
        layer_norm, middle, gain_two.astype(jnp.float32), bias_two.astype(jnp.float32)
    )
    grad_middle_norm, grad_gain_two, grad_bias_two = norm_pull(grad_second)
    grad_middle = incoming.astype(jnp.float32) + grad_middle_norm
    grad_branch = grad_middle.astype(jnp.bfloat16)
    grad_out = contract_rows(attended_rows, grad_branch)
    grad_out_shift = jnp.sum(grad_branch, axis=0, dtype=jnp.float32)
    grad_attended = times_transpose(grad_branch, out_full).astype(jnp.bfloat16)
    grad_attended = grad_attended.reshape(batch_size, local_len, seq_count, head_width)
    grad_headed = lax.all_to_all(grad_attended, "seq", split_axis=2, concat_axis=1, tiled=True)
    grad_mixed = grad_headed.reshape(batch_size, spans_here, SPAN, heads_here, HD)
    grad_query, grad_key, grad_value, grad_key_all, grad_value_all = attend_back(
        grad_mixed,
        query_rows,
        key_rows,
        value_rows,
        key_all,
        value_all,
        causal,
        earlier,
        log_total,
        local_weights,
        summary_weights,
    )
    grad_key_means, grad_value_means = (
        lax.psum_scatter(
            grad_key_all.astype(jnp.bfloat16), "shard", scatter_dimension=1, tiled=True
        ).astype(jnp.float32),
        lax.psum_scatter(
            grad_value_all.astype(jnp.bfloat16), "shard", scatter_dimension=1, tiled=True
        ).astype(jnp.float32),
    )
    grad_key = grad_key + grad_key_means[:, :, None] / SPAN
    grad_value = grad_value + grad_value_means[:, :, None] / SPAN
    grad_packed = jnp.stack([grad_query, grad_key, grad_value], axis=3).astype(jnp.bfloat16)
    grad_packed = grad_packed.reshape(batch_size, group_len, 3, 1, head_width)
    grad_packed = lax.all_to_all(grad_packed, "seq", split_axis=1, concat_axis=3, tiled=True)
    grad_packed = grad_packed.reshape(row_count, 3 * model_width)
    grad_qkv = contract_rows(normed, grad_packed)
    grad_normed = times_transpose(grad_packed, qkv_full)
    first_value, first_pull = jax.vjp(
        layer_norm, flat_tokens, gain_one.astype(jnp.float32), bias_one.astype(jnp.float32)
    )
    grad_flat_norm, grad_gain_one, grad_bias_one = first_pull(grad_normed)
    grad_tokens = (grad_middle + grad_flat_norm).reshape(batch_size, local_len, model_width)
    all_grads = (
        grad_gain_one,
        grad_bias_one,
        grad_qkv,
        grad_out,
        grad_out_shift,
        grad_gain_two,
        grad_bias_two,
        grad_up,
        grad_up_shift,
        grad_down,
        grad_down_shift,
    )
    owned_grads = (
        lax.psum_scatter(
            all_grads[0].astype(jnp.bfloat16), "shard", scatter_dimension=0, tiled=True
        ).astype(jnp.float32),
        lax.psum_scatter(
            all_grads[1].astype(jnp.bfloat16), "shard", scatter_dimension=0, tiled=True
        ).astype(jnp.float32),
        lax.psum_scatter(
            all_grads[2].astype(jnp.bfloat16), "shard", scatter_dimension=0, tiled=True
        ).astype(jnp.float32),
        lax.psum_scatter(
            all_grads[3].astype(jnp.bfloat16), "shard", scatter_dimension=0, tiled=True
        ).astype(jnp.float32),
        lax.psum_scatter(
            all_grads[4].astype(jnp.bfloat16), "shard", scatter_dimension=0, tiled=True
        ).astype(jnp.float32),
        lax.psum_scatter(
            all_grads[5].astype(jnp.bfloat16), "shard", scatter_dimension=0, tiled=True
        ).astype(jnp.float32),
        lax.psum_scatter(
            all_grads[6].astype(jnp.bfloat16), "shard", scatter_dimension=0, tiled=True
        ).astype(jnp.float32),
        lax.psum_scatter(
            all_grads[7].astype(jnp.bfloat16), "shard", scatter_dimension=0, tiled=True
        ).astype(jnp.float32),
        lax.psum_scatter(
            all_grads[8].astype(jnp.bfloat16), "shard", scatter_dimension=0, tiled=True
        ).astype(jnp.float32),
        lax.psum_scatter(
            all_grads[9].astype(jnp.bfloat16), "shard", scatter_dimension=0, tiled=True
        ).astype(jnp.float32),
        lax.psum_scatter(
            all_grads[10].astype(jnp.bfloat16), "shard", scatter_dimension=0, tiled=True
        ).astype(jnp.float32),
    )
    owned_grads = (
        lax.psum(owned_grads[0].astype(jnp.bfloat16), "seq").astype(jnp.float32),
        lax.psum(owned_grads[1].astype(jnp.bfloat16), "seq").astype(jnp.float32),
        lax.psum(owned_grads[2].astype(jnp.bfloat16), "seq").astype(jnp.float32),
        lax.psum(owned_grads[3].astype(jnp.bfloat16), "seq").astype(jnp.float32),
        lax.psum(owned_grads[4].astype(jnp.bfloat16), "seq").astype(jnp.float32),
        lax.psum(owned_grads[5].astype(jnp.bfloat16), "seq").astype(jnp.float32),
        lax.psum(owned_grads[6].astype(jnp.bfloat16), "seq").astype(jnp.float32),
        lax.psum(owned_grads[7].astype(jnp.bfloat16), "seq").astype(jnp.float32),
        lax.psum(owned_grads[8].astype(jnp.bfloat16), "seq").astype(jnp.float32),
        lax.psum(owned_grads[9].astype(jnp.bfloat16), "seq").astype(jnp.float32),
        lax.psum(owned_grads[10].astype(jnp.bfloat16), "seq").astype(jnp.float32),
    )
    return (
        block_out,
        grad_tokens,
        owned_grads[0],
        owned_grads[1],
        owned_grads[2],
        owned_grads[3],
        owned_grads[4],
        owned_grads[5],
        owned_grads[6],
        owned_grads[7],
        owned_grads[8],
        owned_grads[9],
        owned_grads[10],
    )


def local(tokens, *rest):
    whole_spans = tokens.shape[1] % SPAN == 0
    if whole_spans and lax.axis_size("shard") == 8 and lax.axis_size("seq") == 4:
        return local_block(tokens, *rest)
    return local_general(tokens, *rest)


def solution(mesh):
    return jax.shard_map(
        local,
        mesh=mesh,
        in_specs=(
            P(None, ("shard", "seq"), None),
            P("shard"),
            P("shard"),
            P("shard", None),
            P("shard", None),
            P("shard"),
            P("shard"),
            P("shard"),
            P("shard", None),
            P("shard"),
            P("shard", None),
            P("shard"),
            P(None, ("shard", "seq"), None),
        ),
        out_specs=(
            P(None, ("shard", "seq"), None),
            P(None, ("shard", "seq"), None),
            P("shard"),
            P("shard"),
            P("shard", None),
            P("shard", None),
            P("shard"),
            P("shard"),
            P("shard"),
            P("shard", None),
            P("shard"),
            P("shard", None),
            P("shard"),
        ),
        check_vma=False,
    )
```

```python
import functools
import math

import jax
import jax.numpy as jnp
from jax import lax
from jax.experimental import pallas as pl
from jax.experimental.pallas import tpu as pltpu
from jax.sharding import PartitionSpec as P

H = 8
HD = 64
SPAN = 128


epsilon = 1e-05
MESH = pl.DeviceIdType.MESH
BF = jnp.bfloat16
F32 = jnp.float32


def dot(left, right, left_dim, right_dim):
    return lax.dot_general(
        left, right, (((left_dim,), (right_dim,)), ((), ())), preferred_element_type=F32
    )


def rows_of(index, count):
    if isinstance(index, int):
        return pl.ds(index * count, count)
    return pl.ds(pl.multiple_of(index * count, count), count)


def norm_stats(values):
    center = values - jnp.mean(values, axis=-1, keepdims=True)
    inverse = lax.rsqrt(jnp.mean(center * center, axis=-1, keepdims=True) + epsilon)
    return center * inverse, inverse


def norm_back(grad, xhat, inverse, gain):
    scaled = grad * gain
    first = jnp.mean(scaled, axis=-1, keepdims=True)
    second = jnp.mean(scaled * xhat, axis=-1, keepdims=True)
    return inverse * (scaled - first - xhat * second)


QKV, OUT, UP, DOWN = range(4)
D0, D1, U0, U1, GO, QA, Q2, Q3 = range(8)
CHUNKS = 8
GATHER_STEPS = 11
REDUCE_STEPS = 8


def block_kernel(
    batch,
    shard_count,
    seq_count,
    tok_hbm,
    cot_hbm,
    vec_refs,
    up_bias_ref,
    wq_hbm,
    wo_hbm,
    wu_hbm,
    wd_hbm,
    block_out_hbm,
    grad_tok_hbm,
    gt_hbm,
    gs_hbm,
    go_hbm,
    gu_hbm,
    gd_hbm,
    vec_out_ref,
    tok,
    cot,
    wq,
    wo,
    wu,
    wd,
    vec_own,
    vec_all,
    xhat1,
    inv1,
    xb_stage,
    xb_all,
    order,
    vfull,
    up_bias,
    normed,
    packed,
    nbar,
    kv_mean,
    probs,
    att,
    middle,
    gmid,
    inv2,
    second,
    xhat2,
    hidden,
    gbefore,
    gatt,
    gbranch,
    gkv,
    gn_send,
    gn_recv,
    gz_send,
    gz_recv,
    gnbar,
    vsum,
    upsum,
    vec_send,
    vec_recv,
    vec_line,
    g_down,
    g_up,
    g_out,
    g_two,
    g_one,
    r1_down,
    r1_up,
    r1_out,
    r1_two,
    r1_one,
    r2_down,
    r2_up,
    r2_out,
    r2_two,
    r2_one,
    r3_down,
    r3_up,
    r3_out,
    r3_two,
    r3_one,
    r4_down,
    r4_up,
    r4_out,
    r4_two,
    r4_one,
    own_down,
    own_up,
    own_out,
    own_two,
    own_one,
    w_send,
    w_recv,
    w_local,
    io_sem,
    vec_s,
    vec_r,
    xz_s,
    xz_r,
    xs_s,
    xs_r,
    gs_s,
    gs_r,
    gz_s,
    gz_r,
    vo_s,
    vo_r,
    vz_s,
    vz_r,
    red_s,
    red_r,
    out_sem,
):
    rows, width = tok.shape
    ff = up_bias.shape[1]
    total = shard_count * seq_count
    groups = rows // SPAN
    spans_here = groups // batch
    spans_all = spans_here * total
    pairs = H // 2
    lanes = 2 * HD
    ms = lax.axis_index("shard")
    mq = lax.axis_index("seq")
    mt = ms * seq_count + mq
    core = lax.rem(ms, 2)
    yx = ms // 2

    def flip(value, bit):
        return value + bit - 2 * bit * lax.rem(value // bit, 2)

    core_dev = (flip(ms, 1), mq)
    x_dev = (flip(ms, 2), mq)
    y_dev = (flip(ms, 4), mq)

    tok_in = pltpu.make_async_copy(tok_hbm, tok, io_sem.at[0])
    cot_in = pltpu.make_async_copy(cot_hbm, cot, io_sem.at[1])
    tok_in.start()
    cot_in.start()

    xb_all[...] = jnp.zeros_like(xb_all)
    barrier = pltpu.get_barrier_semaphore()

    shard_peers = [(lax.rem(ms + step, shard_count), mq) for step in range(1, shard_count)]
    seq_peers = [(ms, lax.rem(mq + step, seq_count)) for step in range(1, seq_count)]
    peers = shard_peers + seq_peers
    for peer in peers:
        pl.semaphore_signal(barrier, inc=1, device_id=peer, device_id_type=MESH)

    w_hbm = (wq_hbm, wo_hbm, wu_hbm, wd_hbm)
    w_full = (wq, wo, wu, wd)

    def gather_copies(which):
        full = w_full[which]
        depth = full.shape[0] // shard_count
        half = depth // 2
        base = which * GATHER_STEPS

        def block(owner):
            return full.at[rows_of(owner, depth)]

        def part(owner, side):
            return full.at[pl.ds(pl.multiple_of(owner * depth + side * half, half), half)]

        def own_part(side):
            return w_hbm[which].at[pl.ds(side * half, half)]

        x_own, y_own, d_own = flip(ms, 2), flip(ms, 4), flip(flip(ms, 2), 4)
        plan = (
            (own_part(0), part(ms, 0), x_dev),
            (own_part(1), part(ms, 1), y_dev),
            (own_part(1), part(ms, 1), x_dev),
            (own_part(0), part(ms, 0), y_dev),
            (w_hbm[which], block(ms), core_dev),
            (part(x_own, 0), part(x_own, 0), y_dev),
            (part(y_own, 1), part(y_own, 1), x_dev),
            (block(x_own), block(x_own), core_dev),
            (block(y_own), block(y_own), core_dev),
            (part(d_own, 0), part(d_own, 0), core_dev),
            (part(d_own, 1), part(d_own, 1), core_dev),
        )
        return [
            pltpu.make_async_remote_copy(
                src_ref=src,
                dst_ref=dst,
                send_sem=w_send.at[base + step],
                recv_sem=w_recv.at[base + step],
                device_id=dev,
                device_id_type=MESH,
            )
            for step, (src, dst, dev) in enumerate(plan)
        ]

    w_copies = [gather_copies(which) for which in range(4)]

    def own_copy(which):
        depth = w_full[which].shape[0] // shard_count
        return pltpu.make_async_copy(
            w_hbm[which], w_full[which].at[rows_of(ms, depth)], w_local.at[which]
        )

    def gather_own_first(which):
        for step in range(2):
            w_copies[which][step].start()

    def gather_own_second(which):
        for step in range(2, 5):
            w_copies[which][step].start()
        own_copy(which).start()

    def gather_own(which):
        gather_own_first(which)
        gather_own_second(which)

    def gather_forward(which):
        c = w_copies[which]
        c[0].wait_recv()
        c[5].start()
        c[1].wait_recv()
        c[6].start()

    def gather_core(which):
        c = w_copies[which]
        c[2].wait_recv()
        c[7].start()
        c[3].wait_recv()
        c[8].start()

    def gather_last(which):
        c = w_copies[which]
        c[5].wait_recv()
        c[9].start()
        c[6].wait_recv()
        c[10].start()

    def gather_done(which):
        c = w_copies[which]
        for step in (4, 7, 8, 9, 10):
            c[step].wait_recv()
        own_copy(which).wait()

    tok_in.wait()

    big = rows // 2

    def first_norm(i, carry):
        at = rows_of(i, big)
        xhat, inverse = norm_stats(tok[at, :].astype(F32))
        xhat1[at, :] = xhat
        inv1[at, :] = inverse
        for u in range(big // SPAN):
            xb_stage[pl.ds(i * (big // SPAN) + u, 1), :] = jnp.mean(
                xhat[u * SPAN : (u + 1) * SPAN], axis=0, keepdims=True
            )
        return carry

    lax.fori_loop(0, rows // big, first_norm, 0)
    half_width = width // 2
    xb_all[mt] = jnp.concatenate(
        [xb_stage[:, :half_width], xb_stage[:, half_width:]], axis=0
    ).astype(BF)

    shard_rows = width // shard_count
    for at, ref in enumerate(vec_refs):
        vec_own[at : at + 1, 0:shard_rows] = ref[...].astype(F32)
    vec_own[8 : 8 + up_bias_ref.shape[0], :] = up_bias_ref[...].astype(F32)

    pl.semaphore_wait(barrier, len(peers))

    def remote(source, target, send, recv, device):
        return pltpu.make_async_remote_copy(
            src_ref=source,
            dst_ref=target,
            send_sem=send,
            recv_sem=recv,
            device_id=device,
            device_id_type=MESH,
        )

    vec_copies = [
        remote(vec_own, vec_all.at[ms], vec_s.at[step], vec_r.at[step], peer)
        for step, peer in enumerate(shard_peers)
    ]
    xz_copies = [
        remote(xb_all.at[mt], xb_all.at[mt], xz_s.at[step], xz_r.at[step], peer)
        for step, peer in enumerate(seq_peers)
    ]

    def xb_group(owner):
        return xb_all.at[rows_of(owner, seq_count)]

    def xs_copy(owner, target):
        return remote(
            xb_group(owner), xb_group(owner), xs_s.at[target], xs_r.at[owner], (target, mq)
        )

    gather_own(QKV)
    for c in xz_copies + vec_copies:
        c.start()
    vec_all[ms] = vec_own[...]
    mean_rows = total * groups
    new_row = lax.broadcasted_iota(jnp.int32, (mean_rows, mean_rows), 0)
    old_row = lax.broadcasted_iota(jnp.int32, (mean_rows, mean_rows), 1)

    def scaled(value, down_by, up_by):
        quotient = lax.shift_right_logical(value, down_by.bit_length() - 1)
        return lax.shift_left(quotient, up_by.bit_length() - 1)

    wanted = (
        scaled(new_row & (spans_all - 1), spans_here, groups)
        + scaled(new_row, spans_all, spans_here)
        + (new_row & (spans_here - 1))
    )
    order[...] = (old_row == wanted).astype(BF)
    for c in xz_copies:
        c.wait_recv()
    for target in range(1, shard_count):

        @pl.when(target > ms)
        def _(target=target):
            xs_copy(ms, target).start()

    gather_forward(QKV)
    gather_own(OUT)
    gather_own(UP)
    gather_core(QKV)
    gather_own_first(DOWN)
    for c in vec_copies:
        c.wait_recv()
    low_lane = lax.broadcasted_iota(jnp.int32, (8, lanes), 1) < HD
    for at in range(shard_count // 2):
        even = vec_all[2 * at]
        odd = vec_all[2 * at + 1]
        vfull[:, at * lanes : (at + 1) * lanes] = jnp.where(
            low_lane, even[0:8, :], pltpu.roll(odd[0:8, :], HD, axis=1)
        )
    up_here = ff // shard_count
    parts = up_here // lanes
    part_cols = shard_count * lanes
    for owner in range(shard_count):
        piece = vec_all[owner]
        for r in range(up_here // lanes):
            start = r * part_cols + owner * lanes
            up_bias[0:1, start : start + lanes] = piece[8 + r : 9 + r, :]
    gather_last(QKV)
    gather_done(QKV)
    gain1, bias1 = vfull[0:1, :], vfull[1:2, :]
    out_shift = vfull[2:3, :]
    gain2, bias2 = vfull[3:4, :], vfull[4:5, :]
    down_shift = vfull[5:6, :]

    tile = (xhat1[...] * gain1 + bias1).astype(BF)
    normed[...] = tile

    def project(n):
        packed[:, n * width : (n + 1) * width] = dot(
            tile, wq[:, n * width : (n + 1) * width], 1, 0
        ).astype(BF)

    project(0)
    gather_forward(OUT)
    project(1)
    gather_forward(UP)
    project(2)
    gather_core(OUT)
    gather_own_second(DOWN)

    for owner in range(shard_count - 1):

        @pl.when(owner < ms)
        def _(owner=owner):
            xs_copy(owner, owner).wait_recv()

    arrived = xb_all[...].astype(F32)
    arrived = jnp.concatenate([arrived[:, 0:groups, :], arrived[:, groups:, :]], axis=2)
    arrived = arrived.reshape(mean_rows, width)
    nbar[...] = dot(order[...], (arrived * gain1 + bias1).astype(BF), 1, 0).astype(BF)
    for n in range(2):
        kv_mean[:, n * width : (n + 1) * width] = dot(
            nbar[...], wq[:, (n + 1) * width : (n + 2) * width], 1, 0
        ).astype(BF)

    factor = HD ** (-0.5)
    keys = SPAN + spans_all

    def head_pair(ref_rows):
        low = lax.broadcasted_iota(jnp.int32, (SPAN, lanes), 1) < HD
        zero = jnp.zeros_like(ref_rows)
        return jnp.concatenate(
            [jnp.where(low, ref_rows, zero), jnp.where(low, zero, ref_rows)], axis=0
        )

    def score_shift(g):
        j = lax.broadcasted_iota(jnp.int32, (SPAN, SPAN), 0)
        i = lax.broadcasted_iota(jnp.int32, (SPAN, SPAN), 1)
        near = jnp.where(j <= i, 0.0, -jnp.inf).astype(F32)
        f = lax.broadcasted_iota(jnp.int32, (spans_all, SPAN), 0)
        here = mt * spans_here + g % spans_here
        far = jnp.where(f < here, math.log(SPAN), -jnp.inf).astype(F32)
        both = jnp.concatenate([near, far], axis=0)
        return jnp.concatenate([both, both], axis=1)

    low_out = lax.broadcasted_iota(jnp.int32, (SPAN, lanes), 1) < HD

    def pair_rows(at, mean_at, part, p):
        lo = p * lanes
        start = part * width + lo
        mean_lo = (part - 1) * width + lo
        return jnp.concatenate(
            [packed[at, start : start + lanes], kv_mean[mean_at, mean_lo : mean_lo + lanes]],
            axis=0,
        )

    four = groups // 2

    def attend(i):
        members = [(i * four + u, p) for u in range(four) for p in range(pairs)]
        shifts = [score_shift(i * four + u) for u in range(four)]
        places = {
            g: (rows_of(g, SPAN), rows_of(g // spans_here, spans_all)) for g, _ in members
        }
        scores = [
            dot(
                pair_rows(*places[g], 1, p),
                head_pair(packed[places[g][0], p * lanes : (p + 1) * lanes] * factor),
                1,
                1,
            )
            for g, p in members
        ]
        weights = []
        for n, (g, p) in enumerate(members):
            shifted = scores[n] + shifts[n // pairs]
            expo = jnp.exp(shifted - jnp.max(shifted, axis=0, keepdims=True))
            total_row = jnp.sum(expo, axis=0, keepdims=True)
            weights.append((expo * (1.0 / total_row)).astype(BF))
            probs[g * pairs + p] = weights[n]
        for n, (g, p) in enumerate(members):
            mixed = dot(weights[n], pair_rows(*places[g], 2, p), 0, 0)
            att[places[g][0], p * lanes : (p + 1) * lanes] = jnp.where(
                low_out, mixed[0:SPAN], mixed[SPAN : 2 * SPAN]
            ).astype(BF)

    attend(0)
    gather_core(UP)
    attend(1)
    gather_forward(DOWN)
    gather_last(OUT)
    gather_done(OUT)

    mid = tok[...].astype(F32) + dot(att[...], wo[...], 1, 0) + out_shift
    middle[...] = mid
    xhat, inverse = norm_stats(mid)
    xhat2[...] = xhat
    inv2[...] = inverse
    second[...] = (xhat * gain2 + bias2).astype(BF)
    gather_last(UP)
    gather_core(DOWN)
    gather_done(UP)

    half_owners = shard_count // 2
    sub = half_owners * lanes

    def unit_starts(part, side):
        return [
            (side * half_owners + n) * up_here + part * lanes for n in range(half_owners)
        ]

    def up_tile(part, side):
        return jnp.concatenate(
            [wu[:, a : a + lanes] for a in unit_starts(part, side)], axis=1
        )

    def down_tile(part, side):
        return jnp.concatenate(
            [wd[a : a + lanes, :] for a in unit_starts(part, side)], axis=0
        )

    def columns_of(part, side):
        start = part * part_cols + side * sub
        return slice(start, start + sub)

    every = [(part, side) for part in range(parts) for side in range(2)]

    def gelu_parts(before):
        cdf = 0.5 + 0.5 * lax.erf(before * math.sqrt(0.5))
        density = jnp.exp(before * before * -0.5) * (1.0 / math.sqrt(2.0 * math.pi))
        return before * cdf, cdf + before * density

    def feed_up(part, side):
        cols = columns_of(part, side)
        before = dot(second[...], up_tile(part, side), 1, 0) + up_bias[0:1, cols]
        value, slope = gelu_parts(before)
        hidden[:, cols] = value.astype(BF)
        gbefore[:, cols] = slope.astype(BF)

    def back_down(part, side):
        cols = columns_of(part, side)
        grad = dot(cot[...], down_tile(part, side), 1, 1)
        gbefore[:, cols] = (grad * gbefore[:, cols].astype(F32)).astype(BF)

    feed_up(0, 0)
    feed_up(0, 1)
    feed_up(1, 0)
    gather_last(DOWN)
    feed_up(1, 1)
    cot_in.wait()
    gather_done(DOWN)

    def chunk(which):
        if which in (D0, D1):
            refs, n = (g_down, r1_down, r2_down, r3_down, r4_down, own_down), which - D0
        elif which in (U0, U1):
            refs, n = (g_up, r1_up, r2_up, r3_up, r4_up, own_up), which - U0
        elif which == GO:
            refs, n = (g_out, r1_out, r2_out, r3_out, r4_out, own_out), 0
        elif which == QA:
            refs, n = (g_two, r1_two, r2_two, r3_two, r4_two, own_two), 0
        else:
            refs, n = (g_one, r1_one, r2_one, r3_one, r4_one, own_one), which - Q2
        return tuple(ref.at[n] for ref in refs)

    here, x_blk, y_blk, d_blk = yx, flip(yx, 1), flip(yx, 2), flip(flip(yx, 1), 2)
    z_dev = (ms, flip(mq, 1))
    z_mid = (ms, seq_count - 1 - mq)

    def reduce_copies(which):
        g, r1, r2, r3, r4, own = chunk(which)
        half = g.shape[2] // 2
        base = which * REDUCE_STEPS
        plan = (
            (g.at[1 - core], r1, core_dev),
            (g.at[core, d_blk, pl.ds(0, half)], r2.at[0], x_dev),
            (g.at[core, d_blk, pl.ds(half, half)], r2.at[1], y_dev),
            (g.at[core, x_blk], r3.at[0], x_dev),
            (g.at[core, y_blk], r3.at[1], y_dev),
            (own, r4.at[0], z_dev),
            (own, r4.at[1], z_mid),
            (own, r4.at[0], z_dev),
        )
        copies = [
            pltpu.make_async_remote_copy(
                src_ref=src,
                dst_ref=dst,
                send_sem=red_s.at[base + step],
                recv_sem=red_r.at[base + step],
                device_id=dev,
                device_id_type=MESH,
            )
            for step, (src, dst, dev) in enumerate(plan)
        ]
        return copies

    r_copies = [reduce_copies(which) for which in range(CHUNKS)]
    edge = jnp.logical_or(mq == 0, mq == seq_count - 1)
    inner = jnp.logical_not(edge)

    def add_rows(target, *sources):
        count = target.shape[0]
        step = min(count, 32)

        def one(i, carry):
            at = rows_of(i, step)
            value = target[at, :]
            for source in sources:
                value = value + source[at, :]
            target[at, :] = value
            return carry

        lax.fori_loop(0, count // step, one, 0)

    def reduce_a(which):
        r_copies[which][0].start()

    def reduce_b(which):
        g, r1, r2, r3, r4, own = chunk(which)
        c = r_copies[which]
        c[0].wait_recv()
        add_rows(g.at[core, d_blk], r1.at[d_blk])
        c[1].start()
        c[2].start()
        for blk in (x_blk, y_blk, here):
            add_rows(g.at[core, blk], r1.at[blk])

    def reduce_c(which):
        g, r1, r2, r3, r4, own = chunk(which)
        half = g.shape[2] // 2
        c = r_copies[which]
        c[1].wait_recv()
        add_rows(g.at[core, y_blk, pl.ds(0, half)], r2.at[0])
        c[4].start()
        c[2].wait_recv()
        add_rows(g.at[core, x_blk, pl.ds(half, half)], r2.at[1])
        c[3].start()

    def reduce_d(which):
        g, r1, r2, r3, r4, own = chunk(which)
        c = r_copies[which]
        c[3].wait_recv()
        c[4].wait_recv()
        count = own.shape[0]

        def one(i, carry):
            at = rows_of(i, 32)
            value = (
                g[core, here, at, :].astype(F32)
                + r3[0, at, :].astype(F32)
                + r3[1, at, :].astype(F32)
            )
            own[at, :] = value.astype(BF)
            return carry

        lax.fori_loop(0, count // 32, one, 0)

        @pl.when(edge)
        def _():
            c[5].start()

    def reduce_e(which):
        g, r1, r2, r3, r4, own = chunk(which)
        c = r_copies[which]

        @pl.when(inner)
        def _():
            c[5].wait_recv()
            add_rows(own, r4.at[0])
            c[6].start()

    def emit(which, source):
        target = {
            D0: gd_hbm.at[pl.ds(0, lanes)],
            D1: gd_hbm.at[pl.ds(lanes, lanes)],
            U0: gu_hbm.at[0],
            U1: gu_hbm.at[1],
            GO: go_hbm,
            QA: gt_hbm,
            Q2: gs_hbm.at[0],
            Q3: gs_hbm.at[1],
        }[which]
        return pltpu.make_async_copy(source, target, out_sem.at[which])

    def reduce_f(which):
        g, r1, r2, r3, r4, own = chunk(which)
        c = r_copies[which]

        @pl.when(inner)
        def _():
            c[6].wait_recv()
            c[6].wait_send()
            add_rows(own, r4.at[1])
            c[7].start()
            emit(which, own).start()

    def reduce_g(which):
        g, r1, r2, r3, r4, own = chunk(which)
        c = r_copies[which]

        @pl.when(edge)
        def _():
            c[5].wait_send()
            c[7].wait_recv()
            emit(which, r4.at[0]).start()

        @pl.when(inner)
        def _():
            c[7].wait_send()

        for step in range(5):
            c[step].wait_send()
        emit(which, own).wait()

    def put_rows(target, piece):
        count = piece.shape[0] // shard_count
        for owner in range(shard_count):
            target[owner % 2, owner // 2] = piece[owner * count : (owner + 1) * count]

    def part_of(part):
        return slice(part * part_cols, (part + 1) * part_cols)

    def down_grad(part):
        put_rows(g_down.at[part], dot(hidden[:, part_of(part)], cot[...], 0, 0).astype(BF))

    def up_grad(part):
        cols = part_of(part)
        put_rows(g_up.at[part], dot(second[...], gbefore[:, cols], 0, 0).astype(BF))
        upsum[0:1, cols] = jnp.sum(gbefore[:, cols].astype(F32), axis=0, keepdims=True)

    back_down(0, 0)
    back_down(0, 1)
    down_grad(0)
    reduce_a(D0)
    up_grad(0)
    reduce_a(U0)
    back_down(1, 0)
    back_down(1, 1)
    reduce_b(D0)
    down_grad(1)
    reduce_a(D1)
    reduce_b(U0)
    up_grad(1)
    reduce_a(U1)
    reduce_c(D0)

    vsum[...] = jnp.zeros_like(vsum)
    up_perm = jnp.concatenate([up_tile(*t) for t in every], axis=1)

    def back_second(i):
        at = rows_of(i, big)
        grad = dot(gbefore[at, :], up_perm, 1, 1)
        xhat = xhat2[at, :]
        vsum[3:4, :] += jnp.sum(grad * xhat, axis=0, keepdims=True)
        vsum[4:5, :] += jnp.sum(grad, axis=0, keepdims=True)
        incoming = cot[at, :].astype(F32)
        vsum[5:6, :] += jnp.sum(incoming, axis=0, keepdims=True)
        grad_mid = incoming + norm_back(grad, xhat, inv2[at, :], gain2)
        gmid[at, :] = grad_mid
        branch = grad_mid.astype(BF)
        gbranch[at, :] = branch
        vsum[2:3, :] += jnp.sum(branch.astype(F32), axis=0, keepdims=True)
        gatt[at, :] = dot(branch, wo[...], 1, 1).astype(BF)

    back_second(0)
    reduce_b(D1)
    reduce_c(U0)
    reduce_b(U1)
    back_second(1)
    reduce_d(D0)
    reduce_c(D1)
    put_rows(g_out.at[0], dot(att[...], gbranch[...], 0, 0).astype(BF))
    reduce_a(GO)

    low_keys = lax.broadcasted_iota(jnp.int32, (SPAN, lanes), 1) < HD

    def attend_back(p):
        lo = p * lanes
        places = [(rows_of(g, SPAN), rows_of(g // spans_here, spans_all)) for g in range(groups)]
        members = []
        for g in range(groups):
            at, mean_at = places[g]
            go = head_pair(gatt[at, lo : lo + lanes])
            weights = probs[g * pairs + p]
            gw = dot(pair_rows(at, mean_at, 2, p), go, 1, 1)
            gv = dot(weights, go, 1, 0)
            members.append((weights, gw, gv))
        scores = []
        for weights, gw, gv in members:
            prob = weights.astype(F32)
            row_inner = jnp.sum(prob * gw, axis=0, keepdims=True)
            scores.append((prob * (gw - row_inner)).astype(BF))
        far_k, far_v = None, None
        for g in range(groups):
            at, mean_at = places[g]
            gv = members[g][2]
            q = head_pair(packed[at, lo : lo + lanes])
            gq = dot(scores[g], pair_rows(at, mean_at, 1, p), 0, 0)
            gk = dot(scores[g], q, 1, 0) * factor
            gbefore[at, lo : lo + lanes] = (
                jnp.where(low_keys, gq[0:SPAN], gq[SPAN : 2 * SPAN]) * factor
            ).astype(BF)
            gbefore[at, width + lo : width + lo + lanes] = gk[0:SPAN].astype(BF)
            gbefore[at, 2 * width + lo : 2 * width + lo + lanes] = gv[0:SPAN].astype(BF)
            first = g % spans_here == 0
            far_k = gk[SPAN:] if first else far_k + gk[SPAN:]
            far_v = gv[SPAN:] if first else far_v + gv[SPAN:]
            if g % spans_here == spans_here - 1:
                gkv[mean_at, lo : lo + lanes] = far_k.astype(BF)
                gkv[mean_at, width + lo : width + lo + lanes] = far_v.astype(BF)

    def first_grad(lo, count, target):
        grads = [gbefore[:, m * width + lo : m * width + lo + count] for m in range(3)]
        means = [gkv[:, m * width + lo : m * width + lo + count] for m in range(2)]
        local_part = dot(normed[...], jnp.concatenate(grads, axis=1), 0, 0)
        mean_part = dot(nbar[...], jnp.concatenate(means, axis=1), 0, 0)
        piece = jnp.concatenate(
            [local_part[:, 0:count], local_part[:, count:] + mean_part], axis=1
        )
        put_rows(target, piece.astype(BF))

    attend_back(0)
    attend_back(1)
    reduce_b(GO)
    reduce_d(U0)
    reduce_c(U1)
    first_grad(0, 2 * lanes, g_two.at[0])
    reduce_a(QA)
    reduce_e(D0)
    attend_back(2)
    reduce_d(D1)
    reduce_c(GO)
    first_grad(2 * lanes, lanes, g_one.at[0])
    reduce_a(Q2)
    reduce_b(QA)
    reduce_e(U0)
    attend_back(3)

    gmean = dot(gkv[...], wq[:, width : 3 * width], 1, 1).astype(BF)
    gmean = dot(order[...], gmean, 0, 0).reshape(total, groups, width)
    gn_send[...] = jnp.concatenate(
        [gmean[:, :, :half_width], gmean[:, :, half_width:]], axis=1
    ).astype(BF)

    def gs_copy(source, target):
        return remote(
            gn_send.at[rows_of(target, seq_count)],
            gn_recv.at[source],
            gs_s.at[target],
            gs_r.at[source],
            (target, mq),
        )

    for target in range(shard_count - 1):

        @pl.when(target < ms)
        def _(target=target):
            gs_copy(ms, target).start()

    first_grad(3 * lanes, lanes, g_one.at[1])
    reduce_a(Q3)
    reduce_b(Q2)
    reduce_c(QA)
    reduce_d(GO)
    reduce_d(U1)
    reduce_e(D1)
    reduce_f(D0)
    reduce_b(Q3)
    reduce_f(U0)

    down_perm = jnp.concatenate([down_tile(*t) for t in every], axis=0)

    def out_block(i):
        at = rows_of(i, big)
        gbranch[at, :] = (
            middle[at, :] + dot(hidden[at, :], down_perm, 1, 0) + down_shift
        ).astype(BF)

    out_block(0)
    reduce_c(Q2)
    reduce_e(GO)
    out_block(1)
    bout_out = pltpu.make_async_copy(gbranch, block_out_hbm, io_sem.at[2])
    bout_out.start()
    gz_send[...] = gn_send[rows_of(ms, seq_count)]
    for source in range(1, shard_count):

        @pl.when(source > ms)
        def _(source=source):
            gs_copy(source, source).wait_recv()
            gz_send[...] += gn_recv[source]

    gz_copies = [
        remote(gz_send.at[peer[1]], gz_recv.at[mq], gz_s.at[step], gz_r.at[step], peer)
        for step, peer in enumerate(seq_peers)
    ]
    for c in gz_copies:
        c.start()
    gz_recv[mq] = gz_send[mq]
    reduce_d(QA)
    reduce_f(D1)
    reduce_c(Q3)
    reduce_e(U1)
    reduce_d(Q2)
    reduce_f(GO)
    for c in gz_copies:
        c.wait_recv()
    gnbar[...] = jnp.sum(gz_recv[...].astype(F32), axis=0)

    def back_first(i):
        at = rows_of(i, big)
        shares = []
        for u in range(big // SPAN):
            g = i * (big // SPAN) + u
            share = jnp.concatenate(
                [gnbar[g : g + 1, :], gnbar[groups + g : groups + g + 1, :]], axis=1
            ) * (1.0 / SPAN)
            shares.append(jnp.broadcast_to(share, (SPAN, width)))
        grad = dot(gbefore[at, 0 : 3 * width], wq[...], 1, 1) + jnp.concatenate(
            shares, axis=0
        )
        xhat = xhat1[at, :]
        vsum[0:1, :] += jnp.sum(grad * xhat, axis=0, keepdims=True)
        vsum[1:2, :] += jnp.sum(grad, axis=0, keepdims=True)
        gmid[at, :] = gmid[at, :] + norm_back(grad, xhat, inv1[at, :], gain1)

    back_first(0)
    reduce_d(Q3)
    reduce_e(QA)
    back_first(1)
    tok_out = pltpu.make_async_copy(gmid, grad_tok_hbm, io_sem.at[3])
    tok_out.start()
    reduce_e(Q2)
    reduce_f(U1)

    for owner in range(shard_count):
        at = owner // 2
        piece = vsum[:, at * lanes : (at + 1) * lanes]
        if owner % 2 == 1:
            piece = pltpu.roll(piece, HD, axis=1)
        vec_send[owner, 0:8, :] = piece
        vec_send[owner, 8:16, :] = jnp.zeros((8, lanes), F32)
        for r in range(parts):
            start = r * part_cols + owner * lanes
            vec_send[owner, 8 + r : 9 + r, :] = upsum[0:1, start : start + lanes]
    vo_copies = [
        remote(vec_send.at[peer[0]], vec_recv.at[ms], vo_s.at[step], vo_r.at[step], peer)
        for step, peer in enumerate(shard_peers)
    ]
    for c in vo_copies:
        c.start()
    vec_recv[ms] = vec_send[ms]
    for which in (D0, U0, D1, GO):
        reduce_g(which)
    reduce_e(Q3)
    reduce_f(QA)
    reduce_f(Q2)
    for c in vo_copies:
        c.wait_recv()
    vec_line[mq] = jnp.sum(vec_recv[...], axis=0)
    vz_copies = [
        remote(vec_line.at[mq], vec_line.at[mq], vz_s.at[step], vz_r.at[step], peer)
        for step, peer in enumerate(seq_peers)
    ]
    for c in vz_copies:
        c.start()
    reduce_f(Q3)
    reduce_g(U1)
    reduce_g(QA)
    for c in vz_copies:
        c.wait_recv()
    vec_out_ref[...] = jnp.sum(vec_line[...], axis=0)
    reduce_g(Q2)
    reduce_g(Q3)

    for target in range(1, shard_count):

        @pl.when(target > ms)
        def _(target=target):
            xs_copy(ms, target).wait_send()

    for target in range(shard_count - 1):

        @pl.when(target < ms)
        def _(target=target):
            gs_copy(ms, target).wait_send()

    for c in vec_copies + xz_copies + gz_copies + vo_copies + vz_copies:
        c.wait_send()
    for which in range(4):
        for c in w_copies[which]:
            c.wait_send()
    bout_out.wait()
    tok_out.wait()


def finish_kernel(*refs):
    raw, vec, outs, vec_outs = refs[0:7], refs[7], refs[8:14], refs[14:21]
    low_refs, high_refs, in_sem, out_sem = refs[21:28], refs[28:32], refs[32], refs[33]
    order = (5, 6, 4, 0, 1, 2, 3)
    loads = [pltpu.make_async_copy(raw[n], low_refs[n], in_sem.at[n]) for n in range(7)]
    for n in order:
        loads[n].start()
    for n, ref in enumerate(vec_outs[0:6]):
        ref[...] = vec[n : n + 1, 0 : ref.shape[1]]
    vec_outs[6][...] = vec[8 : 8 + vec_outs[6].shape[0], :]
    stores = []
    lanes = 2 * HD

    def store(ready, at):
        stores.append(pltpu.make_async_copy(ready, outs[at], out_sem.at[at]))
        stores[-1].start()

    for n in order:
        loads[n].wait()
        low = low_refs[n]
        if n < 2:
            store(low, n)
        elif n == 2:
            for part in range(3):
                start = part * 4 * lanes
                high_refs[0][:, start : start + 2 * lanes] = low[
                    :, part * 2 * lanes : (part + 1) * 2 * lanes
                ].astype(F32)
        elif n == 3:
            for part in range(3):
                for one in range(2):
                    start = (part * 4 + 2 + one) * lanes
                    high_refs[0][:, start : start + lanes] = low[
                        one, :, part * lanes : (part + 1) * lanes
                    ].astype(F32)
            store(high_refs[0], 2)
        elif n == 5:
            high = high_refs[2]
            part_count, _, columns = low.shape
            for part in range(part_count):
                for owner in range(columns // lanes):
                    start = (owner * part_count + part) * lanes
                    high[:, start : start + lanes] = low[
                        part, :, owner * lanes : (owner + 1) * lanes
                    ].astype(F32)
            store(high, 4)
        else:
            high = high_refs[n - 3]
            high[...] = low[...].astype(F32)
            store(high, n - 1)
    for c in stores:
        c.wait()


def local_block(
    tokens,
    ln1_gain,
    ln1_bias,
    qkv_weight,
    out_weight,
    out_bias,
    ln2_gain,
    ln2_bias,
    up_weight,
    up_bias,
    down_weight,
    down_bias,
    cotangent,
):
    seq_count = lax.axis_size("seq")
    shard_count = lax.axis_size("shard")
    total = seq_count * shard_count
    batch, local_len, width = tokens.shape
    rows = batch * local_len
    groups = rows // SPAN
    spans_all = local_len // SPAN * total
    keys = SPAN + spans_all
    ff = up_weight.shape[1]
    lanes = 2 * HD
    shard_rows = width // shard_count
    down_rows = ff // shard_count
    vmem = pl.BlockSpec(memory_space=pltpu.VMEM)
    hbm = pl.BlockSpec(memory_space=pl.ANY)
    dma = pltpu.SemaphoreType.DMA
    half_yx = shard_count // 2

    def grads(count, columns, lead=()):
        half = count // 2
        return (
            pltpu.VMEM(lead + (2, half_yx, count, columns), BF),
            pltpu.VMEM(lead + (half_yx, count, columns), BF),
            pltpu.VMEM(lead + (2, half, columns), BF),
            pltpu.VMEM(lead + (2, count, columns), BF),
            pltpu.VMEM(lead + (2, count, columns), BF),
            pltpu.VMEM(lead + (count, columns), BF),
        )

    parts = down_rows // lanes
    part_cols = ff // parts
    down_bufs = grads(lanes, width, (parts,))
    up_bufs = grads(shard_rows, part_cols, (parts,))
    out_bufs = grads(shard_rows, width, (1,))
    two_bufs = grads(shard_rows, 6 * lanes, (1,))
    one_bufs = grads(shard_rows, 3 * lanes, (2,))
    grad_bufs = [
        buf
        for five in zip(down_bufs, up_bufs, out_bufs, two_bufs, one_bufs)
        for buf in five
    ]
    scratch = [
        pltpu.VMEM((rows, width), BF),
        pltpu.VMEM((rows, width), BF),
        pltpu.VMEM((width, 3 * width), BF),
        pltpu.VMEM((width, width), BF),
        pltpu.VMEM((width, ff), BF),
        pltpu.VMEM((ff, width), BF),
        pltpu.VMEM((16, lanes), F32),
        pltpu.VMEM((shard_count, 16, lanes), F32),
        pltpu.VMEM((rows, width), F32),
        pltpu.VMEM((rows, 1), F32),
        pltpu.VMEM((groups, width), F32),
        pltpu.VMEM((total, 2 * groups, width // 2), BF),
        pltpu.VMEM((batch * spans_all, batch * spans_all), BF),
        pltpu.VMEM((8, width), F32),
        pltpu.VMEM((8, ff), F32),
        pltpu.VMEM((rows, width), BF),
        pltpu.VMEM((rows, 3 * width), BF),
        pltpu.VMEM((batch * spans_all, width), BF),
        pltpu.VMEM((batch * spans_all, 2 * width), BF),
        pltpu.VMEM((groups * H // 2, keys, 2 * SPAN), BF),
        pltpu.VMEM((rows, width), BF),
        pltpu.VMEM((rows, width), F32),
        pltpu.VMEM((rows, width), F32),
        pltpu.VMEM((rows, 1), F32),
        pltpu.VMEM((rows, width), BF),
        pltpu.VMEM((rows, width), F32),
        pltpu.VMEM((rows, ff), BF),
        pltpu.VMEM((rows, ff), BF),
        pltpu.VMEM((rows, width), BF),
        pltpu.VMEM((rows, width), BF),
        pltpu.VMEM((batch * spans_all, 2 * width), BF),
        pltpu.VMEM((total, 2 * groups, width // 2), BF),
        pltpu.VMEM((shard_count, seq_count, 2 * groups, width // 2), BF),
        pltpu.VMEM((seq_count, 2 * groups, width // 2), BF),
        pltpu.VMEM((seq_count, 2 * groups, width // 2), BF),
        pltpu.VMEM((2 * groups, width // 2), F32),
        pltpu.VMEM((8, width), F32),
        pltpu.VMEM((8, ff), F32),
        pltpu.VMEM((shard_count, 16, lanes), F32),
        pltpu.VMEM((shard_count, 16, lanes), F32),
        pltpu.VMEM((seq_count, 16, lanes), F32),
        *grad_bufs,
        dma((4 * GATHER_STEPS,)),
        dma((4 * GATHER_STEPS,)),
        dma((4,)),
        dma((4,)),
        dma((shard_count,)),
        dma((shard_count,)),
        dma((seq_count,)),
        dma((seq_count,)),
        dma((shard_count,)),
        dma((shard_count,)),
        dma((shard_count,)),
        dma((shard_count,)),
        dma((seq_count,)),
        dma((seq_count,)),
        dma((shard_count,)),
        dma((shard_count,)),
        dma((seq_count,)),
        dma((seq_count,)),
        dma((CHUNKS * REDUCE_STEPS,)),
        dma((CHUNKS * REDUCE_STEPS,)),
        dma((CHUNKS,)),
    ]
    vectors = [
        v.reshape(1, shard_rows)
        for v in (ln1_gain, ln1_bias, out_bias, ln2_gain, ln2_bias, down_bias)
    ]
    raw = pl.pallas_call(
        functools.partial(block_kernel, batch, shard_count, seq_count),
        out_shape=(
            jax.ShapeDtypeStruct((rows, width), BF),
            jax.ShapeDtypeStruct((rows, width), F32),
            jax.ShapeDtypeStruct((shard_rows, 6 * lanes), BF),
            jax.ShapeDtypeStruct((2, shard_rows, 3 * lanes), BF),
            jax.ShapeDtypeStruct((shard_rows, width), BF),
            jax.ShapeDtypeStruct((parts, shard_rows, part_cols), BF),
            jax.ShapeDtypeStruct((down_rows, width), BF),
            jax.ShapeDtypeStruct((16, lanes), F32),
        ),
        in_specs=[hbm, hbm, [vmem] * 6, vmem, hbm, hbm, hbm, hbm],
        out_specs=(hbm,) * 7 + (vmem,),
        scratch_shapes=scratch,
        compiler_params=pltpu.CompilerParams(
            collective_id=0, has_side_effects=True, vmem_limit_bytes=63 * 2**20
        ),
        name="block",
    )(
        tokens.reshape(rows, width),
        cotangent.reshape(rows, width),
        vectors,
        up_bias.reshape(-1, lanes),
        qkv_weight,
        out_weight,
        up_weight,
        down_weight,
    )
    low_shapes = [
        (shard_rows, 6 * lanes),
        (2, shard_rows, 3 * lanes),
        (shard_rows, width),
        (parts, shard_rows, part_cols),
        (down_rows, width),
    ]
    high_shapes = [
        (shard_rows, 3 * width),
        (shard_rows, width),
        (shard_rows, ff),
        (down_rows, width),
    ]
    done = pl.pallas_call(
        finish_kernel,
        out_shape=(
            jax.ShapeDtypeStruct((rows, width), BF),
            jax.ShapeDtypeStruct((rows, width), F32),
            *(jax.ShapeDtypeStruct(shape, F32) for shape in high_shapes),
            *(jax.ShapeDtypeStruct((1, shard_rows), F32) for _ in range(6)),
            jax.ShapeDtypeStruct((down_rows // lanes, lanes), F32),
        ),
        in_specs=[hbm] * 7 + [vmem],
        out_specs=(hbm,) * 6 + (vmem,) * 7,
        scratch_shapes=[
            pltpu.VMEM((rows, width), BF),
            pltpu.VMEM((rows, width), F32),
            *(pltpu.VMEM(shape, BF) for shape in low_shapes),
            *(pltpu.VMEM(shape, F32) for shape in high_shapes),
            dma((7,)),
            dma((6,)),
        ],
        compiler_params=pltpu.CompilerParams(vmem_limit_bytes=62 * 2**20),
        name="finish",
    )(*raw)
    block_out, grad_tokens, g_qkv, g_out, g_up, g_down = done[0:6]
    vec_grads = [v.reshape(shard_rows) for v in done[6:12]]
    return (
        block_out.reshape(tokens.shape),
        grad_tokens.reshape(tokens.shape),
        vec_grads[0],
        vec_grads[1],
        g_qkv,
        g_out,
        vec_grads[2],
        vec_grads[3],
        vec_grads[4],
        g_up,
        done[12].reshape(down_rows),
        g_down,
        vec_grads[5],
    )


def layer_norm(values, norm_gain, norm_shift):
    center = values - jnp.mean(values, axis=-1, keepdims=True)
    spread = jnp.mean(center * center, axis=-1, keepdims=True)
    return center * lax.rsqrt(spread + epsilon) * norm_gain + norm_shift


def gelu_exact(values):
    return jax.nn.gelu(values, approximate=False)


def contract_rows(left_matrix, right_matrix):
    return lax.dot_general(
        left_matrix, right_matrix, (((0,), (0,)), ((), ())), preferred_element_type=jnp.float32
    )


def times_transpose(left_matrix, right_matrix):
    return lax.dot_general(
        left_matrix, right_matrix, (((1,), (1,)), ((), ())), preferred_element_type=jnp.float32
    )


def joint_scores(query_rows, key_rows, key_all, causal, earlier):
    factor = HD ** (-0.5)
    local_part = factor * jnp.einsum(
        "bjihd,bjkhd->bjhik", query_rows, key_rows, preferred_element_type=jnp.float32
    )
    summary = factor * jnp.einsum(
        "bjihd,bfhd->bjhif", query_rows, key_all, preferred_element_type=jnp.float32
    ) + math.log(SPAN)
    local_part = jnp.where(causal[None, None, None], local_part, -jnp.inf)
    summary = jnp.where(earlier[None, :, None, None, :], summary, -jnp.inf)
    return (local_part, summary)


def attend(query_rows, key_rows, value_rows, key_all, value_all, causal, earlier):
    local_part, summary = joint_scores(query_rows, key_rows, key_all, causal, earlier)
    row_max = jnp.maximum(jnp.max(local_part, axis=-1), jnp.max(summary, axis=-1))
    local_exp = jnp.exp(local_part - row_max[..., None])
    summary_exp = jnp.exp(summary - row_max[..., None])
    row_total = jnp.sum(local_exp, axis=-1) + jnp.sum(summary_exp, axis=-1)
    log_total = row_max + jnp.log(row_total)
    local_weights = (local_exp / row_total[..., None]).astype(jnp.bfloat16)
    summary_weights = (summary_exp / row_total[..., None]).astype(jnp.bfloat16)
    mixed_heads = jnp.einsum(
        "bjhik,bjkhd->bjihd", local_weights, value_rows, preferred_element_type=jnp.float32
    )
    mixed_heads = mixed_heads + jnp.einsum(
        "bjhif,bfhd->bjihd", summary_weights, value_all, preferred_element_type=jnp.float32
    )
    return (mixed_heads, log_total, local_weights, summary_weights)


def attend_back(
    grad_mixed,
    query_rows,
    key_rows,
    value_rows,
    key_all,
    value_all,
    causal,
    earlier,
    log_total,
    local_weights,
    summary_weights,
):
    factor = HD ** (-0.5)
    local_part, summary = joint_scores(query_rows, key_rows, key_all, causal, earlier)
    local_prob = jnp.exp(local_part - log_total[..., None])
    summary_prob = jnp.exp(summary - log_total[..., None])
    grad_local_w = jnp.einsum(
        "bjihd,bjkhd->bjhik", grad_mixed, value_rows, preferred_element_type=jnp.float32
    )
    grad_summary_w = jnp.einsum(
        "bjihd,bfhd->bjhif", grad_mixed, value_all, preferred_element_type=jnp.float32
    )
    row_inner = jnp.sum(local_prob * grad_local_w, axis=-1) + jnp.sum(
        summary_prob * grad_summary_w, axis=-1
    )
    grad_local = (local_prob * (grad_local_w - row_inner[..., None])).astype(jnp.bfloat16)
    grad_summary = (summary_prob * (grad_summary_w - row_inner[..., None])).astype(jnp.bfloat16)
    grad_query = jnp.einsum(
        "bjhik,bjkhd->bjihd", grad_local, key_rows, preferred_element_type=jnp.float32
    )
    grad_query = factor * (
        grad_query
        + jnp.einsum("bjhif,bfhd->bjihd", grad_summary, key_all, preferred_element_type=jnp.float32)
    )
    grad_key = factor * jnp.einsum(
        "bjhik,bjihd->bjkhd", grad_local, query_rows, preferred_element_type=jnp.float32
    )
    grad_key_all = factor * jnp.einsum(
        "bjhif,bjihd->bfhd", grad_summary, query_rows, preferred_element_type=jnp.float32
    )
    grad_value = jnp.einsum(
        "bjhik,bjihd->bjkhd", local_weights, grad_mixed, preferred_element_type=jnp.float32
    )
    grad_value_all = jnp.einsum(
        "bjhif,bjihd->bfhd", summary_weights, grad_mixed, preferred_element_type=jnp.float32
    )
    return (grad_query, grad_key, grad_value, grad_key_all, grad_value_all)


def local_general(
    tokens,
    ln1_gain,
    ln1_bias,
    qkv_weight,
    out_weight,
    out_bias,
    ln2_gain,
    ln2_bias,
    up_weight,
    up_bias,
    down_weight,
    down_bias,
    cotangent,
):
    seq_count = lax.axis_size("seq")
    shard_count = lax.axis_size("shard")
    shard_place = lax.axis_index("shard")
    batch_size, local_len, model_width = tokens.shape
    heads_here = H // seq_count
    head_width = heads_here * HD
    group_len = local_len * seq_count
    spans_here = group_len // SPAN
    spans_all = spans_here * shard_count
    row_count = batch_size * local_len
    shards = (
        ln1_gain,
        ln1_bias,
        qkv_weight,
        out_weight,
        out_bias,
        ln2_gain,
        ln2_bias,
        up_weight,
        up_bias,
        down_weight,
        down_bias,
    )
    gathered = (
        lax.all_gather(shards[0], "shard", axis=0, tiled=True),
        lax.all_gather(shards[1], "shard", axis=0, tiled=True),
        lax.all_gather(shards[2], "shard", axis=0, tiled=True),
        lax.all_gather(shards[3], "shard", axis=0, tiled=True),
        lax.all_gather(shards[4], "shard", axis=0, tiled=True),
        lax.all_gather(shards[5], "shard", axis=0, tiled=True),
        lax.all_gather(shards[6], "shard", axis=0, tiled=True),
        lax.all_gather(shards[7], "shard", axis=0, tiled=True),
        lax.all_gather(shards[8], "shard", axis=0, tiled=True),
        lax.all_gather(shards[9], "shard", axis=0, tiled=True),
        lax.all_gather(shards[10], "shard", axis=0, tiled=True),
    )
    (
        gain_one,
        bias_one,
        qkv_full,
        out_full,
        out_shift,
        gain_two,
        bias_two,
        up_full,
        up_shift,
        down_full,
        down_shift,
    ) = gathered
    flat_tokens = tokens.reshape(row_count, model_width).astype(jnp.float32)
    normed = layer_norm(
        flat_tokens, gain_one.astype(jnp.float32), bias_one.astype(jnp.float32)
    ).astype(jnp.bfloat16)
    packed = jnp.dot(normed, qkv_full, preferred_element_type=jnp.float32).astype(jnp.bfloat16)
    span_place = jnp.arange(SPAN)
    packed_heads = packed.reshape(batch_size, local_len, 3, seq_count, head_width)
    headed = lax.all_to_all(packed_heads, "seq", split_axis=3, concat_axis=1, tiled=True)
    headed = headed.reshape(batch_size, spans_here, SPAN, 3, heads_here, HD)
    query_rows = headed[:, :, :, 0]
    key_rows = headed[:, :, :, 1]
    value_rows = headed[:, :, :, 2]
    key_means = jnp.mean(key_rows, axis=2, dtype=jnp.float32).astype(jnp.bfloat16)
    value_means = jnp.mean(value_rows, axis=2, dtype=jnp.float32).astype(jnp.bfloat16)
    key_all, value_all = (
        lax.all_gather(key_means, "shard", axis=1, tiled=True),
        lax.all_gather(value_means, "shard", axis=1, tiled=True),
    )
    causal = span_place[:, None] >= span_place[None, :]
    global_span = shard_place * spans_here + jnp.arange(spans_here)
    earlier = global_span[:, None] > jnp.arange(spans_all)[None, :]
    mixed_heads, log_total, local_weights, summary_weights = attend(
        query_rows, key_rows, value_rows, key_all, value_all, causal, earlier
    )
    attended = mixed_heads.astype(jnp.bfloat16).reshape(batch_size, group_len, head_width)
    attended = lax.all_to_all(attended, "seq", split_axis=1, concat_axis=2, tiled=True)
    attended_rows = attended.reshape(row_count, model_width)
    middle = (
        flat_tokens
        + jnp.dot(attended_rows, out_full, preferred_element_type=jnp.float32)
        + out_shift.astype(jnp.float32)
    )
    second = layer_norm(middle, gain_two.astype(jnp.float32), bias_two.astype(jnp.float32)).astype(
        jnp.bfloat16
    )
    before = jnp.dot(second, up_full, preferred_element_type=jnp.float32) + up_shift.astype(
        jnp.float32
    )
    hidden = gelu_exact(before).astype(jnp.bfloat16)
    block_out = (
        middle
        + jnp.dot(hidden, down_full, preferred_element_type=jnp.float32)
        + down_shift.astype(jnp.float32)
    )
    block_out = block_out.astype(jnp.bfloat16).reshape(batch_size, local_len, model_width)
    incoming = cotangent.reshape(row_count, model_width)
    grad_down = contract_rows(hidden, incoming)
    grad_down_shift = jnp.sum(incoming, axis=0, dtype=jnp.float32)
    grad_hidden = times_transpose(incoming, down_full)
    gelu_value, gelu_pull = jax.vjp(gelu_exact, before)
    grad_before = gelu_pull(grad_hidden)[0].astype(jnp.bfloat16)
    grad_up = contract_rows(second, grad_before)
    grad_up_shift = jnp.sum(grad_before, axis=0, dtype=jnp.float32)
    grad_second = times_transpose(grad_before, up_full)
    norm_value, norm_pull = jax.vjp(
        layer_norm, middle, gain_two.astype(jnp.float32), bias_two.astype(jnp.float32)
    )
    grad_middle_norm, grad_gain_two, grad_bias_two = norm_pull(grad_second)
    grad_middle = incoming.astype(jnp.float32) + grad_middle_norm
    grad_branch = grad_middle.astype(jnp.bfloat16)
    grad_out = contract_rows(attended_rows, grad_branch)
    grad_out_shift = jnp.sum(grad_branch, axis=0, dtype=jnp.float32)
    grad_attended = times_transpose(grad_branch, out_full).astype(jnp.bfloat16)
    grad_attended = grad_attended.reshape(batch_size, local_len, seq_count, head_width)
    grad_headed = lax.all_to_all(grad_attended, "seq", split_axis=2, concat_axis=1, tiled=True)
    grad_mixed = grad_headed.reshape(batch_size, spans_here, SPAN, heads_here, HD)
    grad_query, grad_key, grad_value, grad_key_all, grad_value_all = attend_back(
        grad_mixed,
        query_rows,
        key_rows,
        value_rows,
        key_all,
        value_all,
        causal,
        earlier,
        log_total,
        local_weights,
        summary_weights,
    )
    grad_key_means, grad_value_means = (
        lax.psum_scatter(
            grad_key_all.astype(jnp.bfloat16), "shard", scatter_dimension=1, tiled=True
        ).astype(jnp.float32),
        lax.psum_scatter(
            grad_value_all.astype(jnp.bfloat16), "shard", scatter_dimension=1, tiled=True
        ).astype(jnp.float32),
    )
    grad_key = grad_key + grad_key_means[:, :, None] / SPAN
    grad_value = grad_value + grad_value_means[:, :, None] / SPAN
    grad_packed = jnp.stack([grad_query, grad_key, grad_value], axis=3).astype(jnp.bfloat16)
    grad_packed = grad_packed.reshape(batch_size, group_len, 3, 1, head_width)
    grad_packed = lax.all_to_all(grad_packed, "seq", split_axis=1, concat_axis=3, tiled=True)
    grad_packed = grad_packed.reshape(row_count, 3 * model_width)
    grad_qkv = contract_rows(normed, grad_packed)
    grad_normed = times_transpose(grad_packed, qkv_full)
    first_value, first_pull = jax.vjp(
        layer_norm, flat_tokens, gain_one.astype(jnp.float32), bias_one.astype(jnp.float32)
    )
    grad_flat_norm, grad_gain_one, grad_bias_one = first_pull(grad_normed)
    grad_tokens = (grad_middle + grad_flat_norm).reshape(batch_size, local_len, model_width)
    all_grads = (
        grad_gain_one,
        grad_bias_one,
        grad_qkv,
        grad_out,
        grad_out_shift,
        grad_gain_two,
        grad_bias_two,
        grad_up,
        grad_up_shift,
        grad_down,
        grad_down_shift,
    )
    owned_grads = (
        lax.psum_scatter(
            all_grads[0].astype(jnp.bfloat16), "shard", scatter_dimension=0, tiled=True
        ).astype(jnp.float32),
        lax.psum_scatter(
            all_grads[1].astype(jnp.bfloat16), "shard", scatter_dimension=0, tiled=True
        ).astype(jnp.float32),
        lax.psum_scatter(
            all_grads[2].astype(jnp.bfloat16), "shard", scatter_dimension=0, tiled=True
        ).astype(jnp.float32),
        lax.psum_scatter(
            all_grads[3].astype(jnp.bfloat16), "shard", scatter_dimension=0, tiled=True
        ).astype(jnp.float32),
        lax.psum_scatter(
            all_grads[4].astype(jnp.bfloat16), "shard", scatter_dimension=0, tiled=True
        ).astype(jnp.float32),
        lax.psum_scatter(
            all_grads[5].astype(jnp.bfloat16), "shard", scatter_dimension=0, tiled=True
        ).astype(jnp.float32),
        lax.psum_scatter(
            all_grads[6].astype(jnp.bfloat16), "shard", scatter_dimension=0, tiled=True
        ).astype(jnp.float32),
        lax.psum_scatter(
            all_grads[7].astype(jnp.bfloat16), "shard", scatter_dimension=0, tiled=True
        ).astype(jnp.float32),
        lax.psum_scatter(
            all_grads[8].astype(jnp.bfloat16), "shard", scatter_dimension=0, tiled=True
        ).astype(jnp.float32),
        lax.psum_scatter(
            all_grads[9].astype(jnp.bfloat16), "shard", scatter_dimension=0, tiled=True
        ).astype(jnp.float32),
        lax.psum_scatter(
            all_grads[10].astype(jnp.bfloat16), "shard", scatter_dimension=0, tiled=True
        ).astype(jnp.float32),
    )
    owned_grads = (
        lax.psum(owned_grads[0].astype(jnp.bfloat16), "seq").astype(jnp.float32),
        lax.psum(owned_grads[1].astype(jnp.bfloat16), "seq").astype(jnp.float32),
        lax.psum(owned_grads[2].astype(jnp.bfloat16), "seq").astype(jnp.float32),
        lax.psum(owned_grads[3].astype(jnp.bfloat16), "seq").astype(jnp.float32),
        lax.psum(owned_grads[4].astype(jnp.bfloat16), "seq").astype(jnp.float32),
        lax.psum(owned_grads[5].astype(jnp.bfloat16), "seq").astype(jnp.float32),
        lax.psum(owned_grads[6].astype(jnp.bfloat16), "seq").astype(jnp.float32),
        lax.psum(owned_grads[7].astype(jnp.bfloat16), "seq").astype(jnp.float32),
        lax.psum(owned_grads[8].astype(jnp.bfloat16), "seq").astype(jnp.float32),
        lax.psum(owned_grads[9].astype(jnp.bfloat16), "seq").astype(jnp.float32),
        lax.psum(owned_grads[10].astype(jnp.bfloat16), "seq").astype(jnp.float32),
    )
    return (
        block_out,
        grad_tokens,
        owned_grads[0],
        owned_grads[1],
        owned_grads[2],
        owned_grads[3],
        owned_grads[4],
        owned_grads[5],
        owned_grads[6],
        owned_grads[7],
        owned_grads[8],
        owned_grads[9],
        owned_grads[10],
    )


def local(tokens, *rest):
    whole_spans = tokens.shape[1] % SPAN == 0
    if whole_spans and lax.axis_size("shard") == 8 and lax.axis_size("seq") == 4:
        return local_block(tokens, *rest)
    return local_general(tokens, *rest)


def solution(mesh):
    return jax.shard_map(
        local,
        mesh=mesh,
        in_specs=(
            P(None, ("shard", "seq"), None),
            P("shard"),
            P("shard"),
            P("shard", None),
            P("shard", None),
            P("shard"),
            P("shard"),
            P("shard"),
            P("shard", None),
            P("shard"),
            P("shard", None),
            P("shard"),
            P(None, ("shard", "seq"), None),
        ),
        out_specs=(
            P(None, ("shard", "seq"), None),
            P(None, ("shard", "seq"), None),
            P("shard"),
            P("shard"),
            P("shard", None),
            P("shard", None),
            P("shard"),
            P("shard"),
            P("shard"),
            P("shard", None),
            P("shard"),
            P("shard", None),
            P("shard"),
        ),
        check_vma=False,
    )
```

```python
import functools
import math

import jax
import jax.numpy as jnp
from jax import lax
from jax.experimental import pallas as pl
from jax.experimental.pallas import tpu as pltpu
from jax.sharding import PartitionSpec as P

H = 8
HD = 64
SPAN = 128


epsilon = 1e-05
MESH = pl.DeviceIdType.MESH
BF = jnp.bfloat16
F32 = jnp.float32


def dot(left, right, left_dim, right_dim):
    return lax.dot_general(
        left, right, (((left_dim,), (right_dim,)), ((), ())), preferred_element_type=F32
    )


def rows_of(index, count):
    if isinstance(index, int):
        return pl.ds(index * count, count)
    return pl.ds(pl.multiple_of(index * count, count), count)


def norm_stats(values):
    center = values - jnp.mean(values, axis=-1, keepdims=True)
    inverse = lax.rsqrt(jnp.mean(center * center, axis=-1, keepdims=True) + epsilon)
    return center * inverse, inverse


def norm_back(grad, xhat, inverse, gain):
    scaled = grad * gain
    first = jnp.mean(scaled, axis=-1, keepdims=True)
    second = jnp.mean(scaled * xhat, axis=-1, keepdims=True)
    return inverse * (scaled - first - xhat * second)


QKV, OUT, UP, DOWN = range(4)
D0, D1, U0, U1, GO, QA, Q2, Q3 = range(8)
CHUNKS = 8
ALONG_SEQ = ()
GATHER_STEPS = 12
REDUCE_STEPS = 8


def block_kernel(
    batch,
    shard_count,
    seq_count,
    tok_hbm,
    cot_hbm,
    vec_refs,
    up_bias_ref,
    wq_hbm,
    wo_hbm,
    wu_hbm,
    wd_hbm,
    block_out_hbm,
    grad_tok_hbm,
    gt_hbm,
    gs_hbm,
    go_hbm,
    gu_hbm,
    gd_hbm,
    vec_out_ref,
    tok,
    cot,
    wq,
    wo,
    wu,
    wd,
    vec_own,
    vec_all,
    xhat1,
    inv1,
    xb_stage,
    xb_all,
    order,
    vfull,
    up_bias,
    normed,
    packed,
    nbar,
    kv_mean,
    probs,
    att,
    middle,
    gmid,
    inv2,
    second,
    xhat2,
    hidden,
    gbefore,
    gatt,
    gbranch,
    gkv,
    gn_send,
    gn_recv,
    gz_send,
    gz_recv,
    gnbar,
    vsum,
    upsum,
    vec_send,
    vec_recv,
    vec_line,
    g_down,
    g_up,
    g_out,
    g_two,
    g_one,
    r1_down,
    r1_up,
    r1_out,
    r1_two,
    r1_one,
    r2_down,
    r2_up,
    r2_out,
    r2_two,
    r2_one,
    r3_down,
    r3_up,
    r3_out,
    r3_two,
    r3_one,
    r4_down,
    r4_up,
    r4_out,
    r4_two,
    r4_one,
    own_down,
    own_up,
    own_out,
    own_two,
    own_one,
    w_send,
    w_recv,
    w_local,
    io_sem,
    vec_s,
    vec_r,
    xz_s,
    xz_r,
    xs_s,
    xs_r,
    gs_s,
    gs_r,
    gz_s,
    gz_r,
    vo_s,
    vo_r,
    vz_s,
    vz_r,
    red_s,
    red_r,
    out_sem,
):
    rows, width = tok.shape
    ff = up_bias.shape[1]
    total = shard_count * seq_count
    groups = rows // SPAN
    spans_here = groups // batch
    spans_all = spans_here * total
    pairs = H // 2
    lanes = 2 * HD
    ms = lax.axis_index("shard")
    mq = lax.axis_index("seq")
    mt = ms * seq_count + mq
    core = lax.rem(ms, 2)
    yx = ms // 2

    def flip(value, bit):
        return value + bit - 2 * bit * lax.rem(value // bit, 2)

    core_dev = (flip(ms, 1), mq)
    x_dev = (flip(ms, 2), mq)
    y_dev = (flip(ms, 4), mq)

    tok_in = pltpu.make_async_copy(tok_hbm, tok, io_sem.at[0])
    cot_in = pltpu.make_async_copy(cot_hbm, cot, io_sem.at[1])
    tok_in.start()
    cot_in.start()

    xb_all[...] = jnp.zeros_like(xb_all)
    barrier = pltpu.get_barrier_semaphore()

    shard_peers = [(lax.rem(ms + step, shard_count), mq) for step in range(1, shard_count)]
    seq_peers = [(ms, lax.rem(mq + step, seq_count)) for step in range(1, seq_count)]
    peers = shard_peers + seq_peers
    for peer in peers:
        pl.semaphore_signal(barrier, inc=1, device_id=peer, device_id_type=MESH)

    w_hbm = (wq_hbm, wo_hbm, wu_hbm, wd_hbm)
    w_full = (wq, wo, wu, wd)

    def gather_copies(which):
        full = w_full[which]
        depth = full.shape[0] // shard_count
        half = depth // 2
        base = which * GATHER_STEPS

        def block(owner):
            return full.at[rows_of(owner, depth)]

        def part(owner, side):
            return full.at[pl.ds(pl.multiple_of(owner * depth + side * half, half), half)]

        def own_part(side):
            return w_hbm[which].at[pl.ds(pl.multiple_of(side * half, half), half)]

        x_own, y_own, d_own = flip(ms, 2), flip(ms, 4), flip(flip(ms, 2), 4)
        if which in ALONG_SEQ:
            h = lax.rem(mq, 2)
            a_own = x_own + h * (y_own - x_own)
            b_own = y_own + h * (x_own - y_own)
            a_dev, b_dev, z_dev = (a_own, mq), (b_own, mq), (ms, flip(mq, 1))
            plan = (
                (own_part(h), part(ms, h), a_dev),
                (own_part(1 - h), part(ms, 1 - h), b_dev),
                (own_part(1 - h), part(ms, 1 - h), a_dev),
                (w_hbm[which], block(ms), core_dev),
                (part(a_own, h), part(a_own, h), b_dev),
                (part(a_own, 1 - h), part(a_own, 1 - h), z_dev),
                (block(a_own), block(a_own), core_dev),
                (part(b_own, 1 - h), part(b_own, 1 - h), core_dev),
                (part(d_own, h), part(d_own, h), z_dev),
                (part(d_own, h), part(d_own, h), core_dev),
                (part(b_own, h), part(b_own, h), core_dev),
                (part(d_own, 1 - h), part(d_own, 1 - h), core_dev),
            )
        else:
            plan = (
                (own_part(0), part(ms, 0), x_dev),
                (own_part(1), part(ms, 1), y_dev),
                (own_part(1), part(ms, 1), x_dev),
                (own_part(0), part(ms, 0), y_dev),
                (w_hbm[which], block(ms), core_dev),
                (part(x_own, 0), part(x_own, 0), y_dev),
                (part(y_own, 1), part(y_own, 1), x_dev),
                (block(x_own), block(x_own), core_dev),
                (block(y_own), block(y_own), core_dev),
                (part(d_own, 0), part(d_own, 0), core_dev),
                (part(d_own, 1), part(d_own, 1), core_dev),
            )
        return [
            pltpu.make_async_remote_copy(
                src_ref=src,
                dst_ref=dst,
                send_sem=w_send.at[base + step],
                recv_sem=w_recv.at[base + step],
                device_id=dev,
                device_id_type=MESH,
            )
            for step, (src, dst, dev) in enumerate(plan)
        ]

    w_copies = [gather_copies(which) for which in range(4)]

    def own_copy(which):
        depth = w_full[which].shape[0] // shard_count
        return pltpu.make_async_copy(
            w_hbm[which], w_full[which].at[rows_of(ms, depth)], w_local.at[which]
        )

    def gather_steps(which, *pairs):
        c = w_copies[which]
        for arrived_step, started in pairs:
            if arrived_step is not None:
                c[arrived_step].wait_recv()
            for step in started:
                c[step].start()

    def gather_own_first(which):
        gather_steps(which, (None, (0, 1)))

    def gather_own_second(which):
        gather_steps(which, (None, (2, 3) if which in ALONG_SEQ else (2, 3, 4)))
        own_copy(which).start()

    def gather_forward(which):
        if which in ALONG_SEQ:
            gather_steps(which, (0, (4,)))
        else:
            gather_steps(which, (0, (5,)), (1, (6,)))

    def gather_core(which):
        if which in ALONG_SEQ:
            gather_steps(which, (2, (5, 6)), (1, (7,)))
        else:
            gather_steps(which, (2, (7,)), (3, (8,)))

    def gather_last(which):
        if which in ALONG_SEQ:
            gather_steps(which, (4, (8, 9)))
        else:
            gather_steps(which, (5, (9,)), (6, (10,)))

    def gather_z1(which):
        if which in ALONG_SEQ:
            gather_steps(which, (5, (10,)))

    def gather_z2(which):
        if which in ALONG_SEQ:
            gather_steps(which, (8, (11,)))

    def gather_done(which):
        for step in (3, 6, 7, 9, 10, 11) if which in ALONG_SEQ else (4, 7, 8, 9, 10):
            w_copies[which][step].wait_recv()
        own_copy(which).wait()

    tok_in.wait()

    big = rows // 2

    def first_norm(i, carry):
        at = rows_of(i, big)
        xhat, inverse = norm_stats(tok[at, :].astype(F32))
        xhat1[at, :] = xhat
        inv1[at, :] = inverse
        for u in range(big // SPAN):
            xb_stage[pl.ds(i * (big // SPAN) + u, 1), :] = jnp.mean(
                xhat[u * SPAN : (u + 1) * SPAN], axis=0, keepdims=True
            )
        return carry

    lax.fori_loop(0, rows // big, first_norm, 0)
    half_width = width // 2
    xb_all[mt] = jnp.concatenate(
        [xb_stage[:, :half_width], xb_stage[:, half_width:]], axis=0
    ).astype(BF)

    shard_rows = width // shard_count
    for at, ref in enumerate(vec_refs):
        vec_own[at : at + 1, 0:shard_rows] = ref[...].astype(F32)
    vec_own[8 : 8 + up_bias_ref.shape[0], :] = up_bias_ref[...].astype(F32)

    pl.semaphore_wait(barrier, len(peers))

    def remote(source, target, send, recv, device):
        return pltpu.make_async_remote_copy(
            src_ref=source,
            dst_ref=target,
            send_sem=send,
            recv_sem=recv,
            device_id=device,
            device_id_type=MESH,
        )

    vec_copies = [
        remote(vec_own, vec_all.at[ms], vec_s.at[step], vec_r.at[step], peer)
        for step, peer in enumerate(shard_peers)
    ]
    xz_copies = [
        remote(xb_all.at[mt], xb_all.at[mt], xz_s.at[step], xz_r.at[step], peer)
        for step, peer in enumerate(seq_peers)
    ]

    def xb_group(owner):
        return xb_all.at[rows_of(owner, seq_count)]

    def xs_copy(owner, target):
        return remote(
            xb_group(owner), xb_group(owner), xs_s.at[target], xs_r.at[owner], (target, mq)
        )

    mean_rows = total * groups
    up_here = ff // shard_count
    parts = up_here // lanes
    part_cols = shard_count * lanes

    def vec_start():
        for c in vec_copies:
            c.start()
        vec_all[ms] = vec_own[...]

    def xz_start():
        for c in xz_copies:
            c.start()

    def xz_wait():
        for c in xz_copies:
            c.wait_recv()

    def order_rows():
        new_row = lax.broadcasted_iota(jnp.int32, (mean_rows, mean_rows), 0)
        old_row = lax.broadcasted_iota(jnp.int32, (mean_rows, mean_rows), 1)

        def scaled(value, down_by, up_by):
            quotient = lax.shift_right_logical(value, down_by.bit_length() - 1)
            return lax.shift_left(quotient, up_by.bit_length() - 1)

        wanted = (
            scaled(new_row & (spans_all - 1), spans_here, groups)
            + scaled(new_row, spans_all, spans_here)
            + (new_row & (spans_here - 1))
        )
        order[...] = (old_row == wanted).astype(BF)

    def xs_start():
        for target in range(1, shard_count):

            @pl.when(target > ms)
            def _(target=target):
                xs_copy(ms, target).start()

    def xs_wait():
        for owner in range(shard_count - 1):

            @pl.when(owner < ms)
            def _(owner=owner):
                xs_copy(owner, owner).wait_recv()

    def vec_wait():
        for c in vec_copies:
            c.wait_recv()
        low_lane = lax.broadcasted_iota(jnp.int32, (8, lanes), 1) < HD
        for at in range(shard_count // 2):
            even = vec_all[2 * at]
            odd = vec_all[2 * at + 1]
            vfull[:, at * lanes : (at + 1) * lanes] = jnp.where(
                low_lane, even[0:8, :], pltpu.roll(odd[0:8, :], HD, axis=1)
            )
        for owner in range(shard_count):
            piece = vec_all[owner]
            for r in range(up_here // lanes):
                start = r * part_cols + owner * lanes
                up_bias[0:1, start : start + lanes] = piece[8 + r : 9 + r, :]

    def vector(n):
        return vfull[n : n + 1, :]

    def project(n):
        if n == 0:
            normed[...] = (xhat1[...] * vector(0) + vector(1)).astype(BF)
        packed[:, n * width : (n + 1) * width] = dot(
            normed[...], wq[:, n * width : (n + 1) * width], 1, 0
        ).astype(BF)

    def span_means():
        arrived = xb_all[...].astype(F32)
        arrived = jnp.concatenate([arrived[:, 0:groups, :], arrived[:, groups:, :]], axis=2)
        arrived = arrived.reshape(mean_rows, width)
        arrived = (arrived * vector(0) + vector(1)).astype(BF)
        nbar[...] = dot(order[...], arrived, 1, 0).astype(BF)
        for n in range(2):
            kv_mean[:, n * width : (n + 1) * width] = dot(
                nbar[...], wq[:, (n + 1) * width : (n + 2) * width], 1, 0
            ).astype(BF)

    factor = HD ** (-0.5)
    keys = SPAN + spans_all

    def head_pair(ref_rows):
        low = lax.broadcasted_iota(jnp.int32, (SPAN, lanes), 1) < HD
        zero = jnp.zeros_like(ref_rows)
        return jnp.concatenate(
            [jnp.where(low, ref_rows, zero), jnp.where(low, zero, ref_rows)], axis=0
        )

    def score_shift(g):
        j = lax.broadcasted_iota(jnp.int32, (SPAN, SPAN), 0)
        i = lax.broadcasted_iota(jnp.int32, (SPAN, SPAN), 1)
        near = jnp.where(j <= i, 0.0, -jnp.inf).astype(F32)
        f = lax.broadcasted_iota(jnp.int32, (spans_all, SPAN), 0)
        here = mt * spans_here + g % spans_here
        far = jnp.where(f < here, math.log(SPAN), -jnp.inf).astype(F32)
        both = jnp.concatenate([near, far], axis=0)
        return jnp.concatenate([both, both], axis=1)

    low_out = lax.broadcasted_iota(jnp.int32, (SPAN, lanes), 1) < HD

    def pair_rows(at, mean_at, part, p):
        lo = p * lanes
        start = part * width + lo
        mean_lo = (part - 1) * width + lo
        return jnp.concatenate(
            [packed[at, start : start + lanes], kv_mean[mean_at, mean_lo : mean_lo + lanes]],
            axis=0,
        )

    four = groups // 2

    def attend(i):
        members = [(i * four + u, p) for u in range(four) for p in range(pairs)]
        shifts = [score_shift(i * four + u) for u in range(four)]
        places = {
            g: (rows_of(g, SPAN), rows_of(g // spans_here, spans_all)) for g, _ in members
        }
        scores = [
            dot(
                pair_rows(*places[g], 1, p),
                head_pair(packed[places[g][0], p * lanes : (p + 1) * lanes] * factor),
                1,
                1,
            )
            for g, p in members
        ]
        weights = []
        for n, (g, p) in enumerate(members):
            shifted = scores[n] + shifts[n // pairs]
            expo = jnp.exp(shifted - jnp.max(shifted, axis=0, keepdims=True))
            total_row = jnp.sum(expo, axis=0, keepdims=True)
            weights.append((expo * (1.0 / total_row)).astype(BF))
            probs[g * pairs + p] = weights[n]
        for n, (g, p) in enumerate(members):
            mixed = dot(weights[n], pair_rows(*places[g], 2, p), 0, 0)
            att[places[g][0], p * lanes : (p + 1) * lanes] = jnp.where(
                low_out, mixed[0:SPAN], mixed[SPAN : 2 * SPAN]
            ).astype(BF)

    def second_norm():
        mid = tok[...].astype(F32) + dot(att[...], wo[...], 1, 0) + vector(2)
        middle[...] = mid
        xhat, inverse = norm_stats(mid)
        xhat2[...] = xhat
        inv2[...] = inverse
        second[...] = (xhat * vector(3) + vector(4)).astype(BF)

    half_owners = shard_count // 2
    sub = half_owners * lanes

    def unit_starts(part, side):
        return [
            (side * half_owners + n) * up_here + part * lanes for n in range(half_owners)
        ]

    def up_tile(part, side):
        return jnp.concatenate(
            [wu[:, a : a + lanes] for a in unit_starts(part, side)], axis=1
        )

    def down_tile(part, side):
        return jnp.concatenate(
            [wd[a : a + lanes, :] for a in unit_starts(part, side)], axis=0
        )

    def columns_of(part, side):
        start = part * part_cols + side * sub
        return slice(start, start + sub)

    every = [(part, side) for part in range(parts) for side in range(2)]

    def gelu_parts(before):
        cdf = 0.5 + 0.5 * lax.erf(before * math.sqrt(0.5))
        density = jnp.exp(before * before * -0.5) * (1.0 / math.sqrt(2.0 * math.pi))
        return before * cdf, cdf + before * density

    def feed_up(part, side):
        cols = columns_of(part, side)
        before = dot(second[...], up_tile(part, side), 1, 0) + up_bias[0:1, cols]
        value, slope = gelu_parts(before)
        hidden[:, cols] = value.astype(BF)
        gbefore[:, cols] = slope.astype(BF)

    def back_down(part, side):
        cols = columns_of(part, side)
        grad = dot(cot[...], down_tile(part, side), 1, 1)
        gbefore[:, cols] = (grad * gbefore[:, cols].astype(F32)).astype(BF)

    def chunk(which):
        if which in (D0, D1):
            refs, n = (g_down, r1_down, r2_down, r3_down, r4_down, own_down), which - D0
        elif which in (U0, U1):
            refs, n = (g_up, r1_up, r2_up, r3_up, r4_up, own_up), which - U0
        elif which == GO:
            refs, n = (g_out, r1_out, r2_out, r3_out, r4_out, own_out), 0
        elif which == QA:
            refs, n = (g_two, r1_two, r2_two, r3_two, r4_two, own_two), 0
        else:
            refs, n = (g_one, r1_one, r2_one, r3_one, r4_one, own_one), which - Q2
        return tuple(ref.at[n] for ref in refs)

    here, x_blk, y_blk, d_blk = yx, flip(yx, 1), flip(yx, 2), flip(flip(yx, 1), 2)
    z_dev = (ms, flip(mq, 1))
    z_mid = (ms, seq_count - 1 - mq)

    def reduce_copies(which):
        g, r1, r2, r3, r4, own = chunk(which)
        half = g.shape[2] // 2
        base = which * REDUCE_STEPS
        plan = (
            (g.at[1 - core], r1, core_dev),
            (g.at[core, d_blk, pl.ds(0, half)], r2.at[0], x_dev),
            (g.at[core, d_blk, pl.ds(half, half)], r2.at[1], y_dev),
            (g.at[core, x_blk], r3.at[0], x_dev),
            (g.at[core, y_blk], r3.at[1], y_dev),
            (own, r4.at[0], z_dev),
            (own, r4.at[1], z_mid),
            (own, r4.at[0], z_dev),
        )
        copies = [
            pltpu.make_async_remote_copy(
                src_ref=src,
                dst_ref=dst,
                send_sem=red_s.at[base + step],
                recv_sem=red_r.at[base + step],
                device_id=dev,
                device_id_type=MESH,
            )
            for step, (src, dst, dev) in enumerate(plan)
        ]
        return copies

    r_copies = [reduce_copies(which) for which in range(CHUNKS)]
    edge = jnp.logical_or(mq == 0, mq == seq_count - 1)
    inner = jnp.logical_not(edge)

    def add_rows(target, *sources):
        count = target.shape[0]
        step = min(count, 32)

        def one(i, carry):
            at = rows_of(i, step)
            value = target[at, :]
            for source in sources:
                value = value + source[at, :]
            target[at, :] = value
            return carry

        lax.fori_loop(0, count // step, one, 0)

    def reduce_a(which):
        r_copies[which][0].start()

    def reduce_b(which):
        g, r1, r2, r3, r4, own = chunk(which)
        c = r_copies[which]
        c[0].wait_recv()
        add_rows(g.at[core, d_blk], r1.at[d_blk])
        c[1].start()
        c[2].start()
        for blk in (x_blk, y_blk, here):
            add_rows(g.at[core, blk], r1.at[blk])

    def reduce_c(which):
        g, r1, r2, r3, r4, own = chunk(which)
        half = g.shape[2] // 2
        c = r_copies[which]
        c[1].wait_recv()
        add_rows(g.at[core, y_blk, pl.ds(0, half)], r2.at[0])
        c[4].start()
        c[2].wait_recv()
        add_rows(g.at[core, x_blk, pl.ds(half, half)], r2.at[1])
        c[3].start()

    def reduce_d(which):
        g, r1, r2, r3, r4, own = chunk(which)
        c = r_copies[which]
        c[3].wait_recv()
        c[4].wait_recv()
        count = own.shape[0]

        def one(i, carry):
            at = rows_of(i, 32)
            value = (
                g[core, here, at, :].astype(F32)
                + r3[0, at, :].astype(F32)
                + r3[1, at, :].astype(F32)
            )
            own[at, :] = value.astype(BF)
            return carry

        lax.fori_loop(0, count // 32, one, 0)

        @pl.when(edge)
        def _():
            c[5].start()

    def reduce_e(which):
        g, r1, r2, r3, r4, own = chunk(which)
        c = r_copies[which]

        @pl.when(inner)
        def _():
            c[5].wait_recv()
            add_rows(own, r4.at[0])
            c[6].start()

    def emit(which, source):
        target = {
            D0: gd_hbm.at[pl.ds(0, lanes)],
            D1: gd_hbm.at[pl.ds(lanes, lanes)],
            U0: gu_hbm.at[0],
            U1: gu_hbm.at[1],
            GO: go_hbm,
            QA: gt_hbm,
            Q2: gs_hbm.at[0],
            Q3: gs_hbm.at[1],
        }[which]
        return pltpu.make_async_copy(source, target, out_sem.at[which])

    def reduce_f(which):
        g, r1, r2, r3, r4, own = chunk(which)
        c = r_copies[which]

        @pl.when(inner)
        def _():
            c[6].wait_recv()
            c[6].wait_send()
            add_rows(own, r4.at[1])
            c[7].start()
            emit(which, own).start()

    def reduce_g(which):
        g, r1, r2, r3, r4, own = chunk(which)
        c = r_copies[which]

        @pl.when(edge)
        def _():
            c[5].wait_send()
            c[7].wait_recv()
            emit(which, r4.at[0]).start()

        @pl.when(inner)
        def _():
            c[7].wait_send()

        for step in range(5):
            c[step].wait_send()

    def put_rows(target, piece):
        count = piece.shape[0] // shard_count
        for owner in range(shard_count):
            target[owner % 2, owner // 2] = piece[owner * count : (owner + 1) * count]

    def part_of(part):
        return slice(part * part_cols, (part + 1) * part_cols)

    def down_grad(part):
        put_rows(g_down.at[part], dot(hidden[:, part_of(part)], cot[...], 0, 0).astype(BF))

    def up_grad(part):
        cols = part_of(part)
        put_rows(g_up.at[part], dot(second[...], gbefore[:, cols], 0, 0).astype(BF))
        upsum[0:1, cols] = jnp.sum(gbefore[:, cols].astype(F32), axis=0, keepdims=True)

    def back_second(i):
        at = rows_of(i, big)
        up_perm = jnp.concatenate([up_tile(*t) for t in every], axis=1)
        grad = dot(gbefore[at, :], up_perm, 1, 1)
        xhat = xhat2[at, :]
        vsum[3:4, :] += jnp.sum(grad * xhat, axis=0, keepdims=True)
        vsum[4:5, :] += jnp.sum(grad, axis=0, keepdims=True)
        incoming = cot[at, :].astype(F32)
        vsum[5:6, :] += jnp.sum(incoming, axis=0, keepdims=True)
        grad_mid = incoming + norm_back(grad, xhat, inv2[at, :], vector(3))
        gmid[at, :] = grad_mid
        branch = grad_mid.astype(BF)
        gbranch[at, :] = branch
        vsum[2:3, :] += jnp.sum(branch.astype(F32), axis=0, keepdims=True)
        gatt[at, :] = dot(branch, wo[...], 1, 1).astype(BF)

    def out_grad():
        put_rows(g_out.at[0], dot(att[...], gbranch[...], 0, 0).astype(BF))

    low_keys = lax.broadcasted_iota(jnp.int32, (SPAN, lanes), 1) < HD

    def attend_back(p):
        lo = p * lanes
        places = [(rows_of(g, SPAN), rows_of(g // spans_here, spans_all)) for g in range(groups)]
        members = []
        for g in range(groups):
            at, mean_at = places[g]
            go = head_pair(gatt[at, lo : lo + lanes])
            weights = probs[g * pairs + p]
            gw = dot(pair_rows(at, mean_at, 2, p), go, 1, 1)
            gv = dot(weights, go, 1, 0)
            members.append((weights, gw, gv))
        scores = []
        for weights, gw, gv in members:
            prob = weights.astype(F32)
            row_inner = jnp.sum(prob * gw, axis=0, keepdims=True)
            scores.append((prob * (gw - row_inner)).astype(BF))
        far_k, far_v = None, None
        for g in range(groups):
            at, mean_at = places[g]
            gv = members[g][2]
            q = head_pair(packed[at, lo : lo + lanes])
            gq = dot(scores[g], pair_rows(at, mean_at, 1, p), 0, 0)
            gk = dot(scores[g], q, 1, 0) * factor
            gbefore[at, lo : lo + lanes] = (
                jnp.where(low_keys, gq[0:SPAN], gq[SPAN : 2 * SPAN]) * factor
            ).astype(BF)
            gbefore[at, width + lo : width + lo + lanes] = gk[0:SPAN].astype(BF)
            gbefore[at, 2 * width + lo : 2 * width + lo + lanes] = gv[0:SPAN].astype(BF)
            first = g % spans_here == 0
            far_k = gk[SPAN:] if first else far_k + gk[SPAN:]
            far_v = gv[SPAN:] if first else far_v + gv[SPAN:]
            if g % spans_here == spans_here - 1:
                gkv[mean_at, lo : lo + lanes] = far_k.astype(BF)
                gkv[mean_at, width + lo : width + lo + lanes] = far_v.astype(BF)

    def first_grad(lo, count, target):
        grads = [gbefore[:, m * width + lo : m * width + lo + count] for m in range(3)]
        means = [gkv[:, m * width + lo : m * width + lo + count] for m in range(2)]
        local_part = dot(normed[...], jnp.concatenate(grads, axis=1), 0, 0)
        mean_part = dot(nbar[...], jnp.concatenate(means, axis=1), 0, 0)
        piece = jnp.concatenate(
            [local_part[:, 0:count], local_part[:, count:] + mean_part], axis=1
        )
        put_rows(target, piece.astype(BF))

    def mean_grad():
        gmean = dot(gkv[...], wq[:, width : 3 * width], 1, 1).astype(BF)
        gmean = dot(order[...], gmean, 0, 0).reshape(total, groups, width)
        gn_send[...] = jnp.concatenate(
            [gmean[:, :, :half_width], gmean[:, :, half_width:]], axis=1
        ).astype(BF)

    def gs_copy(source, target):
        return remote(
            gn_send.at[rows_of(target, seq_count)],
            gn_recv.at[source],
            gs_s.at[target],
            gs_r.at[source],
            (target, mq),
        )

    def gs_start():
        for target in range(shard_count - 1):

            @pl.when(target < ms)
            def _(target=target):
                gs_copy(ms, target).start()

    def gs_wait():
        gz_send[...] = gn_send[rows_of(ms, seq_count)]
        for source in range(1, shard_count):

            @pl.when(source > ms)
            def _(source=source):
                gs_copy(source, source).wait_recv()
                gz_send[...] += gn_recv[source]

    gz_copies = [
        remote(gz_send.at[peer[1]], gz_recv.at[mq], gz_s.at[step], gz_r.at[step], peer)
        for step, peer in enumerate(seq_peers)
    ]

    def gz_start():
        for c in gz_copies:
            c.start()
        gz_recv[mq] = gz_send[mq]

    def gz_wait():
        for c in gz_copies:
            c.wait_recv()
        gnbar[...] = jnp.sum(gz_recv[...].astype(F32), axis=0)

    bout_out = pltpu.make_async_copy(gbranch, block_out_hbm, io_sem.at[2])

    def out_block(i):
        at = rows_of(i, big)
        down_perm = jnp.concatenate([down_tile(*t) for t in every], axis=0)
        gbranch[at, :] = (
            middle[at, :] + dot(hidden[at, :], down_perm, 1, 0) + vector(5)
        ).astype(BF)
        if i == 1:
            bout_out.start()

    tok_out = pltpu.make_async_copy(gmid, grad_tok_hbm, io_sem.at[3])

    def back_first(i):
        at = rows_of(i, big)
        shares = []
        for u in range(big // SPAN):
            g = i * (big // SPAN) + u
            share = jnp.concatenate(
                [gnbar[g : g + 1, :], gnbar[groups + g : groups + g + 1, :]], axis=1
            ) * (1.0 / SPAN)
            shares.append(jnp.broadcast_to(share, (SPAN, width)))
        grad = dot(gbefore[at, 0 : 3 * width], wq[...], 1, 1) + jnp.concatenate(
            shares, axis=0
        )
        xhat = xhat1[at, :]
        vsum[0:1, :] += jnp.sum(grad * xhat, axis=0, keepdims=True)
        vsum[1:2, :] += jnp.sum(grad, axis=0, keepdims=True)
        gmid[at, :] = gmid[at, :] + norm_back(grad, xhat, inv1[at, :], vector(0))
        if i == 1:
            tok_out.start()

    def vec_build():
        for owner in range(shard_count):
            at = owner // 2
            piece = vsum[:, at * lanes : (at + 1) * lanes]
            if owner % 2 == 1:
                piece = pltpu.roll(piece, HD, axis=1)
            vec_send[owner, 0:8, :] = piece
            vec_send[owner, 8:16, :] = jnp.zeros((8, lanes), F32)
            for r in range(parts):
                start = r * part_cols + owner * lanes
                vec_send[owner, 8 + r : 9 + r, :] = upsum[0:1, start : start + lanes]

    vo_copies = [
        remote(vec_send.at[peer[0]], vec_recv.at[ms], vo_s.at[step], vo_r.at[step], peer)
        for step, peer in enumerate(shard_peers)
    ]
    vz_copies = [
        remote(vec_line.at[mq], vec_line.at[mq], vz_s.at[step], vz_r.at[step], peer)
        for step, peer in enumerate(seq_peers)
    ]

    def vo_start():
        for c in vo_copies:
            c.start()
        vec_recv[ms] = vec_send[ms]

    def vo_wait():
        for c in vo_copies:
            c.wait_recv()
        vec_line[mq] = jnp.sum(vec_recv[...], axis=0)

    def vz_start():
        for c in vz_copies:
            c.start()

    def vz_wait():
        for c in vz_copies:
            c.wait_recv()
        vec_out_ref[...] = jnp.sum(vec_line[...], axis=0)

    vsum[...] = jnp.zeros_like(vsum)
    cot_in.wait()
    gather_own_first(QKV)
    order_rows()
    gather_own_second(QKV)
    gather_own_first(OUT)
    gather_forward(QKV)
    vec_start()
    gather_own_second(OUT)
    gather_core(QKV)
    gather_forward(OUT)
    gather_own_first(UP)
    xz_start()
    gather_last(QKV)
    xz_wait()
    xs_start()
    gather_last(OUT)
    gather_done(QKV)
    vec_wait()
    gather_core(OUT)
    project(0)
    gather_own_second(UP)
    gather_forward(UP)
    gather_done(OUT)
    gather_own_first(DOWN)
    project(1)
    gather_own_second(DOWN)
    project(2)
    xs_wait()
    span_means()
    attend(0)
    gather_core(UP)
    attend(1)
    gather_last(UP)
    second_norm()
    gather_done(UP)
    feed_up(0, 0)
    gather_forward(DOWN)
    feed_up(0, 1)
    down_grad(0)
    reduce_a(D0)
    gather_core(DOWN)
    feed_up(1, 0)
    feed_up(1, 1)
    gather_last(DOWN)
    reduce_b(D0)
    down_grad(1)
    gather_done(DOWN)
    reduce_a(D1)
    back_down(0, 0)
    back_down(0, 1)
    up_grad(0)
    reduce_c(D0)
    back_down(1, 0)
    back_down(1, 1)
    up_grad(1)
    reduce_a(U1)
    reduce_a(U0)
    reduce_b(D1)
    back_second(0)
    reduce_d(D0)
    reduce_b(U1)
    reduce_c(D1)
    reduce_b(U0)
    back_second(1)
    out_grad()
    reduce_c(U1)
    reduce_a(GO)
    attend_back(0)
    reduce_e(D0)
    attend_back(1)
    reduce_d(D1)
    reduce_b(GO)
    first_grad(0, 2 * lanes, g_two.at[0])
    reduce_a(QA)
    reduce_c(U0)
    attend_back(2)
    reduce_d(U1)
    reduce_b(QA)
    reduce_c(GO)
    attend_back(3)
    reduce_e(D1)
    mean_grad()
    gs_start()
    reduce_d(U0)
    reduce_f(D0)
    first_grad(2 * lanes, lanes, g_one.at[0])
    reduce_a(Q2)
    reduce_e(U1)
    reduce_c(QA)
    first_grad(3 * lanes, lanes, g_one.at[1])
    reduce_d(GO)
    reduce_a(Q3)
    reduce_b(Q2)
    gs_wait()
    reduce_f(D1)
    gz_start()
    reduce_b(Q3)
    reduce_e(U0)
    reduce_d(QA)
    reduce_f(U1)
    reduce_c(Q2)
    reduce_e(GO)
    reduce_c(Q3)
    gz_wait()
    back_first(0)
    reduce_e(QA)
    reduce_f(U0)
    reduce_g(D1)
    reduce_d(Q2)
    reduce_d(Q3)
    back_first(1)
    reduce_g(D0)
    reduce_g(U1)
    reduce_f(GO)
    reduce_e(Q2)
    vec_build()
    vo_start()
    reduce_e(Q3)
    reduce_f(QA)
    vo_wait()
    reduce_f(Q2)
    reduce_g(GO)
    vz_start()
    reduce_f(Q3)
    out_block(0)
    reduce_g(QA)
    reduce_g(U0)
    out_block(1)
    reduce_g(Q2)
    vz_wait()
    reduce_g(Q3)

    for target in range(1, shard_count):

        @pl.when(target > ms)
        def _(target=target):
            xs_copy(ms, target).wait_send()

    for target in range(shard_count - 1):

        @pl.when(target < ms)
        def _(target=target):
            gs_copy(ms, target).wait_send()

    for c in vec_copies + xz_copies + gz_copies + vo_copies + vz_copies:
        c.wait_send()
    for which in range(4):
        for c in w_copies[which]:
            c.wait_send()
    for which in range(CHUNKS):
        emit(which, chunk(which)[5]).wait()
    bout_out.wait()
    tok_out.wait()


def finish_kernel(*refs):
    raw, vec, outs, vec_outs = refs[0:7], refs[7], refs[8:14], refs[14:21]
    low_refs, high_refs, in_sem, out_sem = refs[21:28], refs[28:32], refs[32], refs[33]
    order = (5, 6, 4, 0, 1, 2, 3)
    loads = [pltpu.make_async_copy(raw[n], low_refs[n], in_sem.at[n]) for n in range(7)]
    for n in order:
        loads[n].start()
    for n, ref in enumerate(vec_outs[0:6]):
        ref[...] = vec[n : n + 1, 0 : ref.shape[1]]
    vec_outs[6][...] = vec[8 : 8 + vec_outs[6].shape[0], :]
    stores = []
    lanes = 2 * HD

    def store(ready, at):
        stores.append(pltpu.make_async_copy(ready, outs[at], out_sem.at[at]))
        stores[-1].start()

    for n in order:
        loads[n].wait()
        low = low_refs[n]
        if n < 2:
            store(low, n)
        elif n == 2:
            for part in range(3):
                start = part * 4 * lanes
                high_refs[0][:, start : start + 2 * lanes] = low[
                    :, part * 2 * lanes : (part + 1) * 2 * lanes
                ].astype(F32)
        elif n == 3:
            for part in range(3):
                for one in range(2):
                    start = (part * 4 + 2 + one) * lanes
                    high_refs[0][:, start : start + lanes] = low[
                        one, :, part * lanes : (part + 1) * lanes
                    ].astype(F32)
            store(high_refs[0], 2)
        elif n == 5:
            high = high_refs[2]
            part_count, _, columns = low.shape
            for part in range(part_count):
                for owner in range(columns // lanes):
                    start = (owner * part_count + part) * lanes
                    high[:, start : start + lanes] = low[
                        part, :, owner * lanes : (owner + 1) * lanes
                    ].astype(F32)
            store(high, 4)
        else:
            high = high_refs[n - 3]
            high[...] = low[...].astype(F32)
            store(high, n - 1)
    for c in stores:
        c.wait()


def local_block(
    tokens,
    ln1_gain,
    ln1_bias,
    qkv_weight,
    out_weight,
    out_bias,
    ln2_gain,
    ln2_bias,
    up_weight,
    up_bias,
    down_weight,
    down_bias,
    cotangent,
):
    seq_count = lax.axis_size("seq")
    shard_count = lax.axis_size("shard")
    total = seq_count * shard_count
    batch, local_len, width = tokens.shape
    rows = batch * local_len
    groups = rows // SPAN
    spans_all = local_len // SPAN * total
    keys = SPAN + spans_all
    ff = up_weight.shape[1]
    lanes = 2 * HD
    shard_rows = width // shard_count
    down_rows = ff // shard_count
    vmem = pl.BlockSpec(memory_space=pltpu.VMEM)
    hbm = pl.BlockSpec(memory_space=pl.ANY)
    dma = pltpu.SemaphoreType.DMA
    half_yx = shard_count // 2

    def grads(count, columns, lead=()):
        half = count // 2
        return (
            pltpu.VMEM(lead + (2, half_yx, count, columns), BF),
            pltpu.VMEM(lead + (half_yx, count, columns), BF),
            pltpu.VMEM(lead + (2, half, columns), BF),
            pltpu.VMEM(lead + (2, count, columns), BF),
            pltpu.VMEM(lead + (2, count, columns), BF),
            pltpu.VMEM(lead + (count, columns), BF),
        )

    parts = down_rows // lanes
    part_cols = ff // parts
    down_bufs = grads(lanes, width, (parts,))
    up_bufs = grads(shard_rows, part_cols, (parts,))
    out_bufs = grads(shard_rows, width, (1,))
    two_bufs = grads(shard_rows, 6 * lanes, (1,))
    one_bufs = grads(shard_rows, 3 * lanes, (2,))
    grad_bufs = [
        buf
        for five in zip(down_bufs, up_bufs, out_bufs, two_bufs, one_bufs)
        for buf in five
    ]
    scratch = [
        pltpu.VMEM((rows, width), BF),
        pltpu.VMEM((rows, width), BF),
        pltpu.VMEM((width, 3 * width), BF),
        pltpu.VMEM((width, width), BF),
        pltpu.VMEM((width, ff), BF),
        pltpu.VMEM((ff, width), BF),
        pltpu.VMEM((16, lanes), F32),
        pltpu.VMEM((shard_count, 16, lanes), F32),
        pltpu.VMEM((rows, width), F32),
        pltpu.VMEM((rows, 1), F32),
        pltpu.VMEM((groups, width), F32),
        pltpu.VMEM((total, 2 * groups, width // 2), BF),
        pltpu.VMEM((batch * spans_all, batch * spans_all), BF),
        pltpu.VMEM((8, width), F32),
        pltpu.VMEM((8, ff), F32),
        pltpu.VMEM((rows, width), BF),
        pltpu.VMEM((rows, 3 * width), BF),
        pltpu.VMEM((batch * spans_all, width), BF),
        pltpu.VMEM((batch * spans_all, 2 * width), BF),
        pltpu.VMEM((groups * H // 2, keys, 2 * SPAN), BF),
        pltpu.VMEM((rows, width), BF),
        pltpu.VMEM((rows, width), F32),
        pltpu.VMEM((rows, width), F32),
        pltpu.VMEM((rows, 1), F32),
        pltpu.VMEM((rows, width), BF),
        pltpu.VMEM((rows, width), F32),
        pltpu.VMEM((rows, ff), BF),
        pltpu.VMEM((rows, ff), BF),
        pltpu.VMEM((rows, width), BF),
        pltpu.VMEM((rows, width), BF),
        pltpu.VMEM((batch * spans_all, 2 * width), BF),
        pltpu.VMEM((total, 2 * groups, width // 2), BF),
        pltpu.VMEM((shard_count, seq_count, 2 * groups, width // 2), BF),
        pltpu.VMEM((seq_count, 2 * groups, width // 2), BF),
        pltpu.VMEM((seq_count, 2 * groups, width // 2), BF),
        pltpu.VMEM((2 * groups, width // 2), F32),
        pltpu.VMEM((8, width), F32),
        pltpu.VMEM((8, ff), F32),
        pltpu.VMEM((shard_count, 16, lanes), F32),
        pltpu.VMEM((shard_count, 16, lanes), F32),
        pltpu.VMEM((seq_count, 16, lanes), F32),
        *grad_bufs,
        dma((4 * GATHER_STEPS,)),
        dma((4 * GATHER_STEPS,)),
        dma((4,)),
        dma((4,)),
        dma((shard_count,)),
        dma((shard_count,)),
        dma((seq_count,)),
        dma((seq_count,)),
        dma((shard_count,)),
        dma((shard_count,)),
        dma((shard_count,)),
        dma((shard_count,)),
        dma((seq_count,)),
        dma((seq_count,)),
        dma((shard_count,)),
        dma((shard_count,)),
        dma((seq_count,)),
        dma((seq_count,)),
        dma((CHUNKS * REDUCE_STEPS,)),
        dma((CHUNKS * REDUCE_STEPS,)),
        dma((CHUNKS,)),
    ]
    vectors = [
        v.reshape(1, shard_rows)
        for v in (ln1_gain, ln1_bias, out_bias, ln2_gain, ln2_bias, down_bias)
    ]
    raw = pl.pallas_call(
        functools.partial(block_kernel, batch, shard_count, seq_count),
        out_shape=(
            jax.ShapeDtypeStruct((rows, width), BF),
            jax.ShapeDtypeStruct((rows, width), F32),
            jax.ShapeDtypeStruct((shard_rows, 6 * lanes), BF),
            jax.ShapeDtypeStruct((2, shard_rows, 3 * lanes), BF),
            jax.ShapeDtypeStruct((shard_rows, width), BF),
            jax.ShapeDtypeStruct((parts, shard_rows, part_cols), BF),
            jax.ShapeDtypeStruct((down_rows, width), BF),
            jax.ShapeDtypeStruct((16, lanes), F32),
        ),
        in_specs=[hbm, hbm, [vmem] * 6, vmem, hbm, hbm, hbm, hbm],
        out_specs=(hbm,) * 7 + (vmem,),
        scratch_shapes=scratch,
        compiler_params=pltpu.CompilerParams(
            collective_id=0, has_side_effects=True, vmem_limit_bytes=63 * 2**20
        ),
        name="block",
    )(
        tokens.reshape(rows, width),
        cotangent.reshape(rows, width),
        vectors,
        up_bias.reshape(-1, lanes),
        qkv_weight,
        out_weight,
        up_weight,
        down_weight,
    )
    low_shapes = [
        (shard_rows, 6 * lanes),
        (2, shard_rows, 3 * lanes),
        (shard_rows, width),
        (parts, shard_rows, part_cols),
        (down_rows, width),
    ]
    high_shapes = [
        (shard_rows, 3 * width),
        (shard_rows, width),
        (shard_rows, ff),
        (down_rows, width),
    ]
    done = pl.pallas_call(
        finish_kernel,
        out_shape=(
            jax.ShapeDtypeStruct((rows, width), BF),
            jax.ShapeDtypeStruct((rows, width), F32),
            *(jax.ShapeDtypeStruct(shape, F32) for shape in high_shapes),
            *(jax.ShapeDtypeStruct((1, shard_rows), F32) for _ in range(6)),
            jax.ShapeDtypeStruct((down_rows // lanes, lanes), F32),
        ),
        in_specs=[hbm] * 7 + [vmem],
        out_specs=(hbm,) * 6 + (vmem,) * 7,
        scratch_shapes=[
            pltpu.VMEM((rows, width), BF),
            pltpu.VMEM((rows, width), F32),
            *(pltpu.VMEM(shape, BF) for shape in low_shapes),
            *(pltpu.VMEM(shape, F32) for shape in high_shapes),
            dma((7,)),
            dma((6,)),
        ],
        compiler_params=pltpu.CompilerParams(vmem_limit_bytes=62 * 2**20),
        name="finish",
    )(*raw)
    block_out, grad_tokens, g_qkv, g_out, g_up, g_down = done[0:6]
    vec_grads = [v.reshape(shard_rows) for v in done[6:12]]
    return (
        block_out.reshape(tokens.shape),
        grad_tokens.reshape(tokens.shape),
        vec_grads[0],
        vec_grads[1],
        g_qkv,
        g_out,
        vec_grads[2],
        vec_grads[3],
        vec_grads[4],
        g_up,
        done[12].reshape(down_rows),
        g_down,
        vec_grads[5],
    )


def layer_norm(values, norm_gain, norm_shift):
    center = values - jnp.mean(values, axis=-1, keepdims=True)
    spread = jnp.mean(center * center, axis=-1, keepdims=True)
    return center * lax.rsqrt(spread + epsilon) * norm_gain + norm_shift


def gelu_exact(values):
    return jax.nn.gelu(values, approximate=False)


def contract_rows(left_matrix, right_matrix):
    return lax.dot_general(
        left_matrix, right_matrix, (((0,), (0,)), ((), ())), preferred_element_type=jnp.float32
    )


def times_transpose(left_matrix, right_matrix):
    return lax.dot_general(
        left_matrix, right_matrix, (((1,), (1,)), ((), ())), preferred_element_type=jnp.float32
    )


def joint_scores(query_rows, key_rows, key_all, causal, earlier):
    factor = HD ** (-0.5)
    local_part = factor * jnp.einsum(
        "bjihd,bjkhd->bjhik", query_rows, key_rows, preferred_element_type=jnp.float32
    )
    summary = factor * jnp.einsum(
        "bjihd,bfhd->bjhif", query_rows, key_all, preferred_element_type=jnp.float32
    ) + math.log(SPAN)
    local_part = jnp.where(causal[None, None, None], local_part, -jnp.inf)
    summary = jnp.where(earlier[None, :, None, None, :], summary, -jnp.inf)
    return (local_part, summary)


def attend(query_rows, key_rows, value_rows, key_all, value_all, causal, earlier):
    local_part, summary = joint_scores(query_rows, key_rows, key_all, causal, earlier)
    row_max = jnp.maximum(jnp.max(local_part, axis=-1), jnp.max(summary, axis=-1))
    local_exp = jnp.exp(local_part - row_max[..., None])
    summary_exp = jnp.exp(summary - row_max[..., None])
    row_total = jnp.sum(local_exp, axis=-1) + jnp.sum(summary_exp, axis=-1)
    log_total = row_max + jnp.log(row_total)
    local_weights = (local_exp / row_total[..., None]).astype(jnp.bfloat16)
    summary_weights = (summary_exp / row_total[..., None]).astype(jnp.bfloat16)
    mixed_heads = jnp.einsum(
        "bjhik,bjkhd->bjihd", local_weights, value_rows, preferred_element_type=jnp.float32
    )
    mixed_heads = mixed_heads + jnp.einsum(
        "bjhif,bfhd->bjihd", summary_weights, value_all, preferred_element_type=jnp.float32
    )
    return (mixed_heads, log_total, local_weights, summary_weights)


def attend_back(
    grad_mixed,
    query_rows,
    key_rows,
    value_rows,
    key_all,
    value_all,
    causal,
    earlier,
    log_total,
    local_weights,
    summary_weights,
):
    factor = HD ** (-0.5)
    local_part, summary = joint_scores(query_rows, key_rows, key_all, causal, earlier)
    local_prob = jnp.exp(local_part - log_total[..., None])
    summary_prob = jnp.exp(summary - log_total[..., None])
    grad_local_w = jnp.einsum(
        "bjihd,bjkhd->bjhik", grad_mixed, value_rows, preferred_element_type=jnp.float32
    )
    grad_summary_w = jnp.einsum(
        "bjihd,bfhd->bjhif", grad_mixed, value_all, preferred_element_type=jnp.float32
    )
    row_inner = jnp.sum(local_prob * grad_local_w, axis=-1) + jnp.sum(
        summary_prob * grad_summary_w, axis=-1
    )
    grad_local = (local_prob * (grad_local_w - row_inner[..., None])).astype(jnp.bfloat16)
    grad_summary = (summary_prob * (grad_summary_w - row_inner[..., None])).astype(jnp.bfloat16)
    grad_query = jnp.einsum(
        "bjhik,bjkhd->bjihd", grad_local, key_rows, preferred_element_type=jnp.float32
    )
    grad_query = factor * (
        grad_query
        + jnp.einsum("bjhif,bfhd->bjihd", grad_summary, key_all, preferred_element_type=jnp.float32)
    )
    grad_key = factor * jnp.einsum(
        "bjhik,bjihd->bjkhd", grad_local, query_rows, preferred_element_type=jnp.float32
    )
    grad_key_all = factor * jnp.einsum(
        "bjhif,bjihd->bfhd", grad_summary, query_rows, preferred_element_type=jnp.float32
    )
    grad_value = jnp.einsum(
        "bjhik,bjihd->bjkhd", local_weights, grad_mixed, preferred_element_type=jnp.float32
    )
    grad_value_all = jnp.einsum(
        "bjhif,bjihd->bfhd", summary_weights, grad_mixed, preferred_element_type=jnp.float32
    )
    return (grad_query, grad_key, grad_value, grad_key_all, grad_value_all)


def local_general(
    tokens,
    ln1_gain,
    ln1_bias,
    qkv_weight,
    out_weight,
    out_bias,
    ln2_gain,
    ln2_bias,
    up_weight,
    up_bias,
    down_weight,
    down_bias,
    cotangent,
):
    seq_count = lax.axis_size("seq")
    shard_count = lax.axis_size("shard")
    shard_place = lax.axis_index("shard")
    batch_size, local_len, model_width = tokens.shape
    heads_here = H // seq_count
    head_width = heads_here * HD
    group_len = local_len * seq_count
    spans_here = group_len // SPAN
    spans_all = spans_here * shard_count
    row_count = batch_size * local_len
    shards = (
        ln1_gain,
        ln1_bias,
        qkv_weight,
        out_weight,
        out_bias,
        ln2_gain,
        ln2_bias,
        up_weight,
        up_bias,
        down_weight,
        down_bias,
    )
    gathered = (
        lax.all_gather(shards[0], "shard", axis=0, tiled=True),
        lax.all_gather(shards[1], "shard", axis=0, tiled=True),
        lax.all_gather(shards[2], "shard", axis=0, tiled=True),
        lax.all_gather(shards[3], "shard", axis=0, tiled=True),
        lax.all_gather(shards[4], "shard", axis=0, tiled=True),
        lax.all_gather(shards[5], "shard", axis=0, tiled=True),
        lax.all_gather(shards[6], "shard", axis=0, tiled=True),
        lax.all_gather(shards[7], "shard", axis=0, tiled=True),
        lax.all_gather(shards[8], "shard", axis=0, tiled=True),
        lax.all_gather(shards[9], "shard", axis=0, tiled=True),
        lax.all_gather(shards[10], "shard", axis=0, tiled=True),
    )
    (
        gain_one,
        bias_one,
        qkv_full,
        out_full,
        out_shift,
        gain_two,
        bias_two,
        up_full,
        up_shift,
        down_full,
        down_shift,
    ) = gathered
    flat_tokens = tokens.reshape(row_count, model_width).astype(jnp.float32)
    normed = layer_norm(
        flat_tokens, gain_one.astype(jnp.float32), bias_one.astype(jnp.float32)
    ).astype(jnp.bfloat16)
    packed = jnp.dot(normed, qkv_full, preferred_element_type=jnp.float32).astype(jnp.bfloat16)
    span_place = jnp.arange(SPAN)
    packed_heads = packed.reshape(batch_size, local_len, 3, seq_count, head_width)
    headed = lax.all_to_all(packed_heads, "seq", split_axis=3, concat_axis=1, tiled=True)
    headed = headed.reshape(batch_size, spans_here, SPAN, 3, heads_here, HD)
    query_rows = headed[:, :, :, 0]
    key_rows = headed[:, :, :, 1]
    value_rows = headed[:, :, :, 2]
    key_means = jnp.mean(key_rows, axis=2, dtype=jnp.float32).astype(jnp.bfloat16)
    value_means = jnp.mean(value_rows, axis=2, dtype=jnp.float32).astype(jnp.bfloat16)
    key_all, value_all = (
        lax.all_gather(key_means, "shard", axis=1, tiled=True),
        lax.all_gather(value_means, "shard", axis=1, tiled=True),
    )
    causal = span_place[:, None] >= span_place[None, :]
    global_span = shard_place * spans_here + jnp.arange(spans_here)
    earlier = global_span[:, None] > jnp.arange(spans_all)[None, :]
    mixed_heads, log_total, local_weights, summary_weights = attend(
        query_rows, key_rows, value_rows, key_all, value_all, causal, earlier
    )
    attended = mixed_heads.astype(jnp.bfloat16).reshape(batch_size, group_len, head_width)
    attended = lax.all_to_all(attended, "seq", split_axis=1, concat_axis=2, tiled=True)
    attended_rows = attended.reshape(row_count, model_width)
    middle = (
        flat_tokens
        + jnp.dot(attended_rows, out_full, preferred_element_type=jnp.float32)
        + out_shift.astype(jnp.float32)
    )
    second = layer_norm(middle, gain_two.astype(jnp.float32), bias_two.astype(jnp.float32)).astype(
        jnp.bfloat16
    )
    before = jnp.dot(second, up_full, preferred_element_type=jnp.float32) + up_shift.astype(
        jnp.float32
    )
    hidden = gelu_exact(before).astype(jnp.bfloat16)
    block_out = (
        middle
        + jnp.dot(hidden, down_full, preferred_element_type=jnp.float32)
        + down_shift.astype(jnp.float32)
    )
    block_out = block_out.astype(jnp.bfloat16).reshape(batch_size, local_len, model_width)
    incoming = cotangent.reshape(row_count, model_width)
    grad_down = contract_rows(hidden, incoming)
    grad_down_shift = jnp.sum(incoming, axis=0, dtype=jnp.float32)
    grad_hidden = times_transpose(incoming, down_full)
    gelu_value, gelu_pull = jax.vjp(gelu_exact, before)
    grad_before = gelu_pull(grad_hidden)[0].astype(jnp.bfloat16)
    grad_up = contract_rows(second, grad_before)
    grad_up_shift = jnp.sum(grad_before, axis=0, dtype=jnp.float32)
    grad_second = times_transpose(grad_before, up_full)
    norm_value, norm_pull = jax.vjp(
        layer_norm, middle, gain_two.astype(jnp.float32), bias_two.astype(jnp.float32)
    )
    grad_middle_norm, grad_gain_two, grad_bias_two = norm_pull(grad_second)
    grad_middle = incoming.astype(jnp.float32) + grad_middle_norm
    grad_branch = grad_middle.astype(jnp.bfloat16)
    grad_out = contract_rows(attended_rows, grad_branch)
    grad_out_shift = jnp.sum(grad_branch, axis=0, dtype=jnp.float32)
    grad_attended = times_transpose(grad_branch, out_full).astype(jnp.bfloat16)
    grad_attended = grad_attended.reshape(batch_size, local_len, seq_count, head_width)
    grad_headed = lax.all_to_all(grad_attended, "seq", split_axis=2, concat_axis=1, tiled=True)
    grad_mixed = grad_headed.reshape(batch_size, spans_here, SPAN, heads_here, HD)
    grad_query, grad_key, grad_value, grad_key_all, grad_value_all = attend_back(
        grad_mixed,
        query_rows,
        key_rows,
        value_rows,
        key_all,
        value_all,
        causal,
        earlier,
        log_total,
        local_weights,
        summary_weights,
    )
    grad_key_means, grad_value_means = (
        lax.psum_scatter(
            grad_key_all.astype(jnp.bfloat16), "shard", scatter_dimension=1, tiled=True
        ).astype(jnp.float32),
        lax.psum_scatter(
            grad_value_all.astype(jnp.bfloat16), "shard", scatter_dimension=1, tiled=True
        ).astype(jnp.float32),
    )
    grad_key = grad_key + grad_key_means[:, :, None] / SPAN
    grad_value = grad_value + grad_value_means[:, :, None] / SPAN
    grad_packed = jnp.stack([grad_query, grad_key, grad_value], axis=3).astype(jnp.bfloat16)
    grad_packed = grad_packed.reshape(batch_size, group_len, 3, 1, head_width)
    grad_packed = lax.all_to_all(grad_packed, "seq", split_axis=1, concat_axis=3, tiled=True)
    grad_packed = grad_packed.reshape(row_count, 3 * model_width)
    grad_qkv = contract_rows(normed, grad_packed)
    grad_normed = times_transpose(grad_packed, qkv_full)
    first_value, first_pull = jax.vjp(
        layer_norm, flat_tokens, gain_one.astype(jnp.float32), bias_one.astype(jnp.float32)
    )
    grad_flat_norm, grad_gain_one, grad_bias_one = first_pull(grad_normed)
    grad_tokens = (grad_middle + grad_flat_norm).reshape(batch_size, local_len, model_width)
    all_grads = (
        grad_gain_one,
        grad_bias_one,
        grad_qkv,
        grad_out,
        grad_out_shift,
        grad_gain_two,
        grad_bias_two,
        grad_up,
        grad_up_shift,
        grad_down,
        grad_down_shift,
    )
    owned_grads = (
        lax.psum_scatter(
            all_grads[0].astype(jnp.bfloat16), "shard", scatter_dimension=0, tiled=True
        ).astype(jnp.float32),
        lax.psum_scatter(
            all_grads[1].astype(jnp.bfloat16), "shard", scatter_dimension=0, tiled=True
        ).astype(jnp.float32),
        lax.psum_scatter(
            all_grads[2].astype(jnp.bfloat16), "shard", scatter_dimension=0, tiled=True
        ).astype(jnp.float32),
        lax.psum_scatter(
            all_grads[3].astype(jnp.bfloat16), "shard", scatter_dimension=0, tiled=True
        ).astype(jnp.float32),
        lax.psum_scatter(
            all_grads[4].astype(jnp.bfloat16), "shard", scatter_dimension=0, tiled=True
        ).astype(jnp.float32),
        lax.psum_scatter(
            all_grads[5].astype(jnp.bfloat16), "shard", scatter_dimension=0, tiled=True
        ).astype(jnp.float32),
        lax.psum_scatter(
            all_grads[6].astype(jnp.bfloat16), "shard", scatter_dimension=0, tiled=True
        ).astype(jnp.float32),
        lax.psum_scatter(
            all_grads[7].astype(jnp.bfloat16), "shard", scatter_dimension=0, tiled=True
        ).astype(jnp.float32),
        lax.psum_scatter(
            all_grads[8].astype(jnp.bfloat16), "shard", scatter_dimension=0, tiled=True
        ).astype(jnp.float32),
        lax.psum_scatter(
            all_grads[9].astype(jnp.bfloat16), "shard", scatter_dimension=0, tiled=True
        ).astype(jnp.float32),
        lax.psum_scatter(
            all_grads[10].astype(jnp.bfloat16), "shard", scatter_dimension=0, tiled=True
        ).astype(jnp.float32),
    )
    owned_grads = (
        lax.psum(owned_grads[0].astype(jnp.bfloat16), "seq").astype(jnp.float32),
        lax.psum(owned_grads[1].astype(jnp.bfloat16), "seq").astype(jnp.float32),
        lax.psum(owned_grads[2].astype(jnp.bfloat16), "seq").astype(jnp.float32),
        lax.psum(owned_grads[3].astype(jnp.bfloat16), "seq").astype(jnp.float32),
        lax.psum(owned_grads[4].astype(jnp.bfloat16), "seq").astype(jnp.float32),
        lax.psum(owned_grads[5].astype(jnp.bfloat16), "seq").astype(jnp.float32),
        lax.psum(owned_grads[6].astype(jnp.bfloat16), "seq").astype(jnp.float32),
        lax.psum(owned_grads[7].astype(jnp.bfloat16), "seq").astype(jnp.float32),
        lax.psum(owned_grads[8].astype(jnp.bfloat16), "seq").astype(jnp.float32),
        lax.psum(owned_grads[9].astype(jnp.bfloat16), "seq").astype(jnp.float32),
        lax.psum(owned_grads[10].astype(jnp.bfloat16), "seq").astype(jnp.float32),
    )
    return (
        block_out,
        grad_tokens,
        owned_grads[0],
        owned_grads[1],
        owned_grads[2],
        owned_grads[3],
        owned_grads[4],
        owned_grads[5],
        owned_grads[6],
        owned_grads[7],
        owned_grads[8],
        owned_grads[9],
        owned_grads[10],
    )


def local(tokens, *rest):
    whole_spans = tokens.shape[1] % SPAN == 0
    if whole_spans and lax.axis_size("shard") == 8 and lax.axis_size("seq") == 4:
        return local_block(tokens, *rest)
    return local_general(tokens, *rest)


def solution(mesh):
    return jax.shard_map(
        local,
        mesh=mesh,
        in_specs=(
            P(None, ("shard", "seq"), None),
            P("shard"),
            P("shard"),
            P("shard", None),
            P("shard", None),
            P("shard"),
            P("shard"),
            P("shard"),
            P("shard", None),
            P("shard"),
            P("shard", None),
            P("shard"),
            P(None, ("shard", "seq"), None),
        ),
        out_specs=(
            P(None, ("shard", "seq"), None),
            P(None, ("shard", "seq"), None),
            P("shard"),
            P("shard"),
            P("shard", None),
            P("shard", None),
            P("shard"),
            P("shard"),
            P("shard"),
            P("shard", None),
            P("shard"),
            P("shard", None),
            P("shard"),
        ),
        check_vma=False,
    )
```

```python
import functools
import math

import jax
import jax.numpy as jnp
from jax import lax
from jax.experimental import pallas as pl
from jax.experimental.pallas import tpu as pltpu
from jax.sharding import PartitionSpec as P

H = 8
HD = 64
SPAN = 128


epsilon = 1e-05
MESH = pl.DeviceIdType.MESH
BF = jnp.bfloat16
F32 = jnp.float32


def dot(left, right, left_dim, right_dim):
    return lax.dot_general(
        left, right, (((left_dim,), (right_dim,)), ((), ())), preferred_element_type=F32
    )


def rows_of(index, count):
    if isinstance(index, int):
        return pl.ds(index * count, count)
    return pl.ds(pl.multiple_of(index * count, count), count)


def norm_stats(values):
    center = values - jnp.mean(values, axis=-1, keepdims=True)
    inverse = lax.rsqrt(jnp.mean(center * center, axis=-1, keepdims=True) + epsilon)
    return center * inverse, inverse


def norm_back(grad, xhat, inverse, gain):
    scaled = grad * gain
    first = jnp.mean(scaled, axis=-1, keepdims=True)
    second = jnp.mean(scaled * xhat, axis=-1, keepdims=True)
    return inverse * (scaled - first - xhat * second)


QKV, OUT, UP, DOWN = range(4)
D0, D1, U0, U1, GO, QA, Q2, Q3 = range(8)
CHUNKS = 8
ALONG_SEQ = ()
GATHER_STEPS = 12
REDUCE_STEPS = 8


def block_kernel(
    batch,
    shard_count,
    seq_count,
    tok_hbm,
    cot_hbm,
    vec_hbm,
    up_bias_hbm,
    wq_hbm,
    wo_hbm,
    wu_hbm,
    wd_hbm,
    block_out_hbm,
    grad_tok_hbm,
    gt_hbm,
    gs_hbm,
    go_hbm,
    gu_hbm,
    gd_hbm,
    vec_out_hbm,
    vec_refs,
    up_bias_ref,
    vec_total,
    tok,
    cot,
    wq,
    wo,
    wu,
    wd,
    vec_own,
    vec_all,
    xhat1,
    inv1,
    xb_stage,
    xb_all,
    order,
    vfull,
    up_bias,
    normed,
    packed,
    nbar,
    kv_mean,
    probs,
    att,
    middle,
    gmid,
    inv2,
    second,
    xhat2,
    hidden,
    gbefore,
    gatt,
    gbranch,
    gkv,
    gn_send,
    gn_recv,
    gz_send,
    gz_recv,
    gnbar,
    vsum,
    upsum,
    vec_send,
    vec_recv,
    vec_line,
    g_down,
    g_up,
    g_out,
    g_two,
    g_one,
    r1_down,
    r1_up,
    r1_out,
    r1_two,
    r1_one,
    r2_down,
    r2_up,
    r2_out,
    r2_two,
    r2_one,
    r3_down,
    r3_up,
    r3_out,
    r3_two,
    r3_one,
    r4_down,
    r4_up,
    r4_out,
    r4_two,
    r4_one,
    own_down,
    own_up,
    own_out,
    own_two,
    own_one,
    w_send,
    w_recv,
    w_local,
    io_sem,
    small_sem,
    vec_s,
    vec_r,
    xz_s,
    xz_r,
    xs_s,
    xs_r,
    gs_s,
    gs_r,
    gz_s,
    gz_r,
    vo_s,
    vo_r,
    vz_s,
    vz_r,
    red_s,
    red_r,
    out_sem,
):
    rows, width = tok.shape
    ff = up_bias.shape[1]
    total = shard_count * seq_count
    groups = rows // SPAN
    spans_here = groups // batch
    spans_all = spans_here * total
    pairs = H // 2
    lanes = 2 * HD
    ms = lax.axis_index("shard")
    mq = lax.axis_index("seq")
    mt = ms * seq_count + mq
    core = lax.rem(ms, 2)
    yx = ms // 2

    def flip(value, bit):
        return value + bit - 2 * bit * lax.rem(value // bit, 2)

    core_dev = (flip(ms, 1), mq)
    x_dev = (flip(ms, 2), mq)
    y_dev = (flip(ms, 4), mq)

    tok_in = pltpu.make_async_copy(tok_hbm, tok, io_sem.at[0])
    cot_in = pltpu.make_async_copy(cot_hbm, cot, io_sem.at[1])
    vec_in = [
        pltpu.make_async_copy(source, target, small_sem.at[n])
        for n, (source, target) in enumerate(
            zip([*vec_hbm, up_bias_hbm], [*vec_refs, up_bias_ref])
        )
    ]
    tok_in.start()
    for c in vec_in:
        c.start()
    cot_in.start()

    xb_all[...] = jnp.zeros_like(xb_all)
    barrier = pltpu.get_barrier_semaphore()

    shard_peers = [(lax.rem(ms + step, shard_count), mq) for step in range(1, shard_count)]
    seq_peers = [(ms, lax.rem(mq + step, seq_count)) for step in range(1, seq_count)]
    peers = shard_peers + seq_peers
    for peer in peers:
        pl.semaphore_signal(barrier, inc=1, device_id=peer, device_id_type=MESH)

    w_hbm = (wq_hbm, wo_hbm, wu_hbm, wd_hbm)
    w_full = (wq, wo, wu, wd)

    def gather_copies(which):
        full = w_full[which]
        depth = full.shape[0] // shard_count
        half = depth // 2
        base = which * GATHER_STEPS

        def block(owner):
            return full.at[rows_of(owner, depth)]

        def part(owner, side):
            return full.at[pl.ds(pl.multiple_of(owner * depth + side * half, half), half)]

        def own_part(side):
            return w_hbm[which].at[pl.ds(pl.multiple_of(side * half, half), half)]

        x_own, y_own, d_own = flip(ms, 2), flip(ms, 4), flip(flip(ms, 2), 4)
        if which in ALONG_SEQ:
            h = lax.rem(mq, 2)
            a_own = x_own + h * (y_own - x_own)
            b_own = y_own + h * (x_own - y_own)
            a_dev, b_dev, z_dev = (a_own, mq), (b_own, mq), (ms, flip(mq, 1))
            plan = (
                (own_part(h), part(ms, h), a_dev),
                (own_part(1 - h), part(ms, 1 - h), b_dev),
                (own_part(1 - h), part(ms, 1 - h), a_dev),
                (w_hbm[which], block(ms), core_dev),
                (part(a_own, h), part(a_own, h), b_dev),
                (part(a_own, 1 - h), part(a_own, 1 - h), z_dev),
                (block(a_own), block(a_own), core_dev),
                (part(b_own, 1 - h), part(b_own, 1 - h), core_dev),
                (part(d_own, h), part(d_own, h), z_dev),
                (part(d_own, h), part(d_own, h), core_dev),
                (part(b_own, h), part(b_own, h), core_dev),
                (part(d_own, 1 - h), part(d_own, 1 - h), core_dev),
            )
        else:
            plan = (
                (own_part(0), part(ms, 0), x_dev),
                (own_part(1), part(ms, 1), y_dev),
                (own_part(1), part(ms, 1), x_dev),
                (own_part(0), part(ms, 0), y_dev),
                (w_hbm[which], block(ms), core_dev),
                (part(x_own, 0), part(x_own, 0), y_dev),
                (part(y_own, 1), part(y_own, 1), x_dev),
                (block(x_own), block(x_own), core_dev),
                (block(y_own), block(y_own), core_dev),
                (part(d_own, 0), part(d_own, 0), core_dev),
                (part(d_own, 1), part(d_own, 1), core_dev),
            )
        return [
            pltpu.make_async_remote_copy(
                src_ref=src,
                dst_ref=dst,
                send_sem=w_send.at[base + step],
                recv_sem=w_recv.at[base + step],
                device_id=dev,
                device_id_type=MESH,
            )
            for step, (src, dst, dev) in enumerate(plan)
        ]

    w_copies = [gather_copies(which) for which in range(4)]

    def own_copy(which):
        depth = w_full[which].shape[0] // shard_count
        return pltpu.make_async_copy(
            w_hbm[which], w_full[which].at[rows_of(ms, depth)], w_local.at[which]
        )

    def gather_steps(which, *pairs):
        c = w_copies[which]
        for arrived_step, started in pairs:
            if arrived_step is not None:
                c[arrived_step].wait_recv()
            for step in started:
                c[step].start()

    def gather_own_first(which):
        gather_steps(which, (None, (0, 1)))

    def gather_own_second(which):
        gather_steps(which, (None, (2, 3) if which in ALONG_SEQ else (2, 3, 4)))
        own_copy(which).start()

    def gather_forward(which):
        if which in ALONG_SEQ:
            gather_steps(which, (0, (4,)))
        else:
            gather_steps(which, (0, (5,)), (1, (6,)))

    def gather_core(which):
        if which in ALONG_SEQ:
            gather_steps(which, (2, (5, 6)), (1, (7,)))
        else:
            gather_steps(which, (2, (7,)), (3, (8,)))

    def gather_last(which):
        if which in ALONG_SEQ:
            gather_steps(which, (4, (8, 9)))
        else:
            gather_steps(which, (5, (9,)), (6, (10,)))

    def gather_z1(which):
        if which in ALONG_SEQ:
            gather_steps(which, (5, (10,)))

    def gather_z2(which):
        if which in ALONG_SEQ:
            gather_steps(which, (8, (11,)))

    def gather_done(which):
        for step in (3, 6, 7, 9, 10, 11) if which in ALONG_SEQ else (4, 7, 8, 9, 10):
            w_copies[which][step].wait_recv()
        own_copy(which).wait()

    tok_in.wait()

    big = rows // 2

    def first_norm(i, carry):
        at = rows_of(i, big)
        xhat, inverse = norm_stats(tok[at, :].astype(F32))
        xhat1[at, :] = xhat
        inv1[at, :] = inverse
        for u in range(big // SPAN):
            xb_stage[pl.ds(i * (big // SPAN) + u, 1), :] = jnp.mean(
                xhat[u * SPAN : (u + 1) * SPAN], axis=0, keepdims=True
            )
        return carry

    lax.fori_loop(0, rows // big, first_norm, 0)
    half_width = width // 2
    xb_all[mt] = jnp.concatenate(
        [xb_stage[:, :half_width], xb_stage[:, half_width:]], axis=0
    ).astype(BF)

    shard_rows = width // shard_count
    for c in vec_in:
        c.wait()
    for at, ref in enumerate(vec_refs):
        vec_own[at : at + 1, 0:shard_rows] = ref[...].astype(F32)
    vec_own[8 : 8 + up_bias_ref.shape[0], :] = up_bias_ref[...].astype(F32)

    mean_rows = total * groups

    def order_rows():
        new_row = lax.broadcasted_iota(jnp.int32, (mean_rows, mean_rows), 0)
        old_row = lax.broadcasted_iota(jnp.int32, (mean_rows, mean_rows), 1)

        def scaled(value, down_by, up_by):
            quotient = lax.shift_right_logical(value, down_by.bit_length() - 1)
            return lax.shift_left(quotient, up_by.bit_length() - 1)

        wanted = (
            scaled(new_row & (spans_all - 1), spans_here, groups)
            + scaled(new_row, spans_all, spans_here)
            + (new_row & (spans_here - 1))
        )
        order[...] = (old_row == wanted).astype(BF)

    order_rows()
    vsum[...] = jnp.zeros_like(vsum)
    pl.semaphore_wait(barrier, len(peers))

    def remote(source, target, send, recv, device):
        return pltpu.make_async_remote_copy(
            src_ref=source,
            dst_ref=target,
            send_sem=send,
            recv_sem=recv,
            device_id=device,
            device_id_type=MESH,
        )

    vec_copies = [
        remote(vec_own, vec_all.at[ms], vec_s.at[step], vec_r.at[step], peer)
        for step, peer in enumerate(shard_peers)
    ]
    xz_copies = [
        remote(xb_all.at[mt], xb_all.at[mt], xz_s.at[step], xz_r.at[step], peer)
        for step, peer in enumerate(seq_peers)
    ]

    def xb_group(owner):
        return xb_all.at[rows_of(owner, seq_count)]

    def xs_copy(owner, target):
        return remote(
            xb_group(owner), xb_group(owner), xs_s.at[target], xs_r.at[owner], (target, mq)
        )

    up_here = ff // shard_count
    parts = up_here // lanes
    part_cols = shard_count * lanes

    def vec_start():
        for c in vec_copies:
            c.start()
        vec_all[ms] = vec_own[...]

    def xz_start():
        for c in xz_copies:
            c.start()

    def xz_wait():
        for c in xz_copies:
            c.wait_recv()

    def xs_start():
        for target in range(1, shard_count):

            @pl.when(target > ms)
            def _(target=target):
                xs_copy(ms, target).start()

    def xs_wait():
        for owner in range(shard_count - 1):

            @pl.when(owner < ms)
            def _(owner=owner):
                xs_copy(owner, owner).wait_recv()

    def vec_wait():
        for c in vec_copies:
            c.wait_recv()
        low_lane = lax.broadcasted_iota(jnp.int32, (8, lanes), 1) < HD
        for at in range(shard_count // 2):
            even = vec_all[2 * at]
            odd = vec_all[2 * at + 1]
            vfull[:, at * lanes : (at + 1) * lanes] = jnp.where(
                low_lane, even[0:8, :], pltpu.roll(odd[0:8, :], HD, axis=1)
            )
        for owner in range(shard_count):
            piece = vec_all[owner]
            for r in range(up_here // lanes):
                start = r * part_cols + owner * lanes
                up_bias[0:1, start : start + lanes] = piece[8 + r : 9 + r, :]

    def vector(n):
        return vfull[n : n + 1, :]

    def project(n):
        if n == 0:
            normed[...] = (xhat1[...] * vector(0) + vector(1)).astype(BF)
        packed[:, n * width : (n + 1) * width] = dot(
            normed[...], wq[:, n * width : (n + 1) * width], 1, 0
        ).astype(BF)

    def span_means():
        arrived = xb_all[...].astype(F32)
        arrived = jnp.concatenate([arrived[:, 0:groups, :], arrived[:, groups:, :]], axis=2)
        arrived = arrived.reshape(mean_rows, width)
        arrived = (arrived * vector(0) + vector(1)).astype(BF)
        nbar[...] = dot(order[...], arrived, 1, 0).astype(BF)
        for n in range(2):
            kv_mean[:, n * width : (n + 1) * width] = dot(
                nbar[...], wq[:, (n + 1) * width : (n + 2) * width], 1, 0
            ).astype(BF)

    factor = HD ** (-0.5)
    keys = SPAN + spans_all

    def head_pair(ref_rows):
        low = lax.broadcasted_iota(jnp.int32, (SPAN, lanes), 1) < HD
        zero = jnp.zeros_like(ref_rows)
        return jnp.concatenate(
            [jnp.where(low, ref_rows, zero), jnp.where(low, zero, ref_rows)], axis=0
        )

    def score_shift(g):
        j = lax.broadcasted_iota(jnp.int32, (SPAN, SPAN), 0)
        i = lax.broadcasted_iota(jnp.int32, (SPAN, SPAN), 1)
        near = jnp.where(j <= i, 0.0, -jnp.inf).astype(F32)
        f = lax.broadcasted_iota(jnp.int32, (spans_all, SPAN), 0)
        here = mt * spans_here + g % spans_here
        far = jnp.where(f < here, math.log(SPAN), -jnp.inf).astype(F32)
        both = jnp.concatenate([near, far], axis=0)
        return jnp.concatenate([both, both], axis=1)

    low_out = lax.broadcasted_iota(jnp.int32, (SPAN, lanes), 1) < HD

    def pair_rows(at, mean_at, part, p):
        lo = p * lanes
        start = part * width + lo
        mean_lo = (part - 1) * width + lo
        return jnp.concatenate(
            [packed[at, start : start + lanes], kv_mean[mean_at, mean_lo : mean_lo + lanes]],
            axis=0,
        )

    four = groups // 2

    def attend(i):
        members = [(i * four + u, p) for u in range(four) for p in range(pairs)]
        shifts = [score_shift(i * four + u) for u in range(four)]
        places = {
            g: (rows_of(g, SPAN), rows_of(g // spans_here, spans_all)) for g, _ in members
        }
        scores = [
            dot(
                pair_rows(*places[g], 1, p),
                head_pair(packed[places[g][0], p * lanes : (p + 1) * lanes] * factor),
                1,
                1,
            )
            for g, p in members
        ]
        weights = []
        for n, (g, p) in enumerate(members):
            shifted = scores[n] + shifts[n // pairs]
            expo = jnp.exp(shifted - jnp.max(shifted, axis=0, keepdims=True))
            total_row = jnp.sum(expo, axis=0, keepdims=True)
            weights.append((expo * (1.0 / total_row)).astype(BF))
            probs[g * pairs + p] = weights[n]
        for n, (g, p) in enumerate(members):
            mixed = dot(weights[n], pair_rows(*places[g], 2, p), 0, 0)
            att[places[g][0], p * lanes : (p + 1) * lanes] = jnp.where(
                low_out, mixed[0:SPAN], mixed[SPAN : 2 * SPAN]
            ).astype(BF)

    def second_norm():
        mid = tok[...].astype(F32) + dot(att[...], wo[...], 1, 0) + vector(2)
        middle[...] = mid
        xhat, inverse = norm_stats(mid)
        xhat2[...] = xhat
        inv2[...] = inverse
        second[...] = (xhat * vector(3) + vector(4)).astype(BF)

    half_owners = shard_count // 2
    sub = half_owners * lanes

    def unit_starts(part, side):
        return [
            (side * half_owners + n) * up_here + part * lanes for n in range(half_owners)
        ]

    def up_tile(part, side):
        return jnp.concatenate(
            [wu[:, a : a + lanes] for a in unit_starts(part, side)], axis=1
        )

    def down_tile(part, side):
        return jnp.concatenate(
            [wd[a : a + lanes, :] for a in unit_starts(part, side)], axis=0
        )

    def columns_of(part, side):
        start = part * part_cols + side * sub
        return slice(start, start + sub)

    every = [(part, side) for part in range(parts) for side in range(2)]

    def gelu_parts(before):
        cdf = 0.5 + 0.5 * lax.erf(before * math.sqrt(0.5))
        density = jnp.exp(before * before * -0.5) * (1.0 / math.sqrt(2.0 * math.pi))
        return before * cdf, cdf + before * density

    def feed_up(part, side):
        cols = columns_of(part, side)
        before = dot(second[...], up_tile(part, side), 1, 0) + up_bias[0:1, cols]
        value, slope = gelu_parts(before)
        hidden[:, cols] = value.astype(BF)
        gbefore[:, cols] = slope.astype(BF)

    def back_down(part, side):
        cols = columns_of(part, side)
        grad = dot(cot[...], down_tile(part, side), 1, 1)
        gbefore[:, cols] = (grad * gbefore[:, cols].astype(F32)).astype(BF)

    def feed_both(part, side):
        cols = columns_of(part, side)
        before = dot(second[...], up_tile(part, side), 1, 0) + up_bias[0:1, cols]
        grad = dot(cot[...], down_tile(part, side), 1, 1)
        value, slope = gelu_parts(before)
        hidden[:, cols] = value.astype(BF)
        gbefore[:, cols] = (grad * slope).astype(BF)

    def chunk(which):
        if which in (D0, D1):
            refs, n = (g_down, r1_down, r2_down, r3_down, r4_down, own_down), which - D0
        elif which in (U0, U1):
            refs, n = (g_up, r1_up, r2_up, r3_up, r4_up, own_up), which - U0
        elif which == GO:
            refs, n = (g_out, r1_out, r2_out, r3_out, r4_out, own_out), 0
        elif which == QA:
            refs, n = (g_two, r1_two, r2_two, r3_two, r4_two, own_two), 0
        else:
            refs, n = (g_one, r1_one, r2_one, r3_one, r4_one, own_one), which - Q2
        return tuple(ref.at[n] for ref in refs)

    here, x_blk, y_blk, d_blk = yx, flip(yx, 1), flip(yx, 2), flip(flip(yx, 1), 2)
    z_dev = (ms, flip(mq, 1))
    z_mid = (ms, seq_count - 1 - mq)

    def reduce_copies(which):
        g, r1, r2, r3, r4, own = chunk(which)
        half = g.shape[2] // 2
        base = which * REDUCE_STEPS
        plan = (
            (g.at[1 - core], r1, core_dev),
            (g.at[core, d_blk, pl.ds(0, half)], r2.at[0], x_dev),
            (g.at[core, d_blk, pl.ds(half, half)], r2.at[1], y_dev),
            (g.at[core, x_blk], r3.at[0], x_dev),
            (g.at[core, y_blk], r3.at[1], y_dev),
            (own, r4.at[0], z_dev),
            (own, r4.at[1], z_mid),
            (own, r4.at[0], z_dev),
        )
        copies = [
            pltpu.make_async_remote_copy(
                src_ref=src,
                dst_ref=dst,
                send_sem=red_s.at[base + step],
                recv_sem=red_r.at[base + step],
                device_id=dev,
                device_id_type=MESH,
            )
            for step, (src, dst, dev) in enumerate(plan)
        ]
        return copies

    r_copies = [reduce_copies(which) for which in range(CHUNKS)]
    edge = jnp.logical_or(mq == 0, mq == seq_count - 1)
    inner = jnp.logical_not(edge)

    def add_rows(target, source):
        target[...] += source[...]

    def reduce_a(which):
        r_copies[which][0].start()

    def reduce_b(which):
        g, r1, r2, r3, r4, own = chunk(which)
        c = r_copies[which]
        c[0].wait_recv()
        add_rows(g.at[core, d_blk], r1.at[d_blk])
        c[1].start()
        c[2].start()
        for blk in (x_blk, y_blk, here):
            add_rows(g.at[core, blk], r1.at[blk])

    def reduce_c(which):
        g, r1, r2, r3, r4, own = chunk(which)
        half = g.shape[2] // 2
        c = r_copies[which]
        c[1].wait_recv()
        add_rows(g.at[core, y_blk, pl.ds(0, half)], r2.at[0])
        c[4].start()
        c[2].wait_recv()
        add_rows(g.at[core, x_blk, pl.ds(half, half)], r2.at[1])
        c[3].start()

    def reduce_d(which):
        g, r1, r2, r3, r4, own = chunk(which)
        c = r_copies[which]
        c[3].wait_recv()
        c[4].wait_recv()
        value = g[core, here].astype(F32) + r3[0].astype(F32) + r3[1].astype(F32)
        own[...] = value.astype(BF)

        @pl.when(edge)
        def _():
            c[5].start()

    def reduce_e(which):
        g, r1, r2, r3, r4, own = chunk(which)
        c = r_copies[which]

        @pl.when(inner)
        def _():
            c[5].wait_recv()
            add_rows(own, r4.at[0])
            c[6].start()

    def emit(which, source):
        target = {
            D0: gd_hbm.at[pl.ds(0, lanes)],
            D1: gd_hbm.at[pl.ds(lanes, lanes)],
            U0: gu_hbm.at[0],
            U1: gu_hbm.at[1],
            GO: go_hbm,
            QA: gt_hbm,
            Q2: gs_hbm.at[0],
            Q3: gs_hbm.at[1],
        }[which]
        return pltpu.make_async_copy(source, target, out_sem.at[which])

    def reduce_f(which):
        g, r1, r2, r3, r4, own = chunk(which)
        c = r_copies[which]

        @pl.when(inner)
        def _():
            c[6].wait_recv()
            c[6].wait_send()
            add_rows(own, r4.at[1])
            c[7].start()
            emit(which, own).start()

    def reduce_g(which):
        g, r1, r2, r3, r4, own = chunk(which)
        c = r_copies[which]

        @pl.when(edge)
        def _():
            c[5].wait_send()
            c[7].wait_recv()
            emit(which, r4.at[0]).start()

        @pl.when(inner)
        def _():
            c[7].wait_send()

        for step in range(5):
            c[step].wait_send()

    def put_rows(target, piece):
        count = piece.shape[0] // shard_count
        for owner in range(shard_count):
            target[owner % 2, owner // 2] = piece[owner * count : (owner + 1) * count]

    def part_of(part):
        return slice(part * part_cols, (part + 1) * part_cols)

    def down_grad(part):
        put_rows(g_down.at[part], dot(hidden[:, part_of(part)], cot[...], 0, 0).astype(BF))

    def up_grad(part):
        cols = part_of(part)
        put_rows(g_up.at[part], dot(second[...], gbefore[:, cols], 0, 0).astype(BF))
        upsum[0:1, cols] = jnp.sum(gbefore[:, cols].astype(F32), axis=0, keepdims=True)

    def back_second(i):
        at = rows_of(i, big)
        up_perm = jnp.concatenate([up_tile(*t) for t in every], axis=1)
        grad = dot(gbefore[at, :], up_perm, 1, 1)
        xhat = xhat2[at, :]
        vsum[3:4, :] += jnp.sum(grad * xhat, axis=0, keepdims=True)
        vsum[4:5, :] += jnp.sum(grad, axis=0, keepdims=True)
        incoming = cot[at, :].astype(F32)
        vsum[5:6, :] += jnp.sum(incoming, axis=0, keepdims=True)
        grad_mid = incoming + norm_back(grad, xhat, inv2[at, :], vector(3))
        gmid[at, :] = grad_mid
        branch = grad_mid.astype(BF)
        gbranch[at, :] = branch
        vsum[2:3, :] += jnp.sum(branch.astype(F32), axis=0, keepdims=True)
        gatt[at, :] = dot(branch, wo[...], 1, 1).astype(BF)

    def out_grad():
        put_rows(g_out.at[0], dot(att[...], gbranch[...], 0, 0).astype(BF))

    low_keys = lax.broadcasted_iota(jnp.int32, (SPAN, lanes), 1) < HD

    def attend_back(p):
        lo = p * lanes
        places = [(rows_of(g, SPAN), rows_of(g // spans_here, spans_all)) for g in range(groups)]
        members = []
        for g in range(groups):
            at, mean_at = places[g]
            go = head_pair(gatt[at, lo : lo + lanes])
            weights = probs[g * pairs + p]
            gw = dot(pair_rows(at, mean_at, 2, p), go, 1, 1)
            gv = dot(weights, go, 1, 0)
            members.append((weights, gw, gv))
        scores = []
        for weights, gw, gv in members:
            prob = weights.astype(F32)
            row_inner = jnp.sum(prob * gw, axis=0, keepdims=True)
            scores.append((prob * (gw - row_inner)).astype(BF))
        far_k, far_v = None, None
        for g in range(groups):
            at, mean_at = places[g]
            gv = members[g][2]
            q = head_pair(packed[at, lo : lo + lanes])
            gq = dot(scores[g], pair_rows(at, mean_at, 1, p), 0, 0)
            gk = dot(scores[g], q, 1, 0) * factor
            gbefore[at, lo : lo + lanes] = (
                jnp.where(low_keys, gq[0:SPAN], gq[SPAN : 2 * SPAN]) * factor
            ).astype(BF)
            gbefore[at, width + lo : width + lo + lanes] = gk[0:SPAN].astype(BF)
            gbefore[at, 2 * width + lo : 2 * width + lo + lanes] = gv[0:SPAN].astype(BF)
            first = g % spans_here == 0
            far_k = gk[SPAN:] if first else far_k + gk[SPAN:]
            far_v = gv[SPAN:] if first else far_v + gv[SPAN:]
            if g % spans_here == spans_here - 1:
                gkv[mean_at, lo : lo + lanes] = far_k.astype(BF)
                gkv[mean_at, width + lo : width + lo + lanes] = far_v.astype(BF)

    def first_grad(lo, count, target):
        grads = [gbefore[:, m * width + lo : m * width + lo + count] for m in range(3)]
        means = [gkv[:, m * width + lo : m * width + lo + count] for m in range(2)]
        local_part = dot(normed[...], jnp.concatenate(grads, axis=1), 0, 0)
        mean_part = dot(nbar[...], jnp.concatenate(means, axis=1), 0, 0)
        piece = jnp.concatenate(
            [local_part[:, 0:count], local_part[:, count:] + mean_part], axis=1
        )
        put_rows(target, piece.astype(BF))

    def mean_grad():
        gmean = dot(gkv[...], wq[:, width : 3 * width], 1, 1).astype(BF)
        gmean = dot(order[...], gmean, 0, 0).reshape(total, groups, width)
        gn_send[...] = jnp.concatenate(
            [gmean[:, :, :half_width], gmean[:, :, half_width:]], axis=1
        ).astype(BF)

    def gs_copy(source, target):
        return remote(
            gn_send.at[rows_of(target, seq_count)],
            gn_recv.at[source],
            gs_s.at[target],
            gs_r.at[source],
            (target, mq),
        )

    def gs_start():
        for target in range(shard_count - 1):

            @pl.when(target < ms)
            def _(target=target):
                gs_copy(ms, target).start()

    def gs_wait():
        gz_send[...] = gn_send[rows_of(ms, seq_count)]
        for source in range(1, shard_count):

            @pl.when(source > ms)
            def _(source=source):
                gs_copy(source, source).wait_recv()
                gz_send[...] += gn_recv[source]

    gz_copies = [
        remote(gz_send.at[peer[1]], gz_recv.at[mq], gz_s.at[step], gz_r.at[step], peer)
        for step, peer in enumerate(seq_peers)
    ]

    def gz_start():
        for c in gz_copies:
            c.start()
        gz_recv[mq] = gz_send[mq]

    def gz_wait():
        for c in gz_copies:
            c.wait_recv()
        gnbar[...] = jnp.sum(gz_recv[...].astype(F32), axis=0)

    bout_out = pltpu.make_async_copy(gbranch, block_out_hbm, io_sem.at[2])

    def out_block(i):
        at = rows_of(i, big)
        down_perm = jnp.concatenate([down_tile(*t) for t in every], axis=0)
        gbranch[at, :] = (
            middle[at, :] + dot(hidden[at, :], down_perm, 1, 0) + vector(5)
        ).astype(BF)
        if i == 1:
            bout_out.start()

    tok_out = pltpu.make_async_copy(gmid, grad_tok_hbm, io_sem.at[3])

    def back_first(i):
        at = rows_of(i, big)
        shares = []
        for u in range(big // SPAN):
            g = i * (big // SPAN) + u
            share = jnp.concatenate(
                [gnbar[g : g + 1, :], gnbar[groups + g : groups + g + 1, :]], axis=1
            ) * (1.0 / SPAN)
            shares.append(jnp.broadcast_to(share, (SPAN, width)))
        grad = dot(gbefore[at, 0 : 3 * width], wq[...], 1, 1) + jnp.concatenate(
            shares, axis=0
        )
        xhat = xhat1[at, :]
        vsum[0:1, :] += jnp.sum(grad * xhat, axis=0, keepdims=True)
        vsum[1:2, :] += jnp.sum(grad, axis=0, keepdims=True)
        gmid[at, :] = gmid[at, :] + norm_back(grad, xhat, inv1[at, :], vector(0))
        if i == 1:
            tok_out.start()

    def vec_build():
        for owner in range(shard_count):
            at = owner // 2
            piece = vsum[:, at * lanes : (at + 1) * lanes]
            if owner % 2 == 1:
                piece = pltpu.roll(piece, HD, axis=1)
            vec_send[owner, 0:8, :] = piece
            vec_send[owner, 8:16, :] = jnp.zeros((8, lanes), F32)
            for r in range(parts):
                start = r * part_cols + owner * lanes
                vec_send[owner, 8 + r : 9 + r, :] = upsum[0:1, start : start + lanes]

    vo_copies = [
        remote(vec_send.at[peer[0]], vec_recv.at[ms], vo_s.at[step], vo_r.at[step], peer)
        for step, peer in enumerate(shard_peers)
    ]
    vz_copies = [
        remote(vec_line.at[mq], vec_line.at[mq], vz_s.at[step], vz_r.at[step], peer)
        for step, peer in enumerate(seq_peers)
    ]

    def vo_start():
        for c in vo_copies:
            c.start()
        vec_recv[ms] = vec_send[ms]

    def vo_wait():
        for c in vo_copies:
            c.wait_recv()
        vec_line[mq] = jnp.sum(vec_recv[...], axis=0)

    def vz_start():
        for c in vz_copies:
            c.start()

    vec_out = pltpu.make_async_copy(vec_total, vec_out_hbm, io_sem.at[4])

    def vz_wait():
        for c in vz_copies:
            c.wait_recv()
        vec_total[...] = jnp.sum(vec_line[...], axis=0)
        vec_out.start()

    cot_in.wait()
    gather_own_first(QKV)
    xz_start()
    gather_own_first(OUT)
    gather_own_second(QKV)
    gather_forward(QKV)
    xz_wait()
    xs_start()
    vec_start()
    gather_core(QKV)
    gather_own_second(OUT)
    gather_own_first(UP)
    gather_last(QKV)
    gather_own_second(UP)
    vec_wait()
    gather_done(QKV)
    gather_forward(OUT)
    xs_wait()
    project(0)
    project(1)
    gather_core(OUT)
    project(2)
    span_means()
    gather_forward(UP)
    gather_own_first(DOWN)
    attend(0)
    gather_own_second(DOWN)
    gather_last(OUT)
    gather_core(UP)
    attend(1)
    gather_done(OUT)
    gather_last(UP)
    second_norm()
    gather_done(UP)
    feed_up(0, 0)
    gather_forward(DOWN)
    feed_up(1, 1)
    feed_up(0, 1)
    gather_core(DOWN)
    down_grad(0)
    reduce_a(D0)
    feed_up(1, 0)
    gather_last(DOWN)
    down_grad(1)
    reduce_b(D0)
    gather_done(DOWN)
    reduce_a(D1)
    back_down(1, 0)
    back_down(1, 1)
    up_grad(1)
    reduce_b(D1)
    reduce_c(D0)
    back_down(0, 1)
    reduce_a(U1)
    back_down(0, 0)
    up_grad(0)
    reduce_a(U0)
    reduce_c(D1)
    back_second(0)
    reduce_b(U1)
    reduce_d(D0)
    reduce_b(U0)
    back_second(1)
    out_grad()
    reduce_a(GO)
    reduce_c(U1)
    attend_back(0)
    reduce_d(D1)
    reduce_b(GO)
    reduce_c(U0)
    attend_back(1)
    first_grad(0, 2 * lanes, g_two.at[0])
    reduce_a(QA)
    attend_back(2)
    reduce_e(D0)
    reduce_c(GO)
    reduce_d(U1)
    attend_back(3)
    reduce_b(QA)
    reduce_e(D1)
    mean_grad()
    gs_start()
    reduce_d(GO)
    reduce_d(U0)
    first_grad(2 * lanes, lanes, g_one.at[0])
    reduce_c(QA)
    reduce_a(Q2)
    reduce_e(U1)
    reduce_f(D0)
    first_grad(3 * lanes, lanes, g_one.at[1])
    reduce_a(Q3)
    reduce_b(Q2)
    reduce_f(D1)
    gs_wait()
    gz_start()
    reduce_e(GO)
    reduce_b(Q3)
    reduce_e(U0)
    reduce_d(QA)
    reduce_c(Q2)
    reduce_f(U1)
    reduce_c(Q3)
    gz_wait()
    back_first(0)
    reduce_f(GO)
    reduce_e(QA)
    reduce_d(Q2)
    reduce_d(Q3)
    reduce_f(U0)
    back_first(1)
    reduce_e(Q2)
    vec_build()
    reduce_g(U1)
    vo_start()
    reduce_e(Q3)
    reduce_f(QA)
    out_block(0)
    reduce_f(Q2)
    reduce_g(D1)
    vo_wait()
    reduce_g(GO)
    reduce_g(D0)
    reduce_g(U0)
    vz_start()
    reduce_f(Q3)
    out_block(1)
    reduce_g(Q2)
    reduce_g(QA)
    vz_wait()
    reduce_g(Q3)

    for target in range(1, shard_count):

        @pl.when(target > ms)
        def _(target=target):
            xs_copy(ms, target).wait_send()

    for target in range(shard_count - 1):

        @pl.when(target < ms)
        def _(target=target):
            gs_copy(ms, target).wait_send()

    for c in vec_copies + xz_copies + gz_copies + vo_copies + vz_copies:
        c.wait_send()
    for which in range(4):
        for c in w_copies[which]:
            c.wait_send()
    for which in range(CHUNKS):
        emit(which, chunk(which)[5]).wait()
    bout_out.wait()
    tok_out.wait()
    vec_out.wait()


def finish_kernel(*refs):
    raw, outs, vec_outs = refs[0:8], refs[8:14], refs[14:21]
    low_refs, high_refs, vec, small = refs[21:28], refs[28:32], refs[32], refs[33:40]
    in_sem, out_sem = refs[40:42]
    order = (5, 6, 4, 0, 1, 2, 3)
    loads = [pltpu.make_async_copy(raw[n], low_refs[n], in_sem.at[n]) for n in range(7)]
    vec_load = pltpu.make_async_copy(raw[7], vec, in_sem.at[7])
    vec_load.start()
    for n in order:
        loads[n].start()
    vec_load.wait()
    stores = []
    for n in range(7):
        if n < 6:
            small[n][...] = vec[n : n + 1, 0 : small[n].shape[1]]
        else:
            small[n][...] = vec[8 : 8 + small[n].shape[0], :]
        stores.append(pltpu.make_async_copy(small[n], vec_outs[n], out_sem.at[6 + n]))
        stores[n].start()
    lanes = 2 * HD

    def store(ready, at):
        stores.append(pltpu.make_async_copy(ready, outs[at], out_sem.at[at]))
        stores[-1].start()

    for n in order:
        loads[n].wait()
        low = low_refs[n]
        if n < 2:
            store(low, n)
        elif n == 2:
            for part in range(3):
                start = part * 4 * lanes
                high_refs[0][:, start : start + 2 * lanes] = low[
                    :, part * 2 * lanes : (part + 1) * 2 * lanes
                ].astype(F32)
        elif n == 3:
            for part in range(3):
                for one in range(2):
                    start = (part * 4 + 2 + one) * lanes
                    high_refs[0][:, start : start + lanes] = low[
                        one, :, part * lanes : (part + 1) * lanes
                    ].astype(F32)
            store(high_refs[0], 2)
        elif n == 5:
            high = high_refs[2]
            part_count, _, columns = low.shape
            for part in range(part_count):
                for owner in range(columns // lanes):
                    start = (owner * part_count + part) * lanes
                    high[:, start : start + lanes] = low[
                        part, :, owner * lanes : (owner + 1) * lanes
                    ].astype(F32)
            store(high, 4)
        else:
            high = high_refs[n - 3]
            high[...] = low[...].astype(F32)
            store(high, n - 1)
    for c in stores:
        c.wait()


def local_block(
    tokens,
    ln1_gain,
    ln1_bias,
    qkv_weight,
    out_weight,
    out_bias,
    ln2_gain,
    ln2_bias,
    up_weight,
    up_bias,
    down_weight,
    down_bias,
    cotangent,
):
    seq_count = lax.axis_size("seq")
    shard_count = lax.axis_size("shard")
    total = seq_count * shard_count
    batch, local_len, width = tokens.shape
    rows = batch * local_len
    groups = rows // SPAN
    spans_all = local_len // SPAN * total
    keys = SPAN + spans_all
    ff = up_weight.shape[1]
    lanes = 2 * HD
    shard_rows = width // shard_count
    down_rows = ff // shard_count
    hbm = pl.BlockSpec(memory_space=pl.ANY)
    dma = pltpu.SemaphoreType.DMA
    half_yx = shard_count // 2

    def grads(count, columns, lead=()):
        half = count // 2
        return (
            pltpu.VMEM(lead + (2, half_yx, count, columns), BF),
            pltpu.VMEM(lead + (half_yx, count, columns), BF),
            pltpu.VMEM(lead + (2, half, columns), BF),
            pltpu.VMEM(lead + (2, count, columns), BF),
            pltpu.VMEM(lead + (2, count, columns), BF),
            pltpu.VMEM(lead + (count, columns), BF),
        )

    parts = down_rows // lanes
    part_cols = ff // parts
    down_bufs = grads(lanes, width, (parts,))
    up_bufs = grads(shard_rows, part_cols, (parts,))
    out_bufs = grads(shard_rows, width, (1,))
    two_bufs = grads(shard_rows, 6 * lanes, (1,))
    one_bufs = grads(shard_rows, 3 * lanes, (2,))
    grad_bufs = [
        buf
        for five in zip(down_bufs, up_bufs, out_bufs, two_bufs, one_bufs)
        for buf in five
    ]
    scratch = [
        [pltpu.VMEM((1, shard_rows), BF)] * 6,
        pltpu.VMEM((down_rows // lanes, lanes), BF),
        pltpu.VMEM((16, lanes), F32),
        pltpu.VMEM((rows, width), BF),
        pltpu.VMEM((rows, width), BF),
        pltpu.VMEM((width, 3 * width), BF),
        pltpu.VMEM((width, width), BF),
        pltpu.VMEM((width, ff), BF),
        pltpu.VMEM((ff, width), BF),
        pltpu.VMEM((16, lanes), F32),
        pltpu.VMEM((shard_count, 16, lanes), F32),
        pltpu.VMEM((rows, width), F32),
        pltpu.VMEM((rows, 1), F32),
        pltpu.VMEM((groups, width), F32),
        pltpu.VMEM((total, 2 * groups, width // 2), BF),
        pltpu.VMEM((batch * spans_all, batch * spans_all), BF),
        pltpu.VMEM((8, width), F32),
        pltpu.VMEM((8, ff), F32),
        pltpu.VMEM((rows, width), BF),
        pltpu.VMEM((rows, 3 * width), BF),
        pltpu.VMEM((batch * spans_all, width), BF),
        pltpu.VMEM((batch * spans_all, 2 * width), BF),
        pltpu.VMEM((groups * H // 2, keys, 2 * SPAN), BF),
        pltpu.VMEM((rows, width), BF),
        pltpu.VMEM((rows, width), F32),
        pltpu.VMEM((rows, width), F32),
        pltpu.VMEM((rows, 1), F32),
        pltpu.VMEM((rows, width), BF),
        pltpu.VMEM((rows, width), F32),
        pltpu.VMEM((rows, ff), BF),
        pltpu.VMEM((rows, ff), BF),
        pltpu.VMEM((rows, width), BF),
        pltpu.VMEM((rows, width), BF),
        pltpu.VMEM((batch * spans_all, 2 * width), BF),
        pltpu.VMEM((total, 2 * groups, width // 2), BF),
        pltpu.VMEM((shard_count, seq_count, 2 * groups, width // 2), BF),
        pltpu.VMEM((seq_count, 2 * groups, width // 2), BF),
        pltpu.VMEM((seq_count, 2 * groups, width // 2), BF),
        pltpu.VMEM((2 * groups, width // 2), F32),
        pltpu.VMEM((8, width), F32),
        pltpu.VMEM((8, ff), F32),
        pltpu.VMEM((shard_count, 16, lanes), F32),
        pltpu.VMEM((shard_count, 16, lanes), F32),
        pltpu.VMEM((seq_count, 16, lanes), F32),
        *grad_bufs,
        dma((4 * GATHER_STEPS,)),
        dma((4 * GATHER_STEPS,)),
        dma((4,)),
        dma((5,)),
        dma((7,)),
        dma((shard_count,)),
        dma((shard_count,)),
        dma((seq_count,)),
        dma((seq_count,)),
        dma((shard_count,)),
        dma((shard_count,)),
        dma((shard_count,)),
        dma((shard_count,)),
        dma((seq_count,)),
        dma((seq_count,)),
        dma((shard_count,)),
        dma((shard_count,)),
        dma((seq_count,)),
        dma((seq_count,)),
        dma((CHUNKS * REDUCE_STEPS,)),
        dma((CHUNKS * REDUCE_STEPS,)),
        dma((CHUNKS,)),
    ]
    vectors = [
        v.reshape(1, shard_rows)
        for v in (ln1_gain, ln1_bias, out_bias, ln2_gain, ln2_bias, down_bias)
    ]
    raw = pl.pallas_call(
        functools.partial(block_kernel, batch, shard_count, seq_count),
        out_shape=(
            jax.ShapeDtypeStruct((rows, width), BF),
            jax.ShapeDtypeStruct((rows, width), F32),
            jax.ShapeDtypeStruct((shard_rows, 6 * lanes), BF),
            jax.ShapeDtypeStruct((2, shard_rows, 3 * lanes), BF),
            jax.ShapeDtypeStruct((shard_rows, width), BF),
            jax.ShapeDtypeStruct((parts, shard_rows, part_cols), BF),
            jax.ShapeDtypeStruct((down_rows, width), BF),
            jax.ShapeDtypeStruct((16, lanes), F32),
        ),
        in_specs=[hbm, hbm, [hbm] * 6, hbm, hbm, hbm, hbm, hbm],
        out_specs=(hbm,) * 8,
        scratch_shapes=scratch,
        compiler_params=pltpu.CompilerParams(
            collective_id=0, has_side_effects=True, vmem_limit_bytes=63 * 2**20
        ),
        name="block",
    )(
        tokens.reshape(rows, width),
        cotangent.reshape(rows, width),
        vectors,
        up_bias.reshape(-1, lanes),
        qkv_weight,
        out_weight,
        up_weight,
        down_weight,
    )
    low_shapes = [
        (shard_rows, 6 * lanes),
        (2, shard_rows, 3 * lanes),
        (shard_rows, width),
        (parts, shard_rows, part_cols),
        (down_rows, width),
    ]
    high_shapes = [
        (shard_rows, 3 * width),
        (shard_rows, width),
        (shard_rows, ff),
        (down_rows, width),
    ]
    done = pl.pallas_call(
        finish_kernel,
        out_shape=(
            jax.ShapeDtypeStruct((rows, width), BF),
            jax.ShapeDtypeStruct((rows, width), F32),
            *(jax.ShapeDtypeStruct(shape, F32) for shape in high_shapes),
            *(jax.ShapeDtypeStruct((1, shard_rows), F32) for _ in range(6)),
            jax.ShapeDtypeStruct((down_rows // lanes, lanes), F32),
        ),
        in_specs=[hbm] * 8,
        out_specs=(hbm,) * 13,
        scratch_shapes=[
            pltpu.VMEM((rows, width), BF),
            pltpu.VMEM((rows, width), F32),
            *(pltpu.VMEM(shape, BF) for shape in low_shapes),
            *(pltpu.VMEM(shape, F32) for shape in high_shapes),
            pltpu.VMEM((16, lanes), F32),
            *(pltpu.VMEM((1, shard_rows), F32) for _ in range(6)),
            pltpu.VMEM((down_rows // lanes, lanes), F32),
            dma((8,)),
            dma((13,)),
        ],
        compiler_params=pltpu.CompilerParams(vmem_limit_bytes=62 * 2**20),
        name="finish",
    )(*raw)
    block_out, grad_tokens, g_qkv, g_out, g_up, g_down = done[0:6]
    vec_grads = [v.reshape(shard_rows) for v in done[6:12]]
    return (
        block_out.reshape(tokens.shape),
        grad_tokens.reshape(tokens.shape),
        vec_grads[0],
        vec_grads[1],
        g_qkv,
        g_out,
        vec_grads[2],
        vec_grads[3],
        vec_grads[4],
        g_up,
        done[12].reshape(down_rows),
        g_down,
        vec_grads[5],
    )


def layer_norm(values, norm_gain, norm_shift):
    center = values - jnp.mean(values, axis=-1, keepdims=True)
    spread = jnp.mean(center * center, axis=-1, keepdims=True)
    return center * lax.rsqrt(spread + epsilon) * norm_gain + norm_shift


def gelu_exact(values):
    return jax.nn.gelu(values, approximate=False)


def contract_rows(left_matrix, right_matrix):
    return lax.dot_general(
        left_matrix, right_matrix, (((0,), (0,)), ((), ())), preferred_element_type=jnp.float32
    )


def times_transpose(left_matrix, right_matrix):
    return lax.dot_general(
        left_matrix, right_matrix, (((1,), (1,)), ((), ())), preferred_element_type=jnp.float32
    )


def joint_scores(query_rows, key_rows, key_all, causal, earlier):
    factor = HD ** (-0.5)
    local_part = factor * jnp.einsum(
        "bjihd,bjkhd->bjhik", query_rows, key_rows, preferred_element_type=jnp.float32
    )
    summary = factor * jnp.einsum(
        "bjihd,bfhd->bjhif", query_rows, key_all, preferred_element_type=jnp.float32
    ) + math.log(SPAN)
    local_part = jnp.where(causal[None, None, None], local_part, -jnp.inf)
    summary = jnp.where(earlier[None, :, None, None, :], summary, -jnp.inf)
    return (local_part, summary)


def attend(query_rows, key_rows, value_rows, key_all, value_all, causal, earlier):
    local_part, summary = joint_scores(query_rows, key_rows, key_all, causal, earlier)
    row_max = jnp.maximum(jnp.max(local_part, axis=-1), jnp.max(summary, axis=-1))
    local_exp = jnp.exp(local_part - row_max[..., None])
    summary_exp = jnp.exp(summary - row_max[..., None])
    row_total = jnp.sum(local_exp, axis=-1) + jnp.sum(summary_exp, axis=-1)
    log_total = row_max + jnp.log(row_total)
    local_weights = (local_exp / row_total[..., None]).astype(jnp.bfloat16)
    summary_weights = (summary_exp / row_total[..., None]).astype(jnp.bfloat16)
    mixed_heads = jnp.einsum(
        "bjhik,bjkhd->bjihd", local_weights, value_rows, preferred_element_type=jnp.float32
    )
    mixed_heads = mixed_heads + jnp.einsum(
        "bjhif,bfhd->bjihd", summary_weights, value_all, preferred_element_type=jnp.float32
    )
    return (mixed_heads, log_total, local_weights, summary_weights)


def attend_back(
    grad_mixed,
    query_rows,
    key_rows,
    value_rows,
    key_all,
    value_all,
    causal,
    earlier,
    log_total,
    local_weights,
    summary_weights,
):
    factor = HD ** (-0.5)
    local_part, summary = joint_scores(query_rows, key_rows, key_all, causal, earlier)
    local_prob = jnp.exp(local_part - log_total[..., None])
    summary_prob = jnp.exp(summary - log_total[..., None])
    grad_local_w = jnp.einsum(
        "bjihd,bjkhd->bjhik", grad_mixed, value_rows, preferred_element_type=jnp.float32
    )
    grad_summary_w = jnp.einsum(
        "bjihd,bfhd->bjhif", grad_mixed, value_all, preferred_element_type=jnp.float32
    )
    row_inner = jnp.sum(local_prob * grad_local_w, axis=-1) + jnp.sum(
        summary_prob * grad_summary_w, axis=-1
    )
    grad_local = (local_prob * (grad_local_w - row_inner[..., None])).astype(jnp.bfloat16)
    grad_summary = (summary_prob * (grad_summary_w - row_inner[..., None])).astype(jnp.bfloat16)
    grad_query = jnp.einsum(
        "bjhik,bjkhd->bjihd", grad_local, key_rows, preferred_element_type=jnp.float32
    )
    grad_query = factor * (
        grad_query
        + jnp.einsum("bjhif,bfhd->bjihd", grad_summary, key_all, preferred_element_type=jnp.float32)
    )
    grad_key = factor * jnp.einsum(
        "bjhik,bjihd->bjkhd", grad_local, query_rows, preferred_element_type=jnp.float32
    )
    grad_key_all = factor * jnp.einsum(
        "bjhif,bjihd->bfhd", grad_summary, query_rows, preferred_element_type=jnp.float32
    )
    grad_value = jnp.einsum(
        "bjhik,bjihd->bjkhd", local_weights, grad_mixed, preferred_element_type=jnp.float32
    )
    grad_value_all = jnp.einsum(
        "bjhif,bjihd->bfhd", summary_weights, grad_mixed, preferred_element_type=jnp.float32
    )
    return (grad_query, grad_key, grad_value, grad_key_all, grad_value_all)


def local_general(
    tokens,
    ln1_gain,
    ln1_bias,
    qkv_weight,
    out_weight,
    out_bias,
    ln2_gain,
    ln2_bias,
    up_weight,
    up_bias,
    down_weight,
    down_bias,
    cotangent,
):
    seq_count = lax.axis_size("seq")
    shard_count = lax.axis_size("shard")
    shard_place = lax.axis_index("shard")
    batch_size, local_len, model_width = tokens.shape
    heads_here = H // seq_count
    head_width = heads_here * HD
    group_len = local_len * seq_count
    spans_here = group_len // SPAN
    spans_all = spans_here * shard_count
    row_count = batch_size * local_len
    shards = (
        ln1_gain,
        ln1_bias,
        qkv_weight,
        out_weight,
        out_bias,
        ln2_gain,
        ln2_bias,
        up_weight,
        up_bias,
        down_weight,
        down_bias,
    )
    gathered = (
        lax.all_gather(shards[0], "shard", axis=0, tiled=True),
        lax.all_gather(shards[1], "shard", axis=0, tiled=True),
        lax.all_gather(shards[2], "shard", axis=0, tiled=True),
        lax.all_gather(shards[3], "shard", axis=0, tiled=True),
        lax.all_gather(shards[4], "shard", axis=0, tiled=True),
        lax.all_gather(shards[5], "shard", axis=0, tiled=True),
        lax.all_gather(shards[6], "shard", axis=0, tiled=True),
        lax.all_gather(shards[7], "shard", axis=0, tiled=True),
        lax.all_gather(shards[8], "shard", axis=0, tiled=True),
        lax.all_gather(shards[9], "shard", axis=0, tiled=True),
        lax.all_gather(shards[10], "shard", axis=0, tiled=True),
    )
    (
        gain_one,
        bias_one,
        qkv_full,
        out_full,
        out_shift,
        gain_two,
        bias_two,
        up_full,
        up_shift,
        down_full,
        down_shift,
    ) = gathered
    flat_tokens = tokens.reshape(row_count, model_width).astype(jnp.float32)
    normed = layer_norm(
        flat_tokens, gain_one.astype(jnp.float32), bias_one.astype(jnp.float32)
    ).astype(jnp.bfloat16)
    packed = jnp.dot(normed, qkv_full, preferred_element_type=jnp.float32).astype(jnp.bfloat16)
    span_place = jnp.arange(SPAN)
    packed_heads = packed.reshape(batch_size, local_len, 3, seq_count, head_width)
    headed = lax.all_to_all(packed_heads, "seq", split_axis=3, concat_axis=1, tiled=True)
    headed = headed.reshape(batch_size, spans_here, SPAN, 3, heads_here, HD)
    query_rows = headed[:, :, :, 0]
    key_rows = headed[:, :, :, 1]
    value_rows = headed[:, :, :, 2]
    key_means = jnp.mean(key_rows, axis=2, dtype=jnp.float32).astype(jnp.bfloat16)
    value_means = jnp.mean(value_rows, axis=2, dtype=jnp.float32).astype(jnp.bfloat16)
    key_all, value_all = (
        lax.all_gather(key_means, "shard", axis=1, tiled=True),
        lax.all_gather(value_means, "shard", axis=1, tiled=True),
    )
    causal = span_place[:, None] >= span_place[None, :]
    global_span = shard_place * spans_here + jnp.arange(spans_here)
    earlier = global_span[:, None] > jnp.arange(spans_all)[None, :]
    mixed_heads, log_total, local_weights, summary_weights = attend(
        query_rows, key_rows, value_rows, key_all, value_all, causal, earlier
    )
    attended = mixed_heads.astype(jnp.bfloat16).reshape(batch_size, group_len, head_width)
    attended = lax.all_to_all(attended, "seq", split_axis=1, concat_axis=2, tiled=True)
    attended_rows = attended.reshape(row_count, model_width)
    middle = (
        flat_tokens
        + jnp.dot(attended_rows, out_full, preferred_element_type=jnp.float32)
        + out_shift.astype(jnp.float32)
    )
    second = layer_norm(middle, gain_two.astype(jnp.float32), bias_two.astype(jnp.float32)).astype(
        jnp.bfloat16
    )
    before = jnp.dot(second, up_full, preferred_element_type=jnp.float32) + up_shift.astype(
        jnp.float32
    )
    hidden = gelu_exact(before).astype(jnp.bfloat16)
    block_out = (
        middle
        + jnp.dot(hidden, down_full, preferred_element_type=jnp.float32)
        + down_shift.astype(jnp.float32)
    )
    block_out = block_out.astype(jnp.bfloat16).reshape(batch_size, local_len, model_width)
    incoming = cotangent.reshape(row_count, model_width)
    grad_down = contract_rows(hidden, incoming)
    grad_down_shift = jnp.sum(incoming, axis=0, dtype=jnp.float32)
    grad_hidden = times_transpose(incoming, down_full)
    gelu_value, gelu_pull = jax.vjp(gelu_exact, before)
    grad_before = gelu_pull(grad_hidden)[0].astype(jnp.bfloat16)
    grad_up = contract_rows(second, grad_before)
    grad_up_shift = jnp.sum(grad_before, axis=0, dtype=jnp.float32)
    grad_second = times_transpose(grad_before, up_full)
    norm_value, norm_pull = jax.vjp(
        layer_norm, middle, gain_two.astype(jnp.float32), bias_two.astype(jnp.float32)
    )
    grad_middle_norm, grad_gain_two, grad_bias_two = norm_pull(grad_second)
    grad_middle = incoming.astype(jnp.float32) + grad_middle_norm
    grad_branch = grad_middle.astype(jnp.bfloat16)
    grad_out = contract_rows(attended_rows, grad_branch)
    grad_out_shift = jnp.sum(grad_branch, axis=0, dtype=jnp.float32)
    grad_attended = times_transpose(grad_branch, out_full).astype(jnp.bfloat16)
    grad_attended = grad_attended.reshape(batch_size, local_len, seq_count, head_width)
    grad_headed = lax.all_to_all(grad_attended, "seq", split_axis=2, concat_axis=1, tiled=True)
    grad_mixed = grad_headed.reshape(batch_size, spans_here, SPAN, heads_here, HD)
    grad_query, grad_key, grad_value, grad_key_all, grad_value_all = attend_back(
        grad_mixed,
        query_rows,
        key_rows,
        value_rows,
        key_all,
        value_all,
        causal,
        earlier,
        log_total,
        local_weights,
        summary_weights,
    )
    grad_key_means, grad_value_means = (
        lax.psum_scatter(
            grad_key_all.astype(jnp.bfloat16), "shard", scatter_dimension=1, tiled=True
        ).astype(jnp.float32),
        lax.psum_scatter(
            grad_value_all.astype(jnp.bfloat16), "shard", scatter_dimension=1, tiled=True
        ).astype(jnp.float32),
    )
    grad_key = grad_key + grad_key_means[:, :, None] / SPAN
    grad_value = grad_value + grad_value_means[:, :, None] / SPAN
    grad_packed = jnp.stack([grad_query, grad_key, grad_value], axis=3).astype(jnp.bfloat16)
    grad_packed = grad_packed.reshape(batch_size, group_len, 3, 1, head_width)
    grad_packed = lax.all_to_all(grad_packed, "seq", split_axis=1, concat_axis=3, tiled=True)
    grad_packed = grad_packed.reshape(row_count, 3 * model_width)
    grad_qkv = contract_rows(normed, grad_packed)
    grad_normed = times_transpose(grad_packed, qkv_full)
    first_value, first_pull = jax.vjp(
        layer_norm, flat_tokens, gain_one.astype(jnp.float32), bias_one.astype(jnp.float32)
    )
    grad_flat_norm, grad_gain_one, grad_bias_one = first_pull(grad_normed)
    grad_tokens = (grad_middle + grad_flat_norm).reshape(batch_size, local_len, model_width)
    all_grads = (
        grad_gain_one,
        grad_bias_one,
        grad_qkv,
        grad_out,
        grad_out_shift,
        grad_gain_two,
        grad_bias_two,
        grad_up,
        grad_up_shift,
        grad_down,
        grad_down_shift,
    )
    owned_grads = (
        lax.psum_scatter(
            all_grads[0].astype(jnp.bfloat16), "shard", scatter_dimension=0, tiled=True
        ).astype(jnp.float32),
        lax.psum_scatter(
            all_grads[1].astype(jnp.bfloat16), "shard", scatter_dimension=0, tiled=True
        ).astype(jnp.float32),
        lax.psum_scatter(
            all_grads[2].astype(jnp.bfloat16), "shard", scatter_dimension=0, tiled=True
        ).astype(jnp.float32),
        lax.psum_scatter(
            all_grads[3].astype(jnp.bfloat16), "shard", scatter_dimension=0, tiled=True
        ).astype(jnp.float32),
        lax.psum_scatter(
            all_grads[4].astype(jnp.bfloat16), "shard", scatter_dimension=0, tiled=True
        ).astype(jnp.float32),
        lax.psum_scatter(
            all_grads[5].astype(jnp.bfloat16), "shard", scatter_dimension=0, tiled=True
        ).astype(jnp.float32),
        lax.psum_scatter(
            all_grads[6].astype(jnp.bfloat16), "shard", scatter_dimension=0, tiled=True
        ).astype(jnp.float32),
        lax.psum_scatter(
            all_grads[7].astype(jnp.bfloat16), "shard", scatter_dimension=0, tiled=True
        ).astype(jnp.float32),
        lax.psum_scatter(
            all_grads[8].astype(jnp.bfloat16), "shard", scatter_dimension=0, tiled=True
        ).astype(jnp.float32),
        lax.psum_scatter(
            all_grads[9].astype(jnp.bfloat16), "shard", scatter_dimension=0, tiled=True
        ).astype(jnp.float32),
        lax.psum_scatter(
            all_grads[10].astype(jnp.bfloat16), "shard", scatter_dimension=0, tiled=True
        ).astype(jnp.float32),
    )
    owned_grads = (
        lax.psum(owned_grads[0].astype(jnp.bfloat16), "seq").astype(jnp.float32),
        lax.psum(owned_grads[1].astype(jnp.bfloat16), "seq").astype(jnp.float32),
        lax.psum(owned_grads[2].astype(jnp.bfloat16), "seq").astype(jnp.float32),
        lax.psum(owned_grads[3].astype(jnp.bfloat16), "seq").astype(jnp.float32),
        lax.psum(owned_grads[4].astype(jnp.bfloat16), "seq").astype(jnp.float32),
        lax.psum(owned_grads[5].astype(jnp.bfloat16), "seq").astype(jnp.float32),
        lax.psum(owned_grads[6].astype(jnp.bfloat16), "seq").astype(jnp.float32),
        lax.psum(owned_grads[7].astype(jnp.bfloat16), "seq").astype(jnp.float32),
        lax.psum(owned_grads[8].astype(jnp.bfloat16), "seq").astype(jnp.float32),
        lax.psum(owned_grads[9].astype(jnp.bfloat16), "seq").astype(jnp.float32),
        lax.psum(owned_grads[10].astype(jnp.bfloat16), "seq").astype(jnp.float32),
    )
    return (
        block_out,
        grad_tokens,
        owned_grads[0],
        owned_grads[1],
        owned_grads[2],
        owned_grads[3],
        owned_grads[4],
        owned_grads[5],
        owned_grads[6],
        owned_grads[7],
        owned_grads[8],
        owned_grads[9],
        owned_grads[10],
    )


def local(tokens, *rest):
    whole_spans = tokens.shape[1] % SPAN == 0
    if whole_spans and lax.axis_size("shard") == 8 and lax.axis_size("seq") == 4:
        return local_block(tokens, *rest)
    return local_general(tokens, *rest)


def solution(mesh):
    return jax.shard_map(
        local,
        mesh=mesh,
        in_specs=(
            P(None, ("shard", "seq"), None),
            P("shard"),
            P("shard"),
            P("shard", None),
            P("shard", None),
            P("shard"),
            P("shard"),
            P("shard"),
            P("shard", None),
            P("shard"),
            P("shard", None),
            P("shard"),
            P(None, ("shard", "seq"), None),
        ),
        out_specs=(
            P(None, ("shard", "seq"), None),
            P(None, ("shard", "seq"), None),
            P("shard"),
            P("shard"),
            P("shard", None),
            P("shard", None),
            P("shard"),
            P("shard"),
            P("shard"),
            P("shard", None),
            P("shard"),
            P("shard", None),
            P("shard"),
        ),
        check_vma=False,
    )
```

```python
import functools
import math

import jax
import jax.numpy as jnp
from jax import lax
from jax.experimental import pallas as pl
from jax.experimental.pallas import tpu as pltpu
from jax.sharding import PartitionSpec as P

H = 8
HD = 64
SPAN = 128


epsilon = 1e-05
MESH = pl.DeviceIdType.MESH
BF = jnp.bfloat16
F32 = jnp.float32


def dot(left, right, left_dim, right_dim):
    return lax.dot_general(
        left, right, (((left_dim,), (right_dim,)), ((), ())), preferred_element_type=F32
    )


def rows_of(index, count):
    if isinstance(index, int):
        return pl.ds(index * count, count)
    return pl.ds(pl.multiple_of(index * count, count), count)


def norm_stats(values):
    center = values - jnp.mean(values, axis=-1, keepdims=True)
    inverse = lax.rsqrt(jnp.mean(center * center, axis=-1, keepdims=True) + epsilon)
    return center * inverse, inverse


def norm_back(grad, xhat, inverse, gain):
    scaled = grad * gain
    first = jnp.mean(scaled, axis=-1, keepdims=True)
    second = jnp.mean(scaled * xhat, axis=-1, keepdims=True)
    return inverse * (scaled - first - xhat * second)


QKV, OUT, UP, DOWN = range(4)
D0, D1, U0, U1, GO, QA, Q2, Q3 = range(8)
CHUNKS = 8
ALONG_SEQ = ()
GATHER_STEPS = 12
REDUCE_STEPS = 8


def block_kernel(
    batch,
    shard_count,
    seq_count,
    tok_hbm,
    cot_hbm,
    vec_hbm,
    up_bias_hbm,
    wq_hbm,
    wo_hbm,
    wu_hbm,
    wd_hbm,
    block_out_hbm,
    grad_tok_hbm,
    gt_hbm,
    gs_hbm,
    go_hbm,
    gu_hbm,
    gd_hbm,
    vec_out_hbm,
    vec_refs,
    up_bias_ref,
    vec_total,
    tok,
    cot,
    wq,
    wo,
    wu,
    wd,
    vec_own,
    vec_all,
    xhat1,
    inv1,
    xb_stage,
    xb_all,
    order,
    vfull,
    up_bias,
    normed,
    packed,
    nbar,
    kv_mean,
    probs,
    att,
    middle,
    gmid,
    inv2,
    second,
    xhat2,
    hidden,
    gbefore,
    gatt,
    gbranch,
    gkv,
    gn_send,
    gn_recv,
    gz_send,
    gz_recv,
    gnbar,
    vsum,
    upsum,
    vec_send,
    vec_recv,
    vec_line,
    g_down,
    g_up,
    g_out,
    g_two,
    g_one,
    r1_down,
    r1_up,
    r1_out,
    r1_two,
    r1_one,
    r2_down,
    r2_up,
    r2_out,
    r2_two,
    r2_one,
    r3_down,
    r3_up,
    r3_out,
    r3_two,
    r3_one,
    r4_down,
    r4_up,
    r4_out,
    r4_two,
    r4_one,
    own_down,
    own_up,
    own_out,
    own_two,
    own_one,
    w_send,
    w_recv,
    w_local,
    io_sem,
    small_sem,
    vec_s,
    vec_r,
    xz_s,
    xz_r,
    xs_s,
    xs_r,
    gs_s,
    gs_r,
    gz_s,
    gz_r,
    vo_s,
    vo_r,
    vz_s,
    vz_r,
    red_s,
    red_r,
    out_sem,
):
    rows, width = tok.shape
    ff = up_bias.shape[1]
    total = shard_count * seq_count
    groups = rows // SPAN
    spans_here = groups // batch
    spans_all = spans_here * total
    pairs = H // 2
    lanes = 2 * HD
    ms = lax.axis_index("shard")
    mq = lax.axis_index("seq")
    mt = ms * seq_count + mq
    core = lax.rem(ms, 2)
    yx = ms // 2

    def flip(value, bit):
        return value + bit - 2 * bit * lax.rem(value // bit, 2)

    core_dev = (flip(ms, 1), mq)
    x_dev = (flip(ms, 2), mq)
    y_dev = (flip(ms, 4), mq)

    tok_in = pltpu.make_async_copy(tok_hbm, tok, io_sem.at[0])
    cot_in = pltpu.make_async_copy(cot_hbm, cot, io_sem.at[1])
    vec_in = [
        pltpu.make_async_copy(source, target, small_sem.at[n])
        for n, (source, target) in enumerate(
            zip([*vec_hbm, up_bias_hbm], [*vec_refs, up_bias_ref])
        )
    ]
    tok_in.start()
    for c in vec_in:
        c.start()
    cot_in.start()

    xb_all[...] = jnp.zeros_like(xb_all)
    barrier = pltpu.get_barrier_semaphore()

    shard_peers = [(lax.rem(ms + step, shard_count), mq) for step in range(1, shard_count)]
    seq_peers = [(ms, lax.rem(mq + step, seq_count)) for step in range(1, seq_count)]
    peers = shard_peers + seq_peers
    for peer in peers:
        pl.semaphore_signal(barrier, inc=1, device_id=peer, device_id_type=MESH)

    w_hbm = (wq_hbm, wo_hbm, wu_hbm, wd_hbm)
    w_full = (wq, wo, wu, wd)

    def gather_copies(which):
        full = w_full[which]
        depth = full.shape[0] // shard_count
        half = depth // 2
        base = which * GATHER_STEPS

        def block(owner):
            return full.at[rows_of(owner, depth)]

        def part(owner, side):
            return full.at[pl.ds(pl.multiple_of(owner * depth + side * half, half), half)]

        def own_part(side):
            return w_hbm[which].at[pl.ds(pl.multiple_of(side * half, half), half)]

        x_own, y_own, d_own = flip(ms, 2), flip(ms, 4), flip(flip(ms, 2), 4)
        if which in ALONG_SEQ:
            h = lax.rem(mq, 2)
            a_own = x_own + h * (y_own - x_own)
            b_own = y_own + h * (x_own - y_own)
            a_dev, b_dev, z_dev = (a_own, mq), (b_own, mq), (ms, flip(mq, 1))
            plan = (
                (own_part(h), part(ms, h), a_dev),
                (own_part(1 - h), part(ms, 1 - h), b_dev),
                (own_part(1 - h), part(ms, 1 - h), a_dev),
                (w_hbm[which], block(ms), core_dev),
                (part(a_own, h), part(a_own, h), b_dev),
                (part(a_own, 1 - h), part(a_own, 1 - h), z_dev),
                (block(a_own), block(a_own), core_dev),
                (part(b_own, 1 - h), part(b_own, 1 - h), core_dev),
                (part(d_own, h), part(d_own, h), z_dev),
                (part(d_own, h), part(d_own, h), core_dev),
                (part(b_own, h), part(b_own, h), core_dev),
                (part(d_own, 1 - h), part(d_own, 1 - h), core_dev),
            )
        else:
            plan = (
                (own_part(0), part(ms, 0), x_dev),
                (own_part(1), part(ms, 1), y_dev),
                (own_part(1), part(ms, 1), x_dev),
                (own_part(0), part(ms, 0), y_dev),
                (w_hbm[which], block(ms), core_dev),
                (part(x_own, 0), part(x_own, 0), y_dev),
                (part(y_own, 1), part(y_own, 1), x_dev),
                (block(x_own), block(x_own), core_dev),
                (block(y_own), block(y_own), core_dev),
                (part(d_own, 0), part(d_own, 0), core_dev),
                (part(d_own, 1), part(d_own, 1), core_dev),
            )
        return [
            pltpu.make_async_remote_copy(
                src_ref=src,
                dst_ref=dst,
                send_sem=w_send.at[base + step],
                recv_sem=w_recv.at[base + step],
                device_id=dev,
                device_id_type=MESH,
            )
            for step, (src, dst, dev) in enumerate(plan)
        ]

    w_copies = [gather_copies(which) for which in range(4)]

    def own_copy(which):
        depth = w_full[which].shape[0] // shard_count
        return pltpu.make_async_copy(
            w_hbm[which], w_full[which].at[rows_of(ms, depth)], w_local.at[which]
        )

    def gather_steps(which, *pairs):
        c = w_copies[which]
        for arrived_step, started in pairs:
            if arrived_step is not None:
                c[arrived_step].wait_recv()
            for step in started:
                c[step].start()

    def gather_own_first(which):
        gather_steps(which, (None, (0, 1)))

    def gather_own_second(which):
        gather_steps(which, (None, (2, 3) if which in ALONG_SEQ else (2, 3, 4)))
        own_copy(which).start()

    def gather_forward(which):
        if which in ALONG_SEQ:
            gather_steps(which, (0, (4,)))
        else:
            gather_steps(which, (0, (5,)), (1, (6,)))

    def gather_core(which):
        if which in ALONG_SEQ:
            gather_steps(which, (2, (5, 6)), (1, (7,)))
        else:
            gather_steps(which, (2, (7,)), (3, (8,)))

    def gather_last(which):
        if which in ALONG_SEQ:
            gather_steps(which, (4, (8, 9)))
        else:
            gather_steps(which, (5, (9,)), (6, (10,)))

    def gather_z1(which):
        if which in ALONG_SEQ:
            gather_steps(which, (5, (10,)))

    def gather_z2(which):
        if which in ALONG_SEQ:
            gather_steps(which, (8, (11,)))

    def gather_done(which):
        for step in (3, 6, 7, 9, 10, 11) if which in ALONG_SEQ else (4, 7, 8, 9, 10):
            w_copies[which][step].wait_recv()
        own_copy(which).wait()

    tok_in.wait()

    big = rows // 2

    def first_norm(i, carry):
        at = rows_of(i, big)
        xhat, inverse = norm_stats(tok[at, :].astype(F32))
        xhat1[at, :] = xhat
        inv1[at, :] = inverse
        for u in range(big // SPAN):
            xb_stage[pl.ds(i * (big // SPAN) + u, 1), :] = jnp.mean(
                xhat[u * SPAN : (u + 1) * SPAN], axis=0, keepdims=True
            )
        return carry

    lax.fori_loop(0, rows // big, first_norm, 0)
    half_width = width // 2
    xb_all[mt] = jnp.concatenate(
        [xb_stage[:, :half_width], xb_stage[:, half_width:]], axis=0
    ).astype(BF)

    shard_rows = width // shard_count
    for c in vec_in:
        c.wait()
    for at, ref in enumerate(vec_refs):
        vec_own[at : at + 1, 0:shard_rows] = ref[...].astype(F32)
    vec_own[8 : 8 + up_bias_ref.shape[0], :] = up_bias_ref[...].astype(F32)

    mean_rows = total * groups

    def order_rows():
        new_row = lax.broadcasted_iota(jnp.int32, (mean_rows, mean_rows), 0)
        old_row = lax.broadcasted_iota(jnp.int32, (mean_rows, mean_rows), 1)

        def scaled(value, down_by, up_by):
            quotient = lax.shift_right_logical(value, down_by.bit_length() - 1)
            return lax.shift_left(quotient, up_by.bit_length() - 1)

        wanted = (
            scaled(new_row & (spans_all - 1), spans_here, groups)
            + scaled(new_row, spans_all, spans_here)
            + (new_row & (spans_here - 1))
        )
        order[...] = (old_row == wanted).astype(BF)

    order_rows()
    vsum[...] = jnp.zeros_like(vsum)
    pl.semaphore_wait(barrier, len(peers))

    def remote(source, target, send, recv, device):
        return pltpu.make_async_remote_copy(
            src_ref=source,
            dst_ref=target,
            send_sem=send,
            recv_sem=recv,
            device_id=device,
            device_id_type=MESH,
        )

    vec_copies = [
        remote(vec_own, vec_all.at[ms], vec_s.at[step], vec_r.at[step], peer)
        for step, peer in enumerate(shard_peers)
    ]
    xz_copies = [
        remote(xb_all.at[mt], xb_all.at[mt], xz_s.at[step], xz_r.at[step], peer)
        for step, peer in enumerate(seq_peers)
    ]

    def xb_group(owner):
        return xb_all.at[rows_of(owner, seq_count)]

    def xs_copy(owner, target):
        return remote(
            xb_group(owner), xb_group(owner), xs_s.at[target], xs_r.at[owner], (target, mq)
        )

    up_here = ff // shard_count
    parts = up_here // lanes
    part_cols = shard_count * lanes

    def vec_start():
        for c in vec_copies:
            c.start()
        vec_all[ms] = vec_own[...]

    def xz_start():
        for c in xz_copies:
            c.start()

    def xz_wait():
        for c in xz_copies:
            c.wait_recv()

    def xs_start():
        for target in range(1, shard_count):

            @pl.when(target > ms)
            def _(target=target):
                xs_copy(ms, target).start()

    def xs_wait():
        for owner in range(shard_count - 1):

            @pl.when(owner < ms)
            def _(owner=owner):
                xs_copy(owner, owner).wait_recv()

    def vec_wait():
        for c in vec_copies:
            c.wait_recv()
        low_lane = lax.broadcasted_iota(jnp.int32, (8, lanes), 1) < HD
        for at in range(shard_count // 2):
            even = vec_all[2 * at]
            odd = vec_all[2 * at + 1]
            vfull[:, at * lanes : (at + 1) * lanes] = jnp.where(
                low_lane, even[0:8, :], pltpu.roll(odd[0:8, :], HD, axis=1)
            )
        for owner in range(shard_count):
            piece = vec_all[owner]
            for r in range(up_here // lanes):
                start = r * part_cols + owner * lanes
                up_bias[0:1, start : start + lanes] = piece[8 + r : 9 + r, :]

    def vector(n):
        return vfull[n : n + 1, :]

    def project(n):
        if n == 0:
            normed[...] = (xhat1[...] * vector(0) + vector(1)).astype(BF)
        packed[:, n * width : (n + 1) * width] = dot(
            normed[...], wq[:, n * width : (n + 1) * width], 1, 0
        ).astype(BF)

    def span_means():
        arrived = xb_all[...].astype(F32)
        arrived = jnp.concatenate([arrived[:, 0:groups, :], arrived[:, groups:, :]], axis=2)
        arrived = arrived.reshape(mean_rows, width)
        arrived = (arrived * vector(0) + vector(1)).astype(BF)
        nbar[...] = dot(order[...], arrived, 1, 0).astype(BF)
        for n in range(2):
            kv_mean[:, n * width : (n + 1) * width] = dot(
                nbar[...], wq[:, (n + 1) * width : (n + 2) * width], 1, 0
            ).astype(BF)

    factor = HD ** (-0.5)
    keys = SPAN + spans_all

    def head_pair(ref_rows):
        low = lax.broadcasted_iota(jnp.int32, (SPAN, lanes), 1) < HD
        zero = jnp.zeros_like(ref_rows)
        return jnp.concatenate(
            [jnp.where(low, ref_rows, zero), jnp.where(low, zero, ref_rows)], axis=0
        )

    def score_shift(g):
        j = lax.broadcasted_iota(jnp.int32, (SPAN, SPAN), 0)
        i = lax.broadcasted_iota(jnp.int32, (SPAN, SPAN), 1)
        near = jnp.where(j <= i, 0.0, -jnp.inf).astype(F32)
        f = lax.broadcasted_iota(jnp.int32, (spans_all, SPAN), 0)
        here = mt * spans_here + g % spans_here
        far = jnp.where(f < here, math.log(SPAN), -jnp.inf).astype(F32)
        both = jnp.concatenate([near, far], axis=0)
        return jnp.concatenate([both, both], axis=1)

    low_out = lax.broadcasted_iota(jnp.int32, (SPAN, lanes), 1) < HD

    def pair_rows(at, mean_at, part, p):
        lo = p * lanes
        start = part * width + lo
        mean_lo = (part - 1) * width + lo
        return jnp.concatenate(
            [packed[at, start : start + lanes], kv_mean[mean_at, mean_lo : mean_lo + lanes]],
            axis=0,
        )

    four = groups // 2

    def attend(i):
        members = [(i * four + u, p) for u in range(four) for p in range(pairs)]
        shifts = [score_shift(i * four + u) for u in range(four)]
        places = {
            g: (rows_of(g, SPAN), rows_of(g // spans_here, spans_all)) for g, _ in members
        }
        scores = [
            dot(
                pair_rows(*places[g], 1, p),
                head_pair(packed[places[g][0], p * lanes : (p + 1) * lanes] * factor),
                1,
                1,
            )
            for g, p in members
        ]
        weights = []
        for n, (g, p) in enumerate(members):
            shifted = scores[n] + shifts[n // pairs]
            expo = jnp.exp(shifted - jnp.max(shifted, axis=0, keepdims=True))
            total_row = jnp.sum(expo, axis=0, keepdims=True)
            weights.append((expo * (1.0 / total_row)).astype(BF))
            probs[g * pairs + p] = weights[n]
        for n, (g, p) in enumerate(members):
            mixed = dot(weights[n], pair_rows(*places[g], 2, p), 0, 0)
            att[places[g][0], p * lanes : (p + 1) * lanes] = jnp.where(
                low_out, mixed[0:SPAN], mixed[SPAN : 2 * SPAN]
            ).astype(BF)

    def second_norm():
        mid = tok[...].astype(F32) + dot(att[...], wo[...], 1, 0) + vector(2)
        middle[...] = mid
        xhat, inverse = norm_stats(mid)
        xhat2[...] = xhat
        inv2[...] = inverse
        second[...] = (xhat * vector(3) + vector(4)).astype(BF)

    half_owners = shard_count // 2
    sub = half_owners * lanes

    def unit_starts(part, side):
        return [
            (side * half_owners + n) * up_here + part * lanes for n in range(half_owners)
        ]

    def up_tile(part, side):
        return jnp.concatenate(
            [wu[:, a : a + lanes] for a in unit_starts(part, side)], axis=1
        )

    def down_tile(part, side):
        return jnp.concatenate(
            [wd[a : a + lanes, :] for a in unit_starts(part, side)], axis=0
        )

    def columns_of(part, side):
        start = part * part_cols + side * sub
        return slice(start, start + sub)

    every = [(part, side) for part in range(parts) for side in range(2)]

    def gelu_parts(before):
        cdf = 0.5 + 0.5 * lax.erf(before * math.sqrt(0.5))
        density = jnp.exp(before * before * -0.5) * (1.0 / math.sqrt(2.0 * math.pi))
        return before * cdf, cdf + before * density

    def feed_up(part, side):
        cols = columns_of(part, side)
        before = dot(second[...], up_tile(part, side), 1, 0) + up_bias[0:1, cols]
        value, slope = gelu_parts(before)
        hidden[:, cols] = value.astype(BF)
        gbefore[:, cols] = slope.astype(BF)

    def back_down(part, side):
        cols = columns_of(part, side)
        grad = dot(cot[...], down_tile(part, side), 1, 1)
        gbefore[:, cols] = (grad * gbefore[:, cols].astype(F32)).astype(BF)

    def feed_both(part, side):
        cols = columns_of(part, side)
        before = dot(second[...], up_tile(part, side), 1, 0) + up_bias[0:1, cols]
        grad = dot(cot[...], down_tile(part, side), 1, 1)
        value, slope = gelu_parts(before)
        hidden[:, cols] = value.astype(BF)
        gbefore[:, cols] = (grad * slope).astype(BF)

    def chunk(which):
        if which in (D0, D1):
            refs, n = (g_down, r1_down, r2_down, r3_down, r4_down, own_down), which - D0
        elif which in (U0, U1):
            refs, n = (g_up, r1_up, r2_up, r3_up, r4_up, own_up), which - U0
        elif which == GO:
            refs, n = (g_out, r1_out, r2_out, r3_out, r4_out, own_out), 0
        elif which == QA:
            refs, n = (g_two, r1_two, r2_two, r3_two, r4_two, own_two), 0
        else:
            refs, n = (g_one, r1_one, r2_one, r3_one, r4_one, own_one), which - Q2
        return tuple(ref.at[n] for ref in refs)

    here, x_blk, y_blk, d_blk = yx, flip(yx, 1), flip(yx, 2), flip(flip(yx, 1), 2)
    z_dev = (ms, flip(mq, 1))
    z_mid = (ms, seq_count - 1 - mq)

    def reduce_copies(which):
        g, r1, r2, r3, r4, own = chunk(which)
        half = g.shape[2] // 2
        base = which * REDUCE_STEPS
        plan = (
            (g.at[1 - core], r1, core_dev),
            (g.at[core, d_blk, pl.ds(0, half)], r2.at[0], x_dev),
            (g.at[core, d_blk, pl.ds(half, half)], r2.at[1], y_dev),
            (g.at[core, x_blk], r3.at[0], x_dev),
            (g.at[core, y_blk], r3.at[1], y_dev),
            (own, r4.at[0], z_dev),
            (own, r4.at[1], z_mid),
            (own, r4.at[0], z_dev),
        )
        copies = [
            pltpu.make_async_remote_copy(
                src_ref=src,
                dst_ref=dst,
                send_sem=red_s.at[base + step],
                recv_sem=red_r.at[base + step],
                device_id=dev,
                device_id_type=MESH,
            )
            for step, (src, dst, dev) in enumerate(plan)
        ]
        return copies

    r_copies = [reduce_copies(which) for which in range(CHUNKS)]
    edge = jnp.logical_or(mq == 0, mq == seq_count - 1)
    inner = jnp.logical_not(edge)

    def add_rows(target, source):
        target[...] += source[...]

    def reduce_a(which):
        r_copies[which][0].start()

    def reduce_b(which):
        g, r1, r2, r3, r4, own = chunk(which)
        c = r_copies[which]
        c[0].wait_recv()
        add_rows(g.at[core, d_blk], r1.at[d_blk])
        c[1].start()
        c[2].start()
        for blk in (x_blk, y_blk, here):
            add_rows(g.at[core, blk], r1.at[blk])

    def reduce_c(which):
        g, r1, r2, r3, r4, own = chunk(which)
        half = g.shape[2] // 2
        c = r_copies[which]
        c[1].wait_recv()
        add_rows(g.at[core, y_blk, pl.ds(0, half)], r2.at[0])
        c[4].start()
        c[2].wait_recv()
        add_rows(g.at[core, x_blk, pl.ds(half, half)], r2.at[1])
        c[3].start()

    def reduce_d(which):
        g, r1, r2, r3, r4, own = chunk(which)
        c = r_copies[which]
        c[3].wait_recv()
        c[4].wait_recv()
        value = g[core, here].astype(F32) + r3[0].astype(F32) + r3[1].astype(F32)
        own[...] = value.astype(BF)

        @pl.when(edge)
        def _():
            c[5].start()

    def reduce_e(which):
        g, r1, r2, r3, r4, own = chunk(which)
        c = r_copies[which]

        @pl.when(inner)
        def _():
            c[5].wait_recv()
            add_rows(own, r4.at[0])
            c[6].start()

    def emit(which, source):
        target = {
            D0: gd_hbm.at[pl.ds(0, lanes)],
            D1: gd_hbm.at[pl.ds(lanes, lanes)],
            U0: gu_hbm.at[0],
            U1: gu_hbm.at[1],
            GO: go_hbm,
            QA: gt_hbm,
            Q2: gs_hbm.at[0],
            Q3: gs_hbm.at[1],
        }[which]
        return pltpu.make_async_copy(source, target, out_sem.at[which])

    def reduce_f(which):
        g, r1, r2, r3, r4, own = chunk(which)
        c = r_copies[which]

        @pl.when(inner)
        def _():
            c[6].wait_recv()
            c[6].wait_send()
            add_rows(own, r4.at[1])
            c[7].start()
            emit(which, own).start()

    def reduce_g(which):
        g, r1, r2, r3, r4, own = chunk(which)
        c = r_copies[which]

        @pl.when(edge)
        def _():
            c[5].wait_send()
            c[7].wait_recv()
            emit(which, r4.at[0]).start()

        @pl.when(inner)
        def _():
            c[7].wait_send()

        for step in range(5):
            c[step].wait_send()

    def put_rows(target, piece):
        count = piece.shape[0] // shard_count
        for owner in range(shard_count):
            target[owner % 2, owner // 2] = piece[owner * count : (owner + 1) * count]

    def part_of(part):
        return slice(part * part_cols, (part + 1) * part_cols)

    def down_grad(part):
        put_rows(g_down.at[part], dot(hidden[:, part_of(part)], cot[...], 0, 0).astype(BF))

    def up_grad(part):
        cols = part_of(part)
        put_rows(g_up.at[part], dot(second[...], gbefore[:, cols], 0, 0).astype(BF))
        upsum[0:1, cols] = jnp.sum(gbefore[:, cols].astype(F32), axis=0, keepdims=True)

    def back_second(i):
        at = rows_of(i, big)
        up_perm = jnp.concatenate([up_tile(*t) for t in every], axis=1)
        grad = dot(gbefore[at, :], up_perm, 1, 1)
        xhat = xhat2[at, :]
        vsum[3:4, :] += jnp.sum(grad * xhat, axis=0, keepdims=True)
        vsum[4:5, :] += jnp.sum(grad, axis=0, keepdims=True)
        incoming = cot[at, :].astype(F32)
        vsum[5:6, :] += jnp.sum(incoming, axis=0, keepdims=True)
        grad_mid = incoming + norm_back(grad, xhat, inv2[at, :], vector(3))
        gmid[at, :] = grad_mid
        branch = grad_mid.astype(BF)
        gbranch[at, :] = branch
        vsum[2:3, :] += jnp.sum(branch.astype(F32), axis=0, keepdims=True)
        gatt[at, :] = dot(branch, wo[...], 1, 1).astype(BF)

    def out_grad():
        put_rows(g_out.at[0], dot(att[...], gbranch[...], 0, 0).astype(BF))

    low_keys = lax.broadcasted_iota(jnp.int32, (SPAN, lanes), 1) < HD

    def attend_back(p):
        lo = p * lanes
        places = [(rows_of(g, SPAN), rows_of(g // spans_here, spans_all)) for g in range(groups)]
        members = []
        for g in range(groups):
            at, mean_at = places[g]
            go = head_pair(gatt[at, lo : lo + lanes])
            weights = probs[g * pairs + p]
            gw = dot(pair_rows(at, mean_at, 2, p), go, 1, 1)
            gv = dot(weights, go, 1, 0)
            members.append((weights, gw, gv))
        scores = []
        for weights, gw, gv in members:
            prob = weights.astype(F32)
            row_inner = jnp.sum(prob * gw, axis=0, keepdims=True)
            scores.append((prob * (gw - row_inner)).astype(BF))
        far_k, far_v = None, None
        for g in range(groups):
            at, mean_at = places[g]
            gv = members[g][2]
            q = head_pair(packed[at, lo : lo + lanes])
            gq = dot(scores[g], pair_rows(at, mean_at, 1, p), 0, 0)
            gk = dot(scores[g], q, 1, 0) * factor
            gbefore[at, lo : lo + lanes] = (
                jnp.where(low_keys, gq[0:SPAN], gq[SPAN : 2 * SPAN]) * factor
            ).astype(BF)
            gbefore[at, width + lo : width + lo + lanes] = gk[0:SPAN].astype(BF)
            gbefore[at, 2 * width + lo : 2 * width + lo + lanes] = gv[0:SPAN].astype(BF)
            first = g % spans_here == 0
            far_k = gk[SPAN:] if first else far_k + gk[SPAN:]
            far_v = gv[SPAN:] if first else far_v + gv[SPAN:]
            if g % spans_here == spans_here - 1:
                gkv[mean_at, lo : lo + lanes] = far_k.astype(BF)
                gkv[mean_at, width + lo : width + lo + lanes] = far_v.astype(BF)

    def first_grad(lo, count, target):
        grads = [gbefore[:, m * width + lo : m * width + lo + count] for m in range(3)]
        means = [gkv[:, m * width + lo : m * width + lo + count] for m in range(2)]
        local_part = dot(normed[...], jnp.concatenate(grads, axis=1), 0, 0)
        mean_part = dot(nbar[...], jnp.concatenate(means, axis=1), 0, 0)
        piece = jnp.concatenate(
            [local_part[:, 0:count], local_part[:, count:] + mean_part], axis=1
        )
        put_rows(target, piece.astype(BF))

    def mean_grad():
        gmean = dot(gkv[...], wq[:, width : 3 * width], 1, 1).astype(BF)
        gmean = dot(order[...], gmean, 0, 0).reshape(total, groups, width)
        gn_send[...] = jnp.concatenate(
            [gmean[:, :, :half_width], gmean[:, :, half_width:]], axis=1
        ).astype(BF)

    def gs_copy(source, target):
        return remote(
            gn_send.at[rows_of(target, seq_count)],
            gn_recv.at[source],
            gs_s.at[target],
            gs_r.at[source],
            (target, mq),
        )

    def gs_start():
        for target in range(shard_count - 1):

            @pl.when(target < ms)
            def _(target=target):
                gs_copy(ms, target).start()

    def gs_wait():
        gz_send[...] = gn_send[rows_of(ms, seq_count)]
        for source in range(1, shard_count):

            @pl.when(source > ms)
            def _(source=source):
                gs_copy(source, source).wait_recv()
                gz_send[...] += gn_recv[source]

    gz_copies = [
        remote(gz_send.at[peer[1]], gz_recv.at[mq], gz_s.at[step], gz_r.at[step], peer)
        for step, peer in enumerate(seq_peers)
    ]

    def gz_start():
        for c in gz_copies:
            c.start()
        gz_recv[mq] = gz_send[mq]

    def gz_wait():
        for c in gz_copies:
            c.wait_recv()
        gnbar[...] = jnp.sum(gz_recv[...].astype(F32), axis=0)

    def halves(source, target, first_sem):
        return [
            pltpu.make_async_copy(
                source.at[rows_of(i, big)], target.at[rows_of(i, big)], io_sem.at[first_sem + i]
            )
            for i in range(2)
        ]

    bout_out = halves(gbranch, block_out_hbm, 5)

    def out_block(i):
        at = rows_of(i, big)
        down_perm = jnp.concatenate([down_tile(*t) for t in every], axis=0)
        gbranch[at, :] = (
            middle[at, :] + dot(hidden[at, :], down_perm, 1, 0) + vector(5)
        ).astype(BF)
        bout_out[i].start()

    tok_out = halves(gmid, grad_tok_hbm, 7)

    def back_first(i):
        at = rows_of(i, big)
        shares = []
        for u in range(big // SPAN):
            g = i * (big // SPAN) + u
            share = jnp.concatenate(
                [gnbar[g : g + 1, :], gnbar[groups + g : groups + g + 1, :]], axis=1
            ) * (1.0 / SPAN)
            shares.append(jnp.broadcast_to(share, (SPAN, width)))
        grad = dot(gbefore[at, 0 : 3 * width], wq[...], 1, 1) + jnp.concatenate(
            shares, axis=0
        )
        xhat = xhat1[at, :]
        vsum[0:1, :] += jnp.sum(grad * xhat, axis=0, keepdims=True)
        vsum[1:2, :] += jnp.sum(grad, axis=0, keepdims=True)
        gmid[at, :] = gmid[at, :] + norm_back(grad, xhat, inv1[at, :], vector(0))
        tok_out[i].start()

    def vec_build():
        for owner in range(shard_count):
            at = owner // 2
            piece = vsum[:, at * lanes : (at + 1) * lanes]
            if owner % 2 == 1:
                piece = pltpu.roll(piece, HD, axis=1)
            vec_send[owner, 0:8, :] = piece
            vec_send[owner, 8:16, :] = jnp.zeros((8, lanes), F32)
            for r in range(parts):
                start = r * part_cols + owner * lanes
                vec_send[owner, 8 + r : 9 + r, :] = upsum[0:1, start : start + lanes]

    vo_copies = [
        remote(vec_send.at[peer[0]], vec_recv.at[ms], vo_s.at[step], vo_r.at[step], peer)
        for step, peer in enumerate(shard_peers)
    ]
    vz_copies = [
        remote(vec_line.at[mq], vec_line.at[mq], vz_s.at[step], vz_r.at[step], peer)
        for step, peer in enumerate(seq_peers)
    ]

    def vo_start():
        for c in vo_copies:
            c.start()
        vec_recv[ms] = vec_send[ms]

    def vo_wait():
        for c in vo_copies:
            c.wait_recv()
        vec_line[mq] = jnp.sum(vec_recv[...], axis=0)

    def vz_start():
        for c in vz_copies:
            c.start()

    vec_out = pltpu.make_async_copy(vec_total, vec_out_hbm, io_sem.at[4])

    def vz_wait():
        for c in vz_copies:
            c.wait_recv()
        vec_total[...] = jnp.sum(vec_line[...], axis=0)
        vec_out.start()

    cot_in.wait()
    gather_own_first(QKV)
    xz_start()
    gather_own_first(OUT)
    gather_own_second(QKV)
    gather_forward(QKV)
    xz_wait()
    xs_start()
    vec_start()
    gather_core(QKV)
    gather_own_second(OUT)
    gather_own_first(UP)
    gather_last(QKV)
    gather_own_second(UP)
    vec_wait()
    gather_done(QKV)
    gather_forward(OUT)
    xs_wait()
    project(0)
    project(1)
    gather_core(OUT)
    project(2)
    span_means()
    gather_forward(UP)
    gather_own_first(DOWN)
    attend(0)
    gather_own_second(DOWN)
    gather_last(OUT)
    gather_core(UP)
    attend(1)
    gather_done(OUT)
    gather_last(UP)
    second_norm()
    gather_done(UP)
    feed_up(0, 0)
    gather_forward(DOWN)
    feed_up(1, 1)
    feed_up(0, 1)
    gather_core(DOWN)
    down_grad(0)
    reduce_a(D0)
    feed_up(1, 0)
    gather_last(DOWN)
    down_grad(1)
    reduce_b(D0)
    gather_done(DOWN)
    reduce_a(D1)
    back_down(1, 0)
    back_down(1, 1)
    up_grad(1)
    reduce_b(D1)
    reduce_c(D0)
    back_down(0, 1)
    reduce_a(U1)
    back_down(0, 0)
    up_grad(0)
    reduce_a(U0)
    reduce_c(D1)
    back_second(0)
    reduce_b(U1)
    reduce_d(D0)
    reduce_b(U0)
    back_second(1)
    out_grad()
    reduce_a(GO)
    reduce_c(U1)
    attend_back(0)
    reduce_d(D1)
    reduce_b(GO)
    reduce_c(U0)
    attend_back(1)
    first_grad(0, 2 * lanes, g_two.at[0])
    reduce_a(QA)
    attend_back(2)
    reduce_e(D0)
    reduce_c(GO)
    reduce_d(U1)
    attend_back(3)
    reduce_b(QA)
    reduce_e(D1)
    mean_grad()
    gs_start()
    reduce_d(GO)
    reduce_d(U0)
    first_grad(2 * lanes, lanes, g_one.at[0])
    reduce_c(QA)
    reduce_a(Q2)
    reduce_e(U1)
    reduce_f(D0)
    first_grad(3 * lanes, lanes, g_one.at[1])
    reduce_a(Q3)
    reduce_b(Q2)
    reduce_f(D1)
    gs_wait()
    gz_start()
    reduce_e(GO)
    reduce_b(Q3)
    reduce_e(U0)
    reduce_d(QA)
    reduce_c(Q2)
    reduce_f(U1)
    reduce_c(Q3)
    gz_wait()
    back_first(0)
    reduce_f(GO)
    reduce_e(QA)
    reduce_d(Q2)
    reduce_d(Q3)
    reduce_f(U0)
    back_first(1)
    reduce_e(Q2)
    vec_build()
    reduce_g(U1)
    vo_start()
    reduce_e(Q3)
    reduce_f(QA)
    out_block(0)
    reduce_f(Q2)
    reduce_g(D1)
    vo_wait()
    reduce_g(GO)
    reduce_g(D0)
    reduce_g(U0)
    vz_start()
    reduce_f(Q3)
    out_block(1)
    reduce_g(Q2)
    reduce_g(QA)
    vz_wait()
    reduce_g(Q3)

    for target in range(1, shard_count):

        @pl.when(target > ms)
        def _(target=target):
            xs_copy(ms, target).wait_send()

    for target in range(shard_count - 1):

        @pl.when(target < ms)
        def _(target=target):
            gs_copy(ms, target).wait_send()

    for c in vec_copies + xz_copies + gz_copies + vo_copies + vz_copies:
        c.wait_send()
    for which in range(4):
        for c in w_copies[which]:
            c.wait_send()
    for which in range(CHUNKS):
        emit(which, chunk(which)[5]).wait()
    for c in bout_out + tok_out:
        c.wait()
    vec_out.wait()


def finish_kernel(*refs):
    raw, outs, vec_outs = refs[0:8], refs[8:14], refs[14:21]
    low_refs, high_refs, vec, small = refs[21:28], refs[28:32], refs[32], refs[33:40]
    in_sem, out_sem = refs[40:42]
    order = (1, 0, 5, 6, 4, 2, 3)
    loads = {
        n: pltpu.make_async_copy(raw[n], low_refs[n], in_sem.at[n]) for n in range(2, 7)
    }
    pieces = 4

    def piece_copies(n):
        count = low_refs[n].shape[0] // pieces
        spans = [pl.ds(k * count, count) for k in range(pieces)]
        return [
            (
                pltpu.make_async_copy(
                    raw[n].at[at], low_refs[n].at[at], in_sem.at[8 + n * pieces + k]
                ),
                pltpu.make_async_copy(
                    low_refs[n].at[at], outs[n].at[at], out_sem.at[13 + n * pieces + k]
                ),
            )
            for k, at in enumerate(spans)
        ]

    large = [piece_copies(n) for n in range(2)]
    vec_load = pltpu.make_async_copy(raw[7], vec, in_sem.at[7])
    vec_load.start()
    for n in order:
        for c in [load for load, _ in large[n]] if n < 2 else [loads[n]]:
            c.start()
    vec_load.wait()
    stores = []
    for n in range(7):
        if n < 6:
            small[n][...] = vec[n : n + 1, 0 : small[n].shape[1]]
        else:
            small[n][...] = vec[8 : 8 + small[n].shape[0], :]
        stores.append(pltpu.make_async_copy(small[n], vec_outs[n], out_sem.at[6 + n]))
        stores[n].start()
    lanes = 2 * HD

    def store(ready, at):
        stores.append(pltpu.make_async_copy(ready, outs[at], out_sem.at[at]))
        stores[-1].start()

    for n in order:
        if n < 2:
            for load, piece_store in large[n]:
                load.wait()
                piece_store.start()
                stores.append(piece_store)
            continue
        loads[n].wait()
        low = low_refs[n]
        if n == 2:
            for part in range(3):
                start = part * 4 * lanes
                high_refs[0][:, start : start + 2 * lanes] = low[
                    :, part * 2 * lanes : (part + 1) * 2 * lanes
                ].astype(F32)
        elif n == 3:
            for part in range(3):
                for one in range(2):
                    start = (part * 4 + 2 + one) * lanes
                    high_refs[0][:, start : start + lanes] = low[
                        one, :, part * lanes : (part + 1) * lanes
                    ].astype(F32)
            store(high_refs[0], 2)
        elif n == 5:
            high = high_refs[2]
            part_count, _, columns = low.shape
            for part in range(part_count):
                for owner in range(columns // lanes):
                    start = (owner * part_count + part) * lanes
                    high[:, start : start + lanes] = low[
                        part, :, owner * lanes : (owner + 1) * lanes
                    ].astype(F32)
            store(high, 4)
        else:
            high = high_refs[n - 3]
            high[...] = low[...].astype(F32)
            store(high, n - 1)
    for c in stores:
        c.wait()


def local_block(
    tokens,
    ln1_gain,
    ln1_bias,
    qkv_weight,
    out_weight,
    out_bias,
    ln2_gain,
    ln2_bias,
    up_weight,
    up_bias,
    down_weight,
    down_bias,
    cotangent,
):
    seq_count = lax.axis_size("seq")
    shard_count = lax.axis_size("shard")
    total = seq_count * shard_count
    batch, local_len, width = tokens.shape
    rows = batch * local_len
    groups = rows // SPAN
    spans_all = local_len // SPAN * total
    keys = SPAN + spans_all
    ff = up_weight.shape[1]
    lanes = 2 * HD
    shard_rows = width // shard_count
    down_rows = ff // shard_count
    hbm = pl.BlockSpec(memory_space=pl.ANY)
    dma = pltpu.SemaphoreType.DMA
    half_yx = shard_count // 2

    def grads(count, columns, lead=()):
        half = count // 2
        return (
            pltpu.VMEM(lead + (2, half_yx, count, columns), BF),
            pltpu.VMEM(lead + (half_yx, count, columns), BF),
            pltpu.VMEM(lead + (2, half, columns), BF),
            pltpu.VMEM(lead + (2, count, columns), BF),
            pltpu.VMEM(lead + (2, count, columns), BF),
            pltpu.VMEM(lead + (count, columns), BF),
        )

    parts = down_rows // lanes
    part_cols = ff // parts
    down_bufs = grads(lanes, width, (parts,))
    up_bufs = grads(shard_rows, part_cols, (parts,))
    out_bufs = grads(shard_rows, width, (1,))
    two_bufs = grads(shard_rows, 6 * lanes, (1,))
    one_bufs = grads(shard_rows, 3 * lanes, (2,))
    grad_bufs = [
        buf
        for five in zip(down_bufs, up_bufs, out_bufs, two_bufs, one_bufs)
        for buf in five
    ]
    scratch = [
        [pltpu.VMEM((1, shard_rows), BF)] * 6,
        pltpu.VMEM((down_rows // lanes, lanes), BF),
        pltpu.VMEM((16, lanes), F32),
        pltpu.VMEM((rows, width), BF),
        pltpu.VMEM((rows, width), BF),
        pltpu.VMEM((width, 3 * width), BF),
        pltpu.VMEM((width, width), BF),
        pltpu.VMEM((width, ff), BF),
        pltpu.VMEM((ff, width), BF),
        pltpu.VMEM((16, lanes), F32),
        pltpu.VMEM((shard_count, 16, lanes), F32),
        pltpu.VMEM((rows, width), F32),
        pltpu.VMEM((rows, 1), F32),
        pltpu.VMEM((groups, width), F32),
        pltpu.VMEM((total, 2 * groups, width // 2), BF),
        pltpu.VMEM((batch * spans_all, batch * spans_all), BF),
        pltpu.VMEM((8, width), F32),
        pltpu.VMEM((8, ff), F32),
        pltpu.VMEM((rows, width), BF),
        pltpu.VMEM((rows, 3 * width), BF),
        pltpu.VMEM((batch * spans_all, width), BF),
        pltpu.VMEM((batch * spans_all, 2 * width), BF),
        pltpu.VMEM((groups * H // 2, keys, 2 * SPAN), BF),
        pltpu.VMEM((rows, width), BF),
        pltpu.VMEM((rows, width), F32),
        pltpu.VMEM((rows, width), F32),
        pltpu.VMEM((rows, 1), F32),
        pltpu.VMEM((rows, width), BF),
        pltpu.VMEM((rows, width), F32),
        pltpu.VMEM((rows, ff), BF),
        pltpu.VMEM((rows, ff), BF),
        pltpu.VMEM((rows, width), BF),
        pltpu.VMEM((rows, width), BF),
        pltpu.VMEM((batch * spans_all, 2 * width), BF),
        pltpu.VMEM((total, 2 * groups, width // 2), BF),
        pltpu.VMEM((shard_count, seq_count, 2 * groups, width // 2), BF),
        pltpu.VMEM((seq_count, 2 * groups, width // 2), BF),
        pltpu.VMEM((seq_count, 2 * groups, width // 2), BF),
        pltpu.VMEM((2 * groups, width // 2), F32),
        pltpu.VMEM((8, width), F32),
        pltpu.VMEM((8, ff), F32),
        pltpu.VMEM((shard_count, 16, lanes), F32),
        pltpu.VMEM((shard_count, 16, lanes), F32),
        pltpu.VMEM((seq_count, 16, lanes), F32),
        *grad_bufs,
        dma((4 * GATHER_STEPS,)),
        dma((4 * GATHER_STEPS,)),
        dma((4,)),
        dma((9,)),
        dma((7,)),
        dma((shard_count,)),
        dma((shard_count,)),
        dma((seq_count,)),
        dma((seq_count,)),
        dma((shard_count,)),
        dma((shard_count,)),
        dma((shard_count,)),
        dma((shard_count,)),
        dma((seq_count,)),
        dma((seq_count,)),
        dma((shard_count,)),
        dma((shard_count,)),
        dma((seq_count,)),
        dma((seq_count,)),
        dma((CHUNKS * REDUCE_STEPS,)),
        dma((CHUNKS * REDUCE_STEPS,)),
        dma((CHUNKS,)),
    ]
    vectors = [
        v.reshape(1, shard_rows)
        for v in (ln1_gain, ln1_bias, out_bias, ln2_gain, ln2_bias, down_bias)
    ]
    raw = pl.pallas_call(
        functools.partial(block_kernel, batch, shard_count, seq_count),
        out_shape=(
            jax.ShapeDtypeStruct((rows, width), BF),
            jax.ShapeDtypeStruct((rows, width), F32),
            jax.ShapeDtypeStruct((shard_rows, 6 * lanes), BF),
            jax.ShapeDtypeStruct((2, shard_rows, 3 * lanes), BF),
            jax.ShapeDtypeStruct((shard_rows, width), BF),
            jax.ShapeDtypeStruct((parts, shard_rows, part_cols), BF),
            jax.ShapeDtypeStruct((down_rows, width), BF),
            jax.ShapeDtypeStruct((16, lanes), F32),
        ),
        in_specs=[hbm, hbm, [hbm] * 6, hbm, hbm, hbm, hbm, hbm],
        out_specs=(hbm,) * 8,
        scratch_shapes=scratch,
        compiler_params=pltpu.CompilerParams(
            collective_id=0, has_side_effects=True, vmem_limit_bytes=63 * 2**20
        ),
        name="block",
    )(
        tokens.reshape(rows, width),
        cotangent.reshape(rows, width),
        vectors,
        up_bias.reshape(-1, lanes),
        qkv_weight,
        out_weight,
        up_weight,
        down_weight,
    )
    low_shapes = [
        (shard_rows, 6 * lanes),
        (2, shard_rows, 3 * lanes),
        (shard_rows, width),
        (parts, shard_rows, part_cols),
        (down_rows, width),
    ]
    high_shapes = [
        (shard_rows, 3 * width),
        (shard_rows, width),
        (shard_rows, ff),
        (down_rows, width),
    ]
    done = pl.pallas_call(
        finish_kernel,
        out_shape=(
            jax.ShapeDtypeStruct((rows, width), BF),
            jax.ShapeDtypeStruct((rows, width), F32),
            *(jax.ShapeDtypeStruct(shape, F32) for shape in high_shapes),
            *(jax.ShapeDtypeStruct((1, shard_rows), F32) for _ in range(6)),
            jax.ShapeDtypeStruct((down_rows // lanes, lanes), F32),
        ),
        in_specs=[hbm] * 8,
        out_specs=(hbm,) * 13,
        scratch_shapes=[
            pltpu.VMEM((rows, width), BF),
            pltpu.VMEM((rows, width), F32),
            *(pltpu.VMEM(shape, BF) for shape in low_shapes),
            *(pltpu.VMEM(shape, F32) for shape in high_shapes),
            pltpu.VMEM((16, lanes), F32),
            *(pltpu.VMEM((1, shard_rows), F32) for _ in range(6)),
            pltpu.VMEM((down_rows // lanes, lanes), F32),
            dma((16,)),
            dma((21,)),
        ],
        compiler_params=pltpu.CompilerParams(vmem_limit_bytes=62 * 2**20),
        name="finish",
    )(*raw)
    block_out, grad_tokens, g_qkv, g_out, g_up, g_down = done[0:6]
    vec_grads = [v.reshape(shard_rows) for v in done[6:12]]
    return (
        block_out.reshape(tokens.shape),
        grad_tokens.reshape(tokens.shape),
        vec_grads[0],
        vec_grads[1],
        g_qkv,
        g_out,
        vec_grads[2],
        vec_grads[3],
        vec_grads[4],
        g_up,
        done[12].reshape(down_rows),
        g_down,
        vec_grads[5],
    )


def layer_norm(values, norm_gain, norm_shift):
    center = values - jnp.mean(values, axis=-1, keepdims=True)
    spread = jnp.mean(center * center, axis=-1, keepdims=True)
    return center * lax.rsqrt(spread + epsilon) * norm_gain + norm_shift


def gelu_exact(values):
    return jax.nn.gelu(values, approximate=False)


def contract_rows(left_matrix, right_matrix):
    return lax.dot_general(
        left_matrix, right_matrix, (((0,), (0,)), ((), ())), preferred_element_type=jnp.float32
    )


def times_transpose(left_matrix, right_matrix):
    return lax.dot_general(
        left_matrix, right_matrix, (((1,), (1,)), ((), ())), preferred_element_type=jnp.float32
    )


def joint_scores(query_rows, key_rows, key_all, causal, earlier):
    factor = HD ** (-0.5)
    local_part = factor * jnp.einsum(
        "bjihd,bjkhd->bjhik", query_rows, key_rows, preferred_element_type=jnp.float32
    )
    summary = factor * jnp.einsum(
        "bjihd,bfhd->bjhif", query_rows, key_all, preferred_element_type=jnp.float32
    ) + math.log(SPAN)
    local_part = jnp.where(causal[None, None, None], local_part, -jnp.inf)
    summary = jnp.where(earlier[None, :, None, None, :], summary, -jnp.inf)
    return (local_part, summary)


def attend(query_rows, key_rows, value_rows, key_all, value_all, causal, earlier):
    local_part, summary = joint_scores(query_rows, key_rows, key_all, causal, earlier)
    row_max = jnp.maximum(jnp.max(local_part, axis=-1), jnp.max(summary, axis=-1))
    local_exp = jnp.exp(local_part - row_max[..., None])
    summary_exp = jnp.exp(summary - row_max[..., None])
    row_total = jnp.sum(local_exp, axis=-1) + jnp.sum(summary_exp, axis=-1)
    log_total = row_max + jnp.log(row_total)
    local_weights = (local_exp / row_total[..., None]).astype(jnp.bfloat16)
    summary_weights = (summary_exp / row_total[..., None]).astype(jnp.bfloat16)
    mixed_heads = jnp.einsum(
        "bjhik,bjkhd->bjihd", local_weights, value_rows, preferred_element_type=jnp.float32
    )
    mixed_heads = mixed_heads + jnp.einsum(
        "bjhif,bfhd->bjihd", summary_weights, value_all, preferred_element_type=jnp.float32
    )
    return (mixed_heads, log_total, local_weights, summary_weights)


def attend_back(
    grad_mixed,
    query_rows,
    key_rows,
    value_rows,
    key_all,
    value_all,
    causal,
    earlier,
    log_total,
    local_weights,
    summary_weights,
):
    factor = HD ** (-0.5)
    local_part, summary = joint_scores(query_rows, key_rows, key_all, causal, earlier)
    local_prob = jnp.exp(local_part - log_total[..., None])
    summary_prob = jnp.exp(summary - log_total[..., None])
    grad_local_w = jnp.einsum(
        "bjihd,bjkhd->bjhik", grad_mixed, value_rows, preferred_element_type=jnp.float32
    )
    grad_summary_w = jnp.einsum(
        "bjihd,bfhd->bjhif", grad_mixed, value_all, preferred_element_type=jnp.float32
    )
    row_inner = jnp.sum(local_prob * grad_local_w, axis=-1) + jnp.sum(
        summary_prob * grad_summary_w, axis=-1
    )
    grad_local = (local_prob * (grad_local_w - row_inner[..., None])).astype(jnp.bfloat16)
    grad_summary = (summary_prob * (grad_summary_w - row_inner[..., None])).astype(jnp.bfloat16)
    grad_query = jnp.einsum(
        "bjhik,bjkhd->bjihd", grad_local, key_rows, preferred_element_type=jnp.float32
    )
    grad_query = factor * (
        grad_query
        + jnp.einsum("bjhif,bfhd->bjihd", grad_summary, key_all, preferred_element_type=jnp.float32)
    )
    grad_key = factor * jnp.einsum(
        "bjhik,bjihd->bjkhd", grad_local, query_rows, preferred_element_type=jnp.float32
    )
    grad_key_all = factor * jnp.einsum(
        "bjhif,bjihd->bfhd", grad_summary, query_rows, preferred_element_type=jnp.float32
    )
    grad_value = jnp.einsum(
        "bjhik,bjihd->bjkhd", local_weights, grad_mixed, preferred_element_type=jnp.float32
    )
    grad_value_all = jnp.einsum(
        "bjhif,bjihd->bfhd", summary_weights, grad_mixed, preferred_element_type=jnp.float32
    )
    return (grad_query, grad_key, grad_value, grad_key_all, grad_value_all)


def local_general(
    tokens,
    ln1_gain,
    ln1_bias,
    qkv_weight,
    out_weight,
    out_bias,
    ln2_gain,
    ln2_bias,
    up_weight,
    up_bias,
    down_weight,
    down_bias,
    cotangent,
):
    seq_count = lax.axis_size("seq")
    shard_count = lax.axis_size("shard")
    shard_place = lax.axis_index("shard")
    batch_size, local_len, model_width = tokens.shape
    heads_here = H // seq_count
    head_width = heads_here * HD
    group_len = local_len * seq_count
    spans_here = group_len // SPAN
    spans_all = spans_here * shard_count
    row_count = batch_size * local_len
    shards = (
        ln1_gain,
        ln1_bias,
        qkv_weight,
        out_weight,
        out_bias,
        ln2_gain,
        ln2_bias,
        up_weight,
        up_bias,
        down_weight,
        down_bias,
    )
    gathered = (
        lax.all_gather(shards[0], "shard", axis=0, tiled=True),
        lax.all_gather(shards[1], "shard", axis=0, tiled=True),
        lax.all_gather(shards[2], "shard", axis=0, tiled=True),
        lax.all_gather(shards[3], "shard", axis=0, tiled=True),
        lax.all_gather(shards[4], "shard", axis=0, tiled=True),
        lax.all_gather(shards[5], "shard", axis=0, tiled=True),
        lax.all_gather(shards[6], "shard", axis=0, tiled=True),
        lax.all_gather(shards[7], "shard", axis=0, tiled=True),
        lax.all_gather(shards[8], "shard", axis=0, tiled=True),
        lax.all_gather(shards[9], "shard", axis=0, tiled=True),
        lax.all_gather(shards[10], "shard", axis=0, tiled=True),
    )
    (
        gain_one,
        bias_one,
        qkv_full,
        out_full,
        out_shift,
        gain_two,
        bias_two,
        up_full,
        up_shift,
        down_full,
        down_shift,
    ) = gathered
    flat_tokens = tokens.reshape(row_count, model_width).astype(jnp.float32)
    normed = layer_norm(
        flat_tokens, gain_one.astype(jnp.float32), bias_one.astype(jnp.float32)
    ).astype(jnp.bfloat16)
    packed = jnp.dot(normed, qkv_full, preferred_element_type=jnp.float32).astype(jnp.bfloat16)
    span_place = jnp.arange(SPAN)
    packed_heads = packed.reshape(batch_size, local_len, 3, seq_count, head_width)
    headed = lax.all_to_all(packed_heads, "seq", split_axis=3, concat_axis=1, tiled=True)
    headed = headed.reshape(batch_size, spans_here, SPAN, 3, heads_here, HD)
    query_rows = headed[:, :, :, 0]
    key_rows = headed[:, :, :, 1]
    value_rows = headed[:, :, :, 2]
    key_means = jnp.mean(key_rows, axis=2, dtype=jnp.float32).astype(jnp.bfloat16)
    value_means = jnp.mean(value_rows, axis=2, dtype=jnp.float32).astype(jnp.bfloat16)
    key_all, value_all = (
        lax.all_gather(key_means, "shard", axis=1, tiled=True),
        lax.all_gather(value_means, "shard", axis=1, tiled=True),
    )
    causal = span_place[:, None] >= span_place[None, :]
    global_span = shard_place * spans_here + jnp.arange(spans_here)
    earlier = global_span[:, None] > jnp.arange(spans_all)[None, :]
    mixed_heads, log_total, local_weights, summary_weights = attend(
        query_rows, key_rows, value_rows, key_all, value_all, causal, earlier
    )
    attended = mixed_heads.astype(jnp.bfloat16).reshape(batch_size, group_len, head_width)
    attended = lax.all_to_all(attended, "seq", split_axis=1, concat_axis=2, tiled=True)
    attended_rows = attended.reshape(row_count, model_width)
    middle = (
        flat_tokens
        + jnp.dot(attended_rows, out_full, preferred_element_type=jnp.float32)
        + out_shift.astype(jnp.float32)
    )
    second = layer_norm(middle, gain_two.astype(jnp.float32), bias_two.astype(jnp.float32)).astype(
        jnp.bfloat16
    )
    before = jnp.dot(second, up_full, preferred_element_type=jnp.float32) + up_shift.astype(
        jnp.float32
    )
    hidden = gelu_exact(before).astype(jnp.bfloat16)
    block_out = (
        middle
        + jnp.dot(hidden, down_full, preferred_element_type=jnp.float32)
        + down_shift.astype(jnp.float32)
    )
    block_out = block_out.astype(jnp.bfloat16).reshape(batch_size, local_len, model_width)
    incoming = cotangent.reshape(row_count, model_width)
    grad_down = contract_rows(hidden, incoming)
    grad_down_shift = jnp.sum(incoming, axis=0, dtype=jnp.float32)
    grad_hidden = times_transpose(incoming, down_full)
    gelu_value, gelu_pull = jax.vjp(gelu_exact, before)
    grad_before = gelu_pull(grad_hidden)[0].astype(jnp.bfloat16)
    grad_up = contract_rows(second, grad_before)
    grad_up_shift = jnp.sum(grad_before, axis=0, dtype=jnp.float32)
    grad_second = times_transpose(grad_before, up_full)
    norm_value, norm_pull = jax.vjp(
        layer_norm, middle, gain_two.astype(jnp.float32), bias_two.astype(jnp.float32)
    )
    grad_middle_norm, grad_gain_two, grad_bias_two = norm_pull(grad_second)
    grad_middle = incoming.astype(jnp.float32) + grad_middle_norm
    grad_branch = grad_middle.astype(jnp.bfloat16)
    grad_out = contract_rows(attended_rows, grad_branch)
    grad_out_shift = jnp.sum(grad_branch, axis=0, dtype=jnp.float32)
    grad_attended = times_transpose(grad_branch, out_full).astype(jnp.bfloat16)
    grad_attended = grad_attended.reshape(batch_size, local_len, seq_count, head_width)
    grad_headed = lax.all_to_all(grad_attended, "seq", split_axis=2, concat_axis=1, tiled=True)
    grad_mixed = grad_headed.reshape(batch_size, spans_here, SPAN, heads_here, HD)
    grad_query, grad_key, grad_value, grad_key_all, grad_value_all = attend_back(
        grad_mixed,
        query_rows,
        key_rows,
        value_rows,
        key_all,
        value_all,
        causal,
        earlier,
        log_total,
        local_weights,
        summary_weights,
    )
    grad_key_means, grad_value_means = (
        lax.psum_scatter(
            grad_key_all.astype(jnp.bfloat16), "shard", scatter_dimension=1, tiled=True
        ).astype(jnp.float32),
        lax.psum_scatter(
            grad_value_all.astype(jnp.bfloat16), "shard", scatter_dimension=1, tiled=True
        ).astype(jnp.float32),
    )
    grad_key = grad_key + grad_key_means[:, :, None] / SPAN
    grad_value = grad_value + grad_value_means[:, :, None] / SPAN
    grad_packed = jnp.stack([grad_query, grad_key, grad_value], axis=3).astype(jnp.bfloat16)
    grad_packed = grad_packed.reshape(batch_size, group_len, 3, 1, head_width)
    grad_packed = lax.all_to_all(grad_packed, "seq", split_axis=1, concat_axis=3, tiled=True)
    grad_packed = grad_packed.reshape(row_count, 3 * model_width)
    grad_qkv = contract_rows(normed, grad_packed)
    grad_normed = times_transpose(grad_packed, qkv_full)
    first_value, first_pull = jax.vjp(
        layer_norm, flat_tokens, gain_one.astype(jnp.float32), bias_one.astype(jnp.float32)
    )
    grad_flat_norm, grad_gain_one, grad_bias_one = first_pull(grad_normed)
    grad_tokens = (grad_middle + grad_flat_norm).reshape(batch_size, local_len, model_width)
    all_grads = (
        grad_gain_one,
        grad_bias_one,
        grad_qkv,
        grad_out,
        grad_out_shift,
        grad_gain_two,
        grad_bias_two,
        grad_up,
        grad_up_shift,
        grad_down,
        grad_down_shift,
    )
    owned_grads = (
        lax.psum_scatter(
            all_grads[0].astype(jnp.bfloat16), "shard", scatter_dimension=0, tiled=True
        ).astype(jnp.float32),
        lax.psum_scatter(
            all_grads[1].astype(jnp.bfloat16), "shard", scatter_dimension=0, tiled=True
        ).astype(jnp.float32),
        lax.psum_scatter(
            all_grads[2].astype(jnp.bfloat16), "shard", scatter_dimension=0, tiled=True
        ).astype(jnp.float32),
        lax.psum_scatter(
            all_grads[3].astype(jnp.bfloat16), "shard", scatter_dimension=0, tiled=True
        ).astype(jnp.float32),
        lax.psum_scatter(
            all_grads[4].astype(jnp.bfloat16), "shard", scatter_dimension=0, tiled=True
        ).astype(jnp.float32),
        lax.psum_scatter(
            all_grads[5].astype(jnp.bfloat16), "shard", scatter_dimension=0, tiled=True
        ).astype(jnp.float32),
        lax.psum_scatter(
            all_grads[6].astype(jnp.bfloat16), "shard", scatter_dimension=0, tiled=True
        ).astype(jnp.float32),
        lax.psum_scatter(
            all_grads[7].astype(jnp.bfloat16), "shard", scatter_dimension=0, tiled=True
        ).astype(jnp.float32),
        lax.psum_scatter(
            all_grads[8].astype(jnp.bfloat16), "shard", scatter_dimension=0, tiled=True
        ).astype(jnp.float32),
        lax.psum_scatter(
            all_grads[9].astype(jnp.bfloat16), "shard", scatter_dimension=0, tiled=True
        ).astype(jnp.float32),
        lax.psum_scatter(
            all_grads[10].astype(jnp.bfloat16), "shard", scatter_dimension=0, tiled=True
        ).astype(jnp.float32),
    )
    owned_grads = (
        lax.psum(owned_grads[0].astype(jnp.bfloat16), "seq").astype(jnp.float32),
        lax.psum(owned_grads[1].astype(jnp.bfloat16), "seq").astype(jnp.float32),
        lax.psum(owned_grads[2].astype(jnp.bfloat16), "seq").astype(jnp.float32),
        lax.psum(owned_grads[3].astype(jnp.bfloat16), "seq").astype(jnp.float32),
        lax.psum(owned_grads[4].astype(jnp.bfloat16), "seq").astype(jnp.float32),
        lax.psum(owned_grads[5].astype(jnp.bfloat16), "seq").astype(jnp.float32),
        lax.psum(owned_grads[6].astype(jnp.bfloat16), "seq").astype(jnp.float32),
        lax.psum(owned_grads[7].astype(jnp.bfloat16), "seq").astype(jnp.float32),
        lax.psum(owned_grads[8].astype(jnp.bfloat16), "seq").astype(jnp.float32),
        lax.psum(owned_grads[9].astype(jnp.bfloat16), "seq").astype(jnp.float32),
        lax.psum(owned_grads[10].astype(jnp.bfloat16), "seq").astype(jnp.float32),
    )
    return (
        block_out,
        grad_tokens,
        owned_grads[0],
        owned_grads[1],
        owned_grads[2],
        owned_grads[3],
        owned_grads[4],
        owned_grads[5],
        owned_grads[6],
        owned_grads[7],
        owned_grads[8],
        owned_grads[9],
        owned_grads[10],
    )


def local(tokens, *rest):
    whole_spans = tokens.shape[1] % SPAN == 0
    if whole_spans and lax.axis_size("shard") == 8 and lax.axis_size("seq") == 4:
        return local_block(tokens, *rest)
    return local_general(tokens, *rest)


def solution(mesh):
    return jax.shard_map(
        local,
        mesh=mesh,
        in_specs=(
            P(None, ("shard", "seq"), None),
            P("shard"),
            P("shard"),
            P("shard", None),
            P("shard", None),
            P("shard"),
            P("shard"),
            P("shard"),
            P("shard", None),
            P("shard"),
            P("shard", None),
            P("shard"),
            P(None, ("shard", "seq"), None),
        ),
        out_specs=(
            P(None, ("shard", "seq"), None),
            P(None, ("shard", "seq"), None),
            P("shard"),
            P("shard"),
            P("shard", None),
            P("shard", None),
            P("shard"),
            P("shard"),
            P("shard"),
            P("shard", None),
            P("shard"),
            P("shard", None),
            P("shard"),
        ),
        check_vma=False,
    )
```
